32 devices in a mesh: dp: 8 (over z, y), seq: 4 (over x, core).
Axes of the slice: x: 2, y: 2, z: 4, core: 2. Of those that a mesh axis runs over, the one named last changes fastest.
Arguments:
- inputs: bfloat16 [32, 1024, 512], P('dp', 'seq'), may hold values from -6 to 6
- memory: bfloat16 [32, 1024, 512], P('dp', 'seq'), may hold values from -6 to 6
- seg_ids: int32 [32, 1024], P('dp'), may hold values from 0 to 5, never falling along the last dimension, each value on 1 to 800 neighbouring positions
- mem_lengths: int32 [32, 6], P('dp'), may hold values from 1 to 512, 1024 in all within a row
- cotangent: bfloat16 [32, 1024, 512], P('dp', 'seq'), may hold values from -6 to 6
- qkv_weight: bfloat16 [512, 1536], P(('dp', 'seq')), may hold values from -0.25 to 0.25
- self_out_weight: bfloat16 [512, 512], P(('dp', 'seq')), may hold values from -1 to 1
- cross_q_weight: bfloat16 [512, 512], P(('dp', 'seq')), may hold values from -0.25 to 0.25
- cross_kv_weight: bfloat16 [512, 1024], P(('dp', 'seq')), may hold values from -0.25 to 0.25
- cross_out_weight: bfloat16 [512, 512], P(('dp', 'seq')), may hold values from -1 to 1
- ffn_in_weight: bfloat16 [512, 2048], P(('dp', 'seq')), may hold values from -0.25 to 0.25
- ffn_in_bias: bfloat16 [2048], P(('dp', 'seq')), may hold values from -3 to 3
- ffn_out_weight: bfloat16 [2048, 512], P(('dp', 'seq')), may hold values from -0.125 to 0.125
- norm_gains: bfloat16 [3, 512], P(None, ('dp', 'seq')), may hold values from 0.099609375 to 1.8984375
- shift_vectors: bfloat16 [4, 512], P(None, ('dp', 'seq')), may hold values from -3 to 3
Outputs:
- output: bfloat16 [32, 1024, 512], P('dp', 'seq')
- input_grad: float32 [32, 1024, 512], P('dp', 'seq')
- memory_grad: float32 [32, 1024, 512], P('dp', 'seq')
- qkv_grad: float32 [512, 1536], P(('dp', 'seq'))
- self_out_grad: float32 [512, 512], P(('dp', 'seq'))
- cross_q_grad: float32 [512, 512], P(('dp', 'seq'))
- cross_kv_grad: float32 [512, 1024], P(('dp', 'seq'))
- cross_out_grad: float32 [512, 512], P(('dp', 'seq'))
- ffn_in_grad: float32 [512, 2048], P(('dp', 'seq'))
- ffn_bias_grad: float32 [2048], P(('dp', 'seq'))
- ffn_out_grad: float32 [2048, 512], P(('dp', 'seq'))
- gains_grad: float32 [3, 512], P(None, ('dp', 'seq'))
- shifts_grad: float32 [4, 512], P(None, ('dp', 'seq'))
The draws below stay inside these ranges and needn't reach their ends.
Inputs may be any that keep to these rules, and one draw needn't show every extreme that they name: `seg_ids`: sentence numbers never fall along a row and every number appears; in each row one sentence has exactly 800 tokens. `mem_lengths`: each row's lengths add up to 1024; sentence s reads the memory positions that follow those of sentences before it; the largest of a row is exactly 512.
All inputs are finite; a program needn't handle non-finite values.
Results may differ from the reference program's by a relative error of at most 0.02.
Values may be sent and summed in bfloat16 or wider, within the bound.
No kernel may reach another device: no remote copies, remote signals or barrier semaphores. Data moves between devices by JAX's collectives and lax.ppermute only.
A program may use at most 128 MiB of HBM per device.

```python
import math
import jax
import jax.numpy as jnp
import numpy as np
from jax import lax

D = 512
HEADS = 8
HEAD = 64
FF = 2048
ROW_LEN = 1024
MEM_LEN = 1024
SEGS = 6
ROWS = 32


def block_levels(stream_key, shape, shards, least, high):
    factor_of, own = 1.0, jax.random.fold_in(stream_key, 6)
    for dim, shards_of in shards:
        draws = jnp.exp(jax.random.uniform(jax.random.fold_in(own, dim), (shards_of,), jnp.float32, least / len(shards), high / len(shards)))
        factor_of = factor_of * jnp.repeat(draws, shape[dim] // shards_of).reshape([-1 if axis == dim else 1 for axis in range(len(shape))])
    return factor_of


def length_profile(count, total, most, lean):
    weights = [(1 << 20) // math.isqrt(rank ** lean) + 1 for rank in range(2, count + 1)]
    spare, counts = total - most - (count - 1), [1] * (count - 1)
    while spare > 0:
        free = [i for i in range(count - 1) if counts[i] < most]
        mass, remaining = sum([weights[i] for i in free]), spare
        for i in free:
            addition = min(most - counts[i], max(1, remaining * weights[i] // mass), spare)
            counts[i] = counts[i] + addition
            spare = spare - addition
    return np.array([most] + counts)


def uneven_parts(rng, number_of, total, most, slope):
    if number_of == 2:
        one = jax.random.randint(rng, (), max(1, total - most), min(most, total - 1) + 1)
        return jnp.stack([one, total - one])
    tallies = jnp.asarray(length_profile(number_of, total, most, slope), jnp.int32)
    twos = (number_of - 1) // 2
    source_of, receiver = tallies[1:1 + 2 * twos:2], tallies[2:2 + 2 * twos:2]
    margin = jnp.minimum(source_of - 1, most - receiver)
    passed = jax.random.randint(jax.random.fold_in(rng, 1), (twos,), 0, 1 << 20) % (margin + 1)
    tallies = tallies.at[1:1 + 2 * twos:2].set(source_of - passed).at[2:2 + 2 * twos:2].set(receiver + passed)
    return tallies[jax.random.permutation(jax.random.fold_in(rng, 2), number_of)]


def gaussian(key, extent, scale, limit, cuts=(), held_as=jnp.bfloat16):
    factor_of = block_levels(key, extent, cuts, -0.22, 0.18) if cuts else 1.0
    values = jax.random.normal(key, extent, jnp.float32) * scale * factor_of
    return jnp.minimum(jnp.maximum(values, -limit), limit).astype(held_as)


def setup_inputs(seed: int = 0) -> dict:
    splits = jax.random.split(jax.random.key(seed), 16)
    return {
        "inputs": gaussian(splits[0], (ROWS, ROW_LEN, D), 1.0, 6.0, ((0, 8), (1, 4))),
        "memory": gaussian(splits[1], (ROWS, MEM_LEN, D), 1.0, 6.0, ((0, 8), (1, 4))),
        "seg_ids": jax.vmap(lambda own: jnp.searchsorted(jnp.cumsum(uneven_parts(own, SEGS, ROW_LEN, ROW_LEN * 25 // 32, 2)), jnp.arange(ROW_LEN), side="right"))(jax.random.split(splits[2], ROWS)).reshape((ROWS, ROW_LEN)).astype(jnp.int32),
        "mem_lengths": jax.vmap(lambda own: uneven_parts(own, SEGS, MEM_LEN, MEM_LEN // 2, 2))(jax.random.split(splits[3], ROWS)).reshape((ROWS, SEGS)).astype(jnp.int32),
        "cotangent": gaussian(splits[4], (ROWS, ROW_LEN, D), 1.0, 6.0, ((0, 8), (1, 4))),
        "qkv_weight": gaussian(splits[5], (D, 3 * D), D ** -0.5, 0.25, ((0, 32),)),
        "self_out_weight": gaussian(splits[6], (D, D), (D // 16) ** -0.5, 1.0, ((0, 32),)),
        "cross_q_weight": gaussian(splits[7], (D, D), D ** -0.5, 0.25, ((0, 32),)),
        "cross_kv_weight": gaussian(splits[8], (D, 2 * D), D ** -0.5, 0.25, ((0, 32),)),
        "cross_out_weight": gaussian(splits[9], (D, D), (D // 16) ** -0.5, 1.0, ((0, 32),)),
        "ffn_in_weight": gaussian(splits[10], (D, FF), D ** -0.5, 0.25, ((0, 32),)),
        "ffn_in_bias": gaussian(splits[11], (FF,), 0.5, 3.0, ((0, 32),)),
        "ffn_out_weight": gaussian(splits[12], (FF, D), FF ** -0.5, 0.125, ((0, 32),)),
        "norm_gains": jnp.clip(1.0 + 0.18 * jax.random.normal(splits[13], (3, D), jnp.float32), 0.099609375, 1.8984375).astype(jnp.bfloat16),
        "shift_vectors": gaussian(splits[14], (4, D), 0.5, 3.0, ((1, 32),)),
    }


@jax.custom_vjp
def low(v):
    return lax.optimization_barrier(v.astype(jnp.bfloat16)).astype(jnp.float32)

@jax.custom_vjp
def low_back(v):
    return v

def low_keep(v):
    return (low(v), None)

def low_pass(kept, grad):
    return (grad,)

def back_keep(v):
    return (v, None)

def back_low(kept, grad):
    return (low(grad),)
low.defvjp(low_keep, low_pass)
low_back.defvjp(back_keep, back_low)

def product(left_side, right_side):
    return jnp.dot(left_side, right_side, precision=lax.Precision.HIGHEST)

def norm_rows(values, gain_row, shift_row):
    row_mean = lax.optimization_barrier(jnp.mean(values, axis=-1, keepdims=True))
    centered = values - row_mean
    spread = lax.optimization_barrier(jnp.mean(centered * centered, axis=-1, keepdims=True))
    return centered * lax.rsqrt(spread + 1e-05) * gain_row + shift_row

def attend(queries, keys_in, values_in, allowed):
    row_total = queries.shape[0]
    key_total = keys_in.shape[0]
    query_heads = queries.reshape(row_total, HEADS, HEAD)
    key_heads = keys_in.reshape(key_total, HEADS, HEAD)
    value_heads = values_in.reshape(key_total, HEADS, HEAD)
    scores = low_back(jnp.einsum('qhe,khe->hqk', query_heads, key_heads, precision=lax.Precision.HIGHEST)) * HEAD ** (-0.5)
    scores = jnp.where(allowed[None], scores, -1000000000.0)
    row_max = lax.optimization_barrier(jnp.max(scores, axis=-1, keepdims=True))
    weights = jnp.exp(scores - row_max)
    probs = weights / lax.optimization_barrier(jnp.sum(weights, axis=-1, keepdims=True))
    context = jnp.einsum('hqk,khe->qhe', low(probs), value_heads, precision=lax.Precision.HIGHEST)
    return low_back(low(context.reshape(row_total, D)))

def layer_row(params, row_full, mem_full, segments, mem_segments):
    self_qkv, self_proj, cross_query, cross_pair, cross_proj, ffn_up, ffn_bias, ffn_down, gain_rows, shift_rows = params
    places = jnp.arange(ROW_LEN, dtype=jnp.int32)
    causal = (places[None, :] <= places[:, None]) & (segments[:, None] == segments[None, :])
    qkv = low_back(low(product(row_full, self_qkv))).reshape(ROW_LEN, 3, D)
    self_ctx = attend(qkv[:, 0], qkv[:, 1], qkv[:, 2], causal)
    attn_out = low_back(product(self_ctx, self_proj))
    first = norm_rows(row_full + attn_out, gain_rows[0], shift_rows[0])
    cross_q = low_back(low(product(low(first), cross_query)))
    mem_kv = low_back(low(product(mem_full, cross_pair))).reshape(MEM_LEN, 2, D)
    reach = segments[:, None] == mem_segments[None, :]
    cross_ctx = attend(cross_q, mem_kv[:, 0], mem_kv[:, 1], reach)
    cross_out = low_back(product(cross_ctx, cross_proj))
    second = norm_rows(first + cross_out, gain_rows[1], shift_rows[1])
    pre_act = low_back(product(low(second), ffn_up) + ffn_bias)
    hidden = low(jax.nn.gelu(pre_act))
    ffn_out = low_back(product(hidden, ffn_down)) + shift_rows[3]
    return norm_rows(second + ffn_out + row_full, gain_rows[2], shift_rows[2])

def reference(inputs, memory, seg_ids, mem_lengths, cotangent, qkv_weight, self_out_weight, cross_q_weight, cross_kv_weight, cross_out_weight, ffn_in_weight, ffn_in_bias, ffn_out_weight, norm_gains, shift_vectors):
    params = tuple((weight_arr.astype(jnp.float32) for weight_arr in (qkv_weight, self_out_weight, cross_q_weight, cross_kv_weight, cross_out_weight, ffn_in_weight, ffn_in_bias, ffn_out_weight, norm_gains, shift_vectors)))

    def one_row(summed, packed):
        row_in, mem_in, segments, lengths, row_cot = packed
        ends = jnp.cumsum(lengths).astype(jnp.int32)
        positions = jnp.arange(MEM_LEN, dtype=jnp.int32)
        mem_segments = lax.optimization_barrier(jnp.sum((positions[:, None] >= ends[None, :]).astype(jnp.int32), axis=1)).astype(jnp.int32)

        def forward(weight_set, row_full, mem_full):
            return layer_row(weight_set, row_full, mem_full, segments, mem_segments)
        result, pullback = jax.vjp(forward, params, row_in.astype(jnp.float32), mem_in.astype(jnp.float32))
        weight_grads, row_grad, mem_grad = pullback(row_cot.astype(jnp.float32))
        summed = jax.tree.map(jnp.add, summed, weight_grads)
        return (summed, (result.astype(jnp.bfloat16), row_grad, mem_grad))
    initial = tuple((jnp.zeros(weight_arr.shape, jnp.float32) for weight_arr in params))
    summed, (outputs, row_grads, mem_grads) = lax.scan(one_row, initial, (inputs, memory, seg_ids, mem_lengths, cotangent))
    return (outputs, row_grads, mem_grads, summed[0], summed[1], summed[2], summed[3], summed[4], summed[5], summed[6], summed[7], summed[8], summed[9])
```

```python
import functools

import jax
import jax.numpy as jnp
from jax import lax
from jax.experimental import pallas as pl
from jax.experimental.pallas import tpu as pltpu
from jax.sharding import PartitionSpec as P

HEAD = 64
PAIR = 2 * HEAD
TILE = 256
FAST = 32
AXES = ("dp", "seq")
LOG2E = 1.4426950408889634
AWAY = -1e30
GELU_A = 0.7978845608028654
GELU_B = 0.044715
BF = jnp.bfloat16
F4 = jnp.float32
VMEM_BYTES = 58 << 20


def mm(a, b):
    return lax.dot_general(a, b, (((1,), (0,)), ((), ())), preferred_element_type=F4)


def mt(a, b):
    return lax.dot_general(a, b, (((1,), (1,)), ((), ())), preferred_element_type=F4)


def tm(a, b):
    return lax.dot_general(a, b, (((0,), (0,)), ((), ())), preferred_element_type=F4)


def any_spec():
    return pl.BlockSpec(memory_space=pl.ANY)


def smem_spec():
    return pl.BlockSpec(memory_space=pltpu.SMEM)


def struct(shape, dtype):
    return jax.ShapeDtypeStruct(shape, dtype)


def params(**more):
    return pltpu.CompilerParams(vmem_limit_bytes=VMEM_BYTES, **more)


def cost(flops, bytes_accessed):
    return pl.CostEstimate(flops=int(flops), bytes_accessed=int(bytes_accessed), transcendentals=0)


def rel(p):
    return ((p % 4) << 3) | (((p >> 2) & 1) << 1) | (((p >> 3) & 1) << 2) | (p >> 4)


def wait_all(buffer, sem):
    pltpu.make_async_copy(buffer, buffer, sem).wait()


def start_rows(dst, own, got, seat, sem):
    span = own.shape[1]
    for r in range(len(got) + 1):
        src = own.at[seat] if r == 0 else got[r - 1]
        place = pl.multiple_of((seat ^ r) * span, span)
        pltpu.make_async_copy(src, dst.at[pl.ds(place, span)], sem).start()


def start_weight(dst, parts, first, me, sem):
    rows, columns = dst.shape
    if len(parts) == 1:
        pltpu.make_async_copy(parts[0].at[:, pl.ds(first, columns)], dst, sem).start()
        return
    span = rows // FAST
    for p in range(FAST):
        place = pl.multiple_of((me ^ rel(p)) * span, span)
        src = parts[p // 16].at[pl.ds((p % 16) * span, span), pl.ds(first, columns)]
        pltpu.make_async_copy(src, dst.at[pl.ds(place, span)], sem).start()


def start_grad(src, parts, me, sem):
    if len(parts) == 1:
        pltpu.make_async_copy(src, parts[0], sem).start()
        return
    span = src.shape[0] // FAST
    for p in range(FAST):
        place = pl.multiple_of((me ^ rel(p)) * span, span)
        dst = parts[p // 16].at[pl.ds((p % 16) * span, span)]
        pltpu.make_async_copy(src.at[pl.ds(place, span)], dst, sem).start()


def start_blocks(src, outs, seat, sem):
    span = outs[0].shape[0]
    for r, out in enumerate(outs):
        place = pl.multiple_of((seat ^ r) * span, span)
        pltpu.make_async_copy(src.at[pl.ds(place, span)], out, sem).start()


def grad_shapes(rows, columns, fast):
    if fast:
        return [struct((rows // 2, columns), BF)] * 2
    return [struct((rows, columns), BF)]


def norm(values):
    centered = values - jnp.mean(values, axis=-1, keepdims=True)
    inverse = lax.rsqrt(jnp.mean(centered * centered, axis=-1, keepdims=True) + 1e-05)
    return centered * inverse, inverse


def norm_back(upstream, normed, inverse, gain_row):
    gain_part = jnp.sum(upstream * normed, axis=0, keepdims=True)
    shift_part = jnp.sum(upstream, axis=0, keepdims=True)
    scaled = upstream * gain_row
    centered = scaled - jnp.mean(scaled, axis=-1, keepdims=True)
    value = inverse * (centered - normed * jnp.mean(scaled * normed, axis=-1, keepdims=True))
    return value, gain_part, shift_part


def lane_masks(dtype):
    lane = lax.broadcasted_iota(jnp.int32, (1, PAIR), 1)
    own = [(lane // HEAD == h).astype(dtype) for h in range(2)]

    def spot(h, k):
        return ((lane // HEAD == 1 - h) & (lane % HEAD == k)).astype(dtype)

    return own, spot


def attend_pair(causal, query, key, value, augq, augk, tri, ctx_out, qa_out, ka_out):
    total = key.shape[0]
    own, spot = lane_masks(F4)
    own_low = [mask.astype(BF) for mask in own]
    eighth = [(mask * HEAD ** (-0.5)).astype(BF) for mask in own]
    wide = jnp.concatenate([value, jnp.ones((total, PAIR), BF)], axis=1)
    keys = []
    for h in range(2):
        keys.append(key * own_low[h] + augk[h])
        ka_out[h] = keys[h]
    units = [(i, h) for i in range(query.shape[0] // TILE) for h in range(2)]
    scores, probs, halves = {}, {}, {}

    def score(i, h):
        rows = slice(i * TILE, (i + 1) * TILE)
        width = (i + 1) * TILE if causal else total
        head = query[rows] * eighth[h] + augq[h, rows]
        s = mt(head, keys[h][:width])
        if causal:
            tail = s[:, width - TILE :] + tri[...]
            s = jnp.concatenate([s[:, : width - TILE], tail], axis=1) if i else tail
        return s, head

    def finish(i, h, low, top, head):
        rows = slice(i * TILE, (i + 1) * TILE)
        both = mm(low, wide[: low.shape[1]])
        sums = both[:, PAIR:]
        halves[h] = both[:, :PAIR] / sums
        rest = -(top + jnp.log(sums))
        high = rest.astype(BF).astype(F4)
        rest = rest - high
        middle = rest.astype(BF).astype(F4)
        extra = high * spot(h, 8) + middle * spot(h, 9) + (rest - middle) * spot(h, 10)
        qa_out[h, rows] = head + extra.astype(BF)
        if h == 1:
            ctx_out[rows] = (halves[0] * own[0] + halves[1] * own[1]).astype(BF)

    count = len(units)
    for t in range(count + 2):
        if t < count:
            scores[t] = score(*units[t])
        if 0 <= t - 2 < count:
            finish(*units[t - 2], *probs.pop(t - 2))
        if 0 <= t - 1 < count:
            s, head = scores.pop(t - 1)
            top = jnp.max(s, axis=1, keepdims=True)
            low = jnp.exp2(s * LOG2E - top * LOG2E).astype(BF)
            probs[t - 1] = (low, top, head)


def self_forward_kernel(seats, nparts, *refs):
    place, own = refs[0], refs[1]
    got = refs[2 : 1 + seats]
    rest = refs[1 + seats :]
    parts = rest[:nparts]
    augq, augk, tri, ctx, qa, ka, vo, x_v, w_v, qkv, sems = rest[nparts:]
    pair = pl.program_id(0)
    width = x_v.shape[1]

    @pl.when(pair == 0)
    def _():
        seat, me = place[0], place[1]
        start_rows(x_v, own, got, seat, sems.at[0])
        start_weight(w_v, parts, 0, me, sems.at[1])
        wait_all(x_v, sems.at[0])
        wait_all(w_v, sems.at[1])
        for c in range(0, 3 * width, 512):
            qkv[:, c : c + 512] = mm(x_v[...], w_v[:, c : c + 512]).astype(BF)

    def columns(part):
        return qkv[:, pl.ds(pl.multiple_of(part * width + pair * PAIR, PAIR), PAIR)]

    value = columns(2)
    vo[...] = value
    attend_pair(True, columns(0), columns(1), value, augq, augk, tri, ctx, qa, ka)


def self_forward(place, own, got, parts, augq, augk, tri):
    seats, span, width = own.shape
    full = seats * span
    heads = width // HEAD
    both = pl.BlockSpec((2, full, PAIR), lambda p: (p, 0, 0))
    cols = pl.BlockSpec((full, PAIR), lambda p: (0, p))
    return pl.pallas_call(
        functools.partial(self_forward_kernel, seats, len(parts)),
        name="self_forward",
        grid=(heads // 2,),
        in_specs=[smem_spec()]
        + [any_spec()] * (seats + len(parts))
        + [
            pl.BlockSpec((2, full, PAIR), lambda p: (0, 0, 0)),
            pl.BlockSpec((2, full, PAIR), lambda p: (0, 0, 0)),
            pl.BlockSpec((TILE, TILE), lambda p: (0, 0)),
        ],
        out_specs=[cols, both, both, cols],
        out_shape=[
            struct((full, width), BF),
            struct((heads, full, PAIR), BF),
            struct((heads, full, PAIR), BF),
            struct((full, width), BF),
        ],
        scratch_shapes=[
            pltpu.VMEM((full, width), BF),
            pltpu.VMEM((width, 3 * width), BF),
            pltpu.VMEM((full, 3 * width), BF),
            pltpu.SemaphoreType.DMA((2,)),
        ],
        compiler_params=params(),
        cost_estimate=cost(11e9, 8e6),
    )(place, own, *got, *parts, augq, augk, tri)


def cross_forward_kernel(seats, nparts, *refs):
    place, x_own = refs[0], refs[1]
    x_got = refs[2 : 1 + seats]
    mem_own = refs[1 + seats]
    mem_got = refs[2 + seats : 1 + 2 * seats]
    rest = refs[1 + 2 * seats :]
    parts = rest[:nparts]
    (ctx, vec, augq, augk, cctx, qa, ka, vo, xhat, inv, x_v, m_v, w_v, q_v, kv, sems) = rest[nparts:]
    pair = pl.program_id(0)
    full, width = x_v.shape

    @pl.when(pair == 0)
    def _():
        seat, me = place[0], place[1]
        start_weight(w_v, parts, 0, me, sems.at[0])
        start_rows(x_v, x_own, x_got, seat, sems.at[1])
        start_rows(m_v, mem_own, mem_got, seat, sems.at[2])
        wait_all(w_v, sems.at[0])
        wait_all(x_v, sems.at[1])
        for i in range(0, full, TILE):
            rows = slice(i, i + TILE)
            attn = mm(ctx[rows], w_v[:, :width])
            normed, inverse = norm(x_v[rows].astype(F4) + attn)
            xhat[rows] = normed
            inv[rows] = jnp.broadcast_to(inverse, (TILE, PAIR))
            first = (normed * vec[0:1] + vec[3:4]).astype(BF)
            q_v[rows] = mm(first, w_v[:, width : 2 * width]).astype(BF)
        wait_all(m_v, sems.at[2])
        for c in range(0, 2 * width, 512):
            kv[:, c : c + 512] = mm(m_v[...], w_v[:, 2 * width + c : 2 * width + c + 512]).astype(BF)

    lanes = pl.ds(pl.multiple_of(pair * PAIR, PAIR), PAIR)
    late = pl.ds(pl.multiple_of(width + pair * PAIR, PAIR), PAIR)
    value = kv[:, late]
    vo[...] = value
    attend_pair(False, q_v[:, lanes], kv[:, lanes], value, augq, augk, None, cctx, qa, ka)


def cross_forward(place, x_own, x_got, mem_own, mem_got, parts, ctx, vec, augq, augk):
    seats, span, width = x_own.shape
    full = seats * span
    heads = width // HEAD
    both = pl.BlockSpec((2, full, PAIR), lambda p: (p, 0, 0))
    cols = pl.BlockSpec((full, PAIR), lambda p: (0, p))
    return pl.pallas_call(
        functools.partial(cross_forward_kernel, seats, len(parts)),
        name="cross_forward",
        grid=(heads // 2,),
        in_specs=[smem_spec()]
        + [any_spec()] * (2 * seats + len(parts))
        + [
            pl.BlockSpec((full, width), lambda p: (0, 0)),
            pl.BlockSpec(vec.shape, lambda p: (0, 0)),
            pl.BlockSpec((2, full, PAIR), lambda p: (0, 0, 0)),
            pl.BlockSpec((2, full, PAIR), lambda p: (0, 0, 0)),
        ],
        out_specs=[
            cols,
            both,
            both,
            cols,
            pl.BlockSpec((full, width), lambda p: (0, 0)),
            pl.BlockSpec((full, PAIR), lambda p: (0, 0)),
        ],
        out_shape=[
            struct((full, width), BF),
            struct((heads, full, PAIR), BF),
            struct((heads, full, PAIR), BF),
            struct((full, width), BF),
            struct((full, width), F4),
            struct((full, PAIR), F4),
        ],
        scratch_shapes=[
            pltpu.VMEM((full, width), BF),
            pltpu.VMEM((full, width), BF),
            pltpu.VMEM((width, 4 * width), BF),
            pltpu.VMEM((full, width), BF),
            pltpu.VMEM((full, 2 * width), BF),
            pltpu.SemaphoreType.DMA((3,)),
        ],
        compiler_params=params(),
        cost_estimate=cost(15e9, 14e6),
    )(place, x_own, *x_got, mem_own, *mem_got, *parts, ctx, vec, augq, augk)


def middle_kernel(seats, nparts, *refs):
    place, x_own = refs[0], refs[1]
    x_got = refs[2 : 1 + seats]
    g_own = refs[1 + seats]
    g_got = refs[2 + seats : 1 + 2 * seats]
    rest = refs[1 + 2 * seats :]
    co_parts, rest = rest[:nparts], rest[nparts:]
    up_parts, rest = rest[:nparts], rest[nparts:]
    down_parts, rest = rest[:nparts], rest[nparts:]
    (cctx, xhat, vec, bias), rest = rest[:4], rest[4:]
    outs, rest = rest[:seats], rest[seats:]
    (d3_o, d2_o, dcctx, vec_o, bias_o), rest = rest[:5], rest[5:]
    upco_g, rest = rest[:nparts], rest[nparts:]
    down_g, rest = rest[:nparts], rest[nparts:]
    (x_v, g_v, co_v, up_v, down_v, out_v, s_v, h_v, dp_v, df_v, dc_v, gu_v, gd_v, sems) = rest
    full, width = x_v.shape
    hidden = up_v.shape[1]
    seat, me = place[0], place[1]
    start_weight(co_v, co_parts, 4 * width, me, sems.at[0])
    start_weight(up_v, up_parts, 0, me, sems.at[1])
    start_weight(down_v, down_parts, 0, me, sems.at[2])
    start_rows(x_v, x_own, x_got, seat, sems.at[3])
    start_rows(g_v, g_own, g_got, seat, sems.at[4])
    vec_o[...] = jnp.zeros(vec_o.shape, F4)
    bias_o[...] = jnp.zeros(bias_o.shape, F4)
    wait_all(co_v, sems.at[0])
    wait_all(up_v, sems.at[1])
    wait_all(down_v, sems.at[2])
    wait_all(x_v, sems.at[3])
    wait_all(g_v, sems.at[4])

    def tile(i, carry):
        rows = pl.ds(pl.multiple_of(i * TILE, TILE), TILE)
        first = xhat[rows] * vec[0:1] + vec[3:4]
        normed_one, inverse_one = norm(first + mm(cctx[rows], co_v[...]))
        second = normed_one * vec[1:2] + vec[4:5]
        low = second.astype(BF)
        s_v[rows] = low
        pre = mm(low, up_v[...]) + bias[...]
        square = pre * pre
        slope = GELU_A * GELU_B * square + GELU_A
        t = jnp.tanh(pre * slope)
        half = 0.5 * t + 0.5
        hid = (pre * half).astype(BF)
        h_v[rows] = hid
        d_gelu = half + (0.5 - 0.5 * t * t) * pre * (3.0 * slope - 2.0 * GELU_A)
        ffn = mm(hid, down_v[...]) + vec[6:7]
        normed_two, inverse_two = norm(second + ffn + x_v[rows].astype(F4))
        out_v[rows] = (normed_two * vec[2:3] + vec[5:6]).astype(BF)
        d_three, gain_two, shift_two = norm_back(g_v[rows].astype(F4), normed_two, inverse_two, vec[2:3])
        d3_o[rows] = d_three
        df = d_three.astype(BF)
        df_v[rows] = df
        d_pre = (mt(df, down_v[...]) * d_gelu).astype(BF)
        dp_v[rows] = d_pre
        bias_o[...] += jnp.sum(d_pre.astype(F4), axis=0, keepdims=True)
        d_second = d_three + mt(d_pre, up_v[...])
        d_two, gain_one, shift_one = norm_back(d_second, normed_one, inverse_one, vec[1:2])
        d2_o[rows] = d_two
        dc = d_two.astype(BF)
        dc_v[rows] = dc
        dcctx[rows] = mt(dc, co_v[...]).astype(BF)
        vec_o[1:2] += gain_one
        vec_o[2:3] += gain_two
        vec_o[4:5] += shift_one
        vec_o[5:6] += shift_two
        vec_o[6:7] += jnp.sum(d_three, axis=0, keepdims=True)
        return carry

    lax.fori_loop(0, full // TILE, tile, 0)
    start_blocks(out_v, outs, seat, sems.at[0])
    for c in range(0, hidden, 512):
        gd_v[c : c + 512] = tm(h_v[:, c : c + 512], df_v[...]).astype(BF)
    start_grad(gd_v, down_g, me, sems.at[1])
    for c in range(0, hidden, 512):
        gu_v[:, c : c + 512] = tm(s_v[...], dp_v[:, c : c + 512]).astype(BF)
    gu_v[:, hidden:] = tm(cctx[...], dc_v[...]).astype(BF)
    start_grad(gu_v, upco_g, me, sems.at[2])
    wait_all(out_v, sems.at[0])
    wait_all(gd_v, sems.at[1])
    wait_all(gu_v, sems.at[2])


def middle(place, x_own, x_got, g_own, g_got, co_parts, up_parts, down_parts, cctx, xhat, vec, bias, fast):
    seats, span, width = x_own.shape
    full = seats * span
    hidden = bias.shape[1]
    whole = pl.BlockSpec(memory_space=pltpu.VMEM)
    nparts = len(co_parts)
    out_shape = (
        [struct((span, width), BF)] * seats
        + [struct((full, width), F4), struct((full, width), F4), struct((full, width), BF)]
        + [struct((8, width), F4), struct((1, hidden), F4)]
        + grad_shapes(width, hidden + width, fast)
        + grad_shapes(hidden, width, fast)
    )
    result = pl.pallas_call(
        functools.partial(middle_kernel, seats, nparts),
        name="middle",
        in_specs=[smem_spec()] + [any_spec()] * (2 * seats + 3 * nparts) + [whole] * 4,
        out_specs=[any_spec()] * seats + [whole] * 5 + [any_spec()] * (2 * nparts),
        out_shape=out_shape,
        scratch_shapes=[
            pltpu.VMEM((full, width), BF),
            pltpu.VMEM((full, width), BF),
            pltpu.VMEM((width, width), BF),
            pltpu.VMEM((width, hidden), BF),
            pltpu.VMEM((hidden, width), BF),
            pltpu.VMEM((full, width), BF),
            pltpu.VMEM((full, width), BF),
            pltpu.VMEM((full, hidden), BF),
            pltpu.VMEM((full, hidden), BF),
            pltpu.VMEM((full, width), BF),
            pltpu.VMEM((full, width), BF),
            pltpu.VMEM((width, hidden + width), BF),
            pltpu.VMEM((hidden, width), BF),
            pltpu.SemaphoreType.DMA((5,)),
        ],
        compiler_params=params(),
        cost_estimate=cost(20e9, 25e6),
    )(place, x_own, *x_got, g_own, *g_got, *co_parts, *up_parts, *down_parts, cctx, xhat, vec, bias)
    outs, rest = result[:seats], result[seats:]
    return outs, rest[:5], rest[5 : 5 + nparts], rest[5 + nparts :]


def attend_back_kernel(causal, qa, ka, value, ctx, dctx, tri, dq, dk, dv):
    own, spot = lane_masks(F4)
    total = value.shape[0]
    blocks = total // TILE
    upstream = dctx[...].astype(F4)
    product = upstream * ctx[...].astype(F4)
    row = lax.broadcasted_iota(jnp.int32, (PAIR, PAIR), 0) // HEAD
    col = lax.broadcasted_iota(jnp.int32, (PAIR, PAIR), 1) // HEAD
    swap = jnp.where(row != col, -1.0, 0.0).astype(BF)
    high = product.astype(BF)
    delta = mm(high, swap) + mm((product - high.astype(F4)).astype(BF), swap)
    delta_high = delta.astype(BF).astype(F4)
    delta_low = delta - delta_high
    values = value[...].astype(F4)
    d_query, d_key, d_value = [], [], []
    for h in range(2):
        spots = spot(h, 0) + spot(h, 1)
        do = (upstream * own[h] + delta_high * spot(h, 0) + delta_low * spot(h, 1)).astype(BF)
        va = (values * own[h] + spots).astype(BF)
        query, key = qa[h], ka[h]
        query_t = query.T[h * HEAD : (h + 1) * HEAD]
        do_t = do.T[h * HEAD : (h + 1) * HEAD]
        keys, vals, sums = [], [], [None] * blocks
        for j in range(blocks):
            start = j * TILE if causal else 0
            key_j, va_j = key[j * TILE : (j + 1) * TILE], va[j * TILE : (j + 1) * TILE]
            s = mt(query[start:], key_j)
            if causal:
                head = s[:TILE] + tri[...]
                s = jnp.concatenate([head, s[TILE:]], axis=0) if j < blocks - 1 else head
            prob = jnp.exp2(s * LOG2E)
            ds = (prob * mt(do[start:], va_j)).astype(BF)
            vals.append(mm(do_t[:, start:], prob.astype(BF)))
            keys.append(mm(query_t[:, start:], ds))
            back = mm(ds, key_j)
            for i in range(start // TILE, blocks):
                part = back[i * TILE - start : (i + 1) * TILE - start]
                sums[i] = part if sums[i] is None else sums[i] + part
        d_query.append(jnp.concatenate(sums, axis=0))
        d_key.append(jnp.concatenate(keys, axis=1))
        d_value.append(jnp.concatenate(vals, axis=1))
    dq[...] = ((d_query[0] * own[0] + d_query[1] * own[1]) * HEAD ** (-0.5)).astype(BF)
    dk[...] = jnp.concatenate(d_key, axis=0).T.astype(BF)
    dv[...] = jnp.concatenate(d_value, axis=0).T.astype(BF)


def attend_back(causal, qa, ka, value, ctx, dctx, tri):
    full, width = value.shape
    both = pl.BlockSpec((2, full, PAIR), lambda p: (p, 0, 0))
    cols = pl.BlockSpec((full, PAIR), lambda p: (0, p))
    return pl.pallas_call(
        functools.partial(attend_back_kernel, causal),
        name="self_back" if causal else "cross_back",
        grid=(width // PAIR,),
        in_specs=[both, both, cols, cols, cols, pl.BlockSpec((TILE, TILE), lambda p: (0, 0))],
        out_specs=[cols] * 3,
        out_shape=[struct((full, width), BF)] * 3,
        compiler_params=params(),
        cost_estimate=cost(20e9, 10e6),
    )(qa, ka, value, ctx, dctx, tri)


def cross_grads_kernel(seats, nparts, *refs):
    place, mem_own = refs[0], refs[1]
    mem_got = refs[2 : 1 + seats]
    rest = refs[1 + seats :]
    parts, rest = rest[:nparts], rest[nparts:]
    (dq, dk, dv, ctx, xhat, inv, d2, d3, vec), rest = rest[:9], rest[9:]
    outs, rest = rest[:seats], rest[seats:]
    (d13, dctx, vec_o), rest = rest[:3], rest[3:]
    grads, rest = rest[:nparts], rest[nparts:]
    (m_v, w_v, mg_v, f_v, da_v, g_v, sems) = rest
    full, width = m_v.shape
    seat, me = place[0], place[1]
    start_weight(w_v, parts, 0, me, sems.at[0])
    start_rows(m_v, mem_own, mem_got, seat, sems.at[1])
    vec_o[...] = jnp.zeros(vec_o.shape, F4)
    wait_all(w_v, sems.at[0])
    wait_all(m_v, sems.at[1])

    def tile(i, carry):
        rows = pl.ds(pl.multiple_of(i * TILE, TILE), TILE)
        normed = xhat[rows]
        f_v[rows] = (normed * vec[0:1] + vec[3:4]).astype(BF)
        d_first = d2[rows] + mt(dq[rows], w_v[:, width : 2 * width])
        inverse = jnp.concatenate([inv[rows]] * (width // PAIR), axis=1)
        d_one, gain, shift = norm_back(d_first, normed, inverse, vec[0:1])
        d13[rows] = d3[rows] + d_one
        da = d_one.astype(BF)
        da_v[rows] = da
        dctx[rows] = mt(da, w_v[:, :width]).astype(BF)
        vec_o[0:1] += gain
        vec_o[3:4] += shift
        back = mt(dk[rows], w_v[:, 2 * width : 3 * width]) + mt(dv[rows], w_v[:, 3 * width :])
        mg_v[rows] = back.astype(BF)
        return carry

    lax.fori_loop(0, full // TILE, tile, 0)
    start_blocks(mg_v, outs, seat, sems.at[0])
    g_v[:, :width] = tm(ctx[...], da_v[...]).astype(BF)
    g_v[:, width : 2 * width] = tm(f_v[...], dq[...]).astype(BF)
    g_v[:, 2 * width : 3 * width] = tm(m_v[...], dk[...]).astype(BF)
    g_v[:, 3 * width :] = tm(m_v[...], dv[...]).astype(BF)
    start_grad(g_v, grads, me, sems.at[1])
    wait_all(mg_v, sems.at[0])
    wait_all(g_v, sems.at[1])


def cross_grads(place, mem_own, mem_got, parts, dq, dk, dv, ctx, xhat, inv, d2, d3, vec, fast):
    seats, span, width = mem_own.shape
    full = seats * span
    nparts = len(parts)
    whole = pl.BlockSpec(memory_space=pltpu.VMEM)
    result = pl.pallas_call(
        functools.partial(cross_grads_kernel, seats, nparts),
        name="cross_grads",
        in_specs=[smem_spec()] + [any_spec()] * (seats + nparts) + [whole] * 9,
        out_specs=[any_spec()] * seats + [whole] * 3 + [any_spec()] * nparts,
        out_shape=[struct((span, width), BF)] * seats
        + [struct((full, width), F4), struct((full, width), BF), struct((8, width), F4)]
        + grad_shapes(width, 4 * width, fast),
        scratch_shapes=[
            pltpu.VMEM((full, width), BF),
            pltpu.VMEM((width, 4 * width), BF),
            pltpu.VMEM((full, width), BF),
            pltpu.VMEM((full, width), BF),
            pltpu.VMEM((full, width), BF),
            pltpu.VMEM((width, 4 * width), BF),
            pltpu.SemaphoreType.DMA((2,)),
        ],
        compiler_params=params(),
        cost_estimate=cost(5e9, 20e6),
    )(place, mem_own, *mem_got, *parts, dq, dk, dv, ctx, xhat, inv, d2, d3, vec)
    return result[:seats], result[seats : seats + 3], result[seats + 3 :]


def self_grads_kernel(seats, nparts, *refs):
    place, x_own = refs[0], refs[1]
    x_got = refs[2 : 1 + seats]
    rest = refs[1 + seats :]
    parts, rest = rest[:nparts], rest[nparts:]
    (dq, dk, dv, d13), rest = rest[:4], rest[4:]
    outs, rest = rest[:seats], rest[seats:]
    grads, rest = rest[:nparts], rest[nparts:]
    (x_v, w_v, ig_v, g_v, sems) = rest
    full, width = x_v.shape
    seat, me = place[0], place[1]
    start_rows(x_v, x_own, x_got, seat, sems.at[0])
    start_weight(w_v, parts, 0, me, sems.at[1])
    wait_all(x_v, sems.at[0])
    for c, d in enumerate((dq, dk, dv)):
        g_v[:, c * width : (c + 1) * width] = tm(x_v[...], d[...]).astype(BF)
    start_grad(g_v, grads, me, sems.at[0])
    wait_all(w_v, sems.at[1])
    for i in range(0, full, TILE):
        rows = slice(i, i + TILE)
        back = d13[rows]
        for c, d in enumerate((dq, dk, dv)):
            back = back + mt(d[rows], w_v[:, c * width : (c + 1) * width])
        ig_v[rows] = back.astype(BF)
    start_blocks(ig_v, outs, seat, sems.at[1])
    wait_all(g_v, sems.at[0])
    wait_all(ig_v, sems.at[1])


def self_grads(place, x_own, x_got, parts, dq, dk, dv, d13, fast):
    seats, span, width = x_own.shape
    full = seats * span
    nparts = len(parts)
    whole = pl.BlockSpec(memory_space=pltpu.VMEM)
    result = pl.pallas_call(
        functools.partial(self_grads_kernel, seats, nparts),
        name="self_grads",
        in_specs=[smem_spec()] + [any_spec()] * (seats + nparts) + [whole] * 4,
        out_specs=[any_spec()] * (seats + nparts),
        out_shape=[struct((span, width), BF)] * seats + grad_shapes(width, 3 * width, fast),
        scratch_shapes=[
            pltpu.VMEM((full, width), BF),
            pltpu.VMEM((width, 3 * width), BF),
            pltpu.VMEM((full, width), BF),
            pltpu.VMEM((width, 3 * width), BF),
            pltpu.SemaphoreType.DMA((2,)),
        ],
        compiler_params=params(),
        cost_estimate=cost(3.5e9, 12e6),
    )(place, x_own, *x_got, *parts, dq, dk, dv, d13)
    return result[:seats], result[seats:]


def unpack_kernel(place, *refs):
    out = refs[-1]
    for r, block in enumerate(refs[:-1]):
        out[place[0] ^ r] = block[...].astype(out.dtype)


def unpack(place, blocks, dtype):
    span, width = blocks[0].shape
    seats = len(blocks)
    whole = pl.BlockSpec(memory_space=pltpu.VMEM)
    return pl.pallas_call(
        unpack_kernel,
        name="unpack",
        in_specs=[smem_spec()] + [whole] * seats,
        out_specs=whole,
        out_shape=struct((seats, span, width), dtype),
        compiler_params=params(),
        cost_estimate=cost(0, 3e6),
    )(place, *blocks)


def pick_kernel(count, place, *refs):
    sources, outs, sem = refs[:count], refs[count:-1], refs[-1]
    seats = sources[0].shape[0]
    copies = []
    for n, out in enumerate(outs):
        src = sources[n // (seats - 1)].at[place[0] ^ (n % (seats - 1) + 1)]
        copies.append(pltpu.make_async_copy(src, out, sem.at[n]))
    for copy in copies:
        copy.start()
    for copy in copies:
        copy.wait()


def pick(place, *sources):
    seats, span, width = sources[0].shape
    number = len(sources) * (seats - 1)
    outs = pl.pallas_call(
        functools.partial(pick_kernel, len(sources)),
        name="pick",
        in_specs=[smem_spec()] + [any_spec()] * len(sources),
        out_specs=[any_spec()] * number,
        out_shape=[struct((span, width), BF)] * number,
        scratch_shapes=[pltpu.SemaphoreType.DMA((number,))],
        compiler_params=params(),
        cost_estimate=cost(0, 2e6),
    )(place, *sources)
    return [outs[k * (seats - 1) : (k + 1) * (seats - 1)] for k in range(len(sources))]


def swap_seats(blocks, seats):
    return [
        lax.ppermute(block, "seq", [(i, i ^ (r + 1)) for i in range(seats)]) for r, block in enumerate(blocks)
    ]


def swap(value, bits):
    return lax.ppermute(value, AXES, [(i, i ^ bits) for i in range(FAST)])


def gather_chain(shard):
    held = jnp.concatenate([shard] + [swap(shard, z << 3) for z in (1, 2, 3)], axis=0)
    for bits in (2, 4):
        held = jnp.concatenate([held, swap(held, bits)], axis=0)
    return [held, swap(held, 1)]


def reduce_chain(parts):
    keep, send = parts
    total = keep.astype(F4) + swap(send, 1).astype(F4)
    for bits in (4, 2):
        half = total.shape[0] // 2
        total = total[:half] + swap(total[half:].astype(BF), bits).astype(F4)
    span = total.shape[0] // 4
    result = total[:span]
    for z in (1, 2, 3):
        result = result + swap(total[z * span : (z + 1) * span].astype(BF), z << 3).astype(F4)
    return result


def on_device(
    inputs,
    memory,
    seg_ids,
    mem_lengths,
    cotangent,
    qkv_weight,
    self_out_weight,
    cross_q_weight,
    cross_kv_weight,
    cross_out_weight,
    ffn_in_weight,
    ffn_in_bias,
    ffn_out_weight,
    norm_gains,
    shift_vectors,
):
    seats = lax.axis_size("seq")
    devices = lax.axis_size("dp") * seats
    span, width = inputs.shape[1:]
    full = seats * span
    seat = lax.axis_index("seq")
    me = lax.axis_index("dp") * seats + seat
    fast = devices == FAST and qkv_weight.shape[0] % 16 == 0
    place = jnp.stack([seat, me]).astype(jnp.int32)

    x_send = pick(place, inputs)[0]
    x_got = swap_seats(x_send, seats)
    second_group = [self_out_weight, cross_q_weight, cross_kv_weight, cross_out_weight]
    if fast:
        qkv_parts = gather_chain(qkv_weight)
        rows, piece = qkv_weight.shape[0], norm_gains.shape[1]
        bias_piece = ffn_in_bias.shape[0]
        block = jnp.concatenate(
            [
                jnp.pad(norm_gains, ((0, 0), (0, PAIR - piece))),
                jnp.pad(shift_vectors, ((0, 0), (0, PAIR - piece))),
                jnp.pad(ffn_in_bias[None], ((0, rows - 8), (0, PAIR - bias_piece))),
            ],
            axis=0,
        )
        two_parts = gather_chain(jnp.concatenate(second_group + [block], axis=1))
        up_parts = gather_chain(ffn_in_weight)
        down_parts = gather_chain(ffn_out_weight)
        blocks = jnp.concatenate([part[:, 5 * width :].reshape(16, rows * PAIR) for part in two_parts], axis=0)
        order = jnp.asarray([rel(p) for p in range(FAST)], jnp.int32)
        chosen = (order[None, :] ^ me) == jnp.arange(FAST, dtype=jnp.int32)[:, None]
        natural = jnp.dot(chosen.astype(BF), blocks, preferred_element_type=F4).reshape(FAST, rows, PAIR)
        vec = jnp.transpose(natural[:, :8, :piece], (1, 0, 2)).reshape(8, FAST * piece)
        bias = natural[:, 7, :bias_piece].reshape(1, FAST * bias_piece)
    else:
        qkv_parts = [lax.all_gather(qkv_weight, AXES, axis=0, tiled=True)]
        two_parts = [lax.all_gather(jnp.concatenate(second_group, axis=1), AXES, axis=0, tiled=True)]
        up_parts = [lax.all_gather(ffn_in_weight, AXES, axis=0, tiled=True)]
        down_parts = [lax.all_gather(ffn_out_weight, AXES, axis=0, tiled=True)]
        vec = lax.all_gather(jnp.concatenate([norm_gains, shift_vectors], axis=0), AXES, axis=1, tiled=True)
        vec = jnp.pad(vec.astype(F4), ((0, 1), (0, 0)))
        bias = lax.all_gather(ffn_in_bias, AXES, axis=0, tiled=True).astype(F4)[None]
    mem_send, cot_send = pick(place, memory, cotangent)
    mem_got = swap_seats(mem_send, seats)
    cot_got = swap_seats(cot_send, seats)

    segments = lax.dynamic_index_in_dim(seg_ids, seat, 0, keepdims=False)
    ends = jnp.cumsum(lax.dynamic_index_in_dim(mem_lengths, seat, 0, keepdims=False))
    places = jnp.arange(full, dtype=jnp.int32)
    mem_segments = jnp.sum((places[:, None] >= ends[None, :]).astype(jnp.int32), axis=1)
    lane = jnp.arange(PAIR, dtype=jnp.int32)
    half = jnp.arange(2, dtype=jnp.int32)[:, None, None]
    free = (lane // HEAD)[None, None] == 1 - half
    number = (lane % HEAD)[None, None]

    def key_side(ids):
        away = jnp.where(ids[None, :, None] == number, 0.0, AWAY)
        ones = jnp.where(number < 11, 1.0, 0.0)
        return jnp.where(free, jnp.where(number < 8, away, ones), 0.0).astype(BF)

    augq = jnp.where(free & (number < 8) & (segments[None, :, None] == number), 1.0, 0.0).astype(BF)
    augk, augm = key_side(segments), key_side(mem_segments)
    corner = jnp.arange(TILE, dtype=jnp.int32)
    tri = jnp.where(corner[None, :] <= corner[:, None], 0.0, AWAY).astype(F4)

    ctx, qa, ka, value = self_forward(place, inputs, x_got, qkv_parts, augq, augk, tri)
    cctx, cqa, cka, cvalue, xhat, inv = cross_forward(
        place, inputs, x_got, memory, mem_got, two_parts, ctx, vec, augq, augm
    )
    outs, (d3, d2, dcctx, vec_mid, bias_grad), upco_g, down_g = middle(
        place, inputs, x_got, cotangent, cot_got, two_parts, up_parts, down_parts, cctx, xhat, vec, bias, fast
    )
    out_got = swap_seats(outs[1:], seats)
    cdq, cdk, cdv = attend_back(False, cqa, cka, cvalue, cctx, dcctx, tri)
    mem_outs, (d13, dctx, vec_first), two_g = cross_grads(
        place, memory, mem_got, two_parts, cdq, cdk, cdv, ctx, xhat, inv, d2, d3, vec, fast
    )
    mg_got = swap_seats(mem_outs[1:], seats)
    dq, dk, dv = attend_back(True, qa, ka, value, ctx, dctx, tri)
    in_outs, qkv_g = self_grads(place, inputs, x_got, qkv_parts, dq, dk, dv, d13, fast)
    ig_got = swap_seats(in_outs[1:], seats)

    vec_sum = (vec_mid + vec_first)[:7]
    if fast:
        down_sum = reduce_chain(down_g)
        upco_sum = reduce_chain(upco_g)
        two_sum = reduce_chain(two_g)
        small = jnp.concatenate([vec_sum, jnp.zeros((1, width), F4), bias_grad.reshape(-1, width)], axis=0)
        for bits in (1, 2, 4, 8, 16):
            small = small + swap(small, bits)
        mine = lax.dynamic_slice_in_dim(small[:7], me * piece, piece, axis=1)
        bias_mine = lax.dynamic_slice_in_dim(small[8:].reshape(-1), me * bias_piece, bias_piece)
        qkv_sum = reduce_chain(qkv_g)
    else:

        def scatter(value, dim=0):
            return lax.psum_scatter(value.astype(F4), AXES, scatter_dimension=dim, tiled=True)

        down_sum, upco_sum, two_sum, qkv_sum = [scatter(g[0]) for g in (down_g, upco_g, two_g, qkv_g)]
        mine, bias_mine = scatter(vec_sum, 1), scatter(bias_grad[0])
    hidden = ffn_in_weight.shape[1]
    return (
        unpack(place, [outs[0], *out_got], BF),
        unpack(place, [in_outs[0], *ig_got], F4),
        unpack(place, [mem_outs[0], *mg_got], F4),
        qkv_sum,
        two_sum[:, :width],
        two_sum[:, width : 2 * width],
        two_sum[:, 2 * width :],
        upco_sum[:, hidden:],
        upco_sum[:, :hidden],
        bias_mine,
        down_sum,
        mine[:3],
        mine[3:],
    )


def solution(mesh):
    rows = P("dp", "seq", None)
    weight = P(AXES, None)
    vector = P(None, AXES)
    return jax.shard_map(
        on_device,
        mesh=mesh,
        in_specs=(rows, rows, P("dp", None), P("dp", None), rows)
        + (weight,) * 6
        + (P(AXES), weight, vector, vector),
        out_specs=(rows,) * 3 + (weight,) * 6 + (P(AXES), weight, vector, vector),
        check_vma=False,
    )
```

```python
import types

import jax
import jax.numpy as jnp
from jax import lax
from jax.experimental import pallas as pl
from jax.experimental.pallas import tpu as pltpu
from jax.sharding import PartitionSpec as P

HEAD = 64
PAIR = 2 * HEAD
TILE = 256
FAST = 32
HALF = FAST // 2
AXES = ("dp", "seq")
LOG2E = 1.4426950408889634
AWAY = -1e30
GELU_A = 0.7978845608028654
GELU_B = 0.044715
BF = jnp.bfloat16
F4 = jnp.float32
VMEM_BYTES = 58 << 20


def mm(a, b):
    return lax.dot_general(a, b, (((1,), (0,)), ((), ())), preferred_element_type=F4)


def mt(a, b):
    return lax.dot_general(a, b, (((1,), (1,)), ((), ())), preferred_element_type=F4)


def tm(a, b):
    return lax.dot_general(a, b, (((0,), (0,)), ((), ())), preferred_element_type=F4)


def struct(shape, dtype=BF):
    return jax.ShapeDtypeStruct(tuple(shape), dtype)


ANY = pl.BlockSpec(memory_space=pl.ANY)
WHOLE = pl.BlockSpec(memory_space=pltpu.VMEM)
SMEM = pl.BlockSpec(memory_space=pltpu.SMEM)


def aslist(value):
    return list(value) if isinstance(value, (list, tuple)) else [value]


LAST = []
COST = dict(
    self_forward=16,
    cross_forward=22,
    middle=31,
    cross_back=13,
    cross_grads=16,
    self_back=10,
    self_grads=5,
    input_back=6,
    total=2,
)
SCALE = 1.0


def call(body, name, ins, outs, scratch, grid=(), after=()):
    us = COST.get(name, 1.5)
    ins = dict(ins, after=(LAST + list(after), ANY))
    layout = [(key, len(aslist(value)), isinstance(value, (list, tuple))) for key, (value, _) in ins.items()]
    layout += [(key, len(aslist(value)), isinstance(value, (list, tuple))) for key, (value, _) in outs.items()]
    layout += [(key, 1, False) for key in scratch]

    def kernel(*refs):
        held, at = {}, 0
        for key, count, many in layout:
            held[key] = list(refs[at : at + count]) if many else refs[at]
            at += count
        body(types.SimpleNamespace(**held))

    arrays = [x for value, _ in ins.values() for x in aslist(value)]
    in_specs = []
    for value, spec in ins.values():
        in_specs += spec if isinstance(spec, list) else [spec] * len(aslist(value))
    out_specs = [spec for value, spec in outs.values() for _ in aslist(value)]
    out_shape = [x for value, _ in outs.values() for x in aslist(value)]
    result = pl.pallas_call(
        kernel,
        name=name,
        grid=grid,
        in_specs=in_specs,
        out_specs=out_specs,
        out_shape=out_shape,
        scratch_shapes=list(scratch.values()),
        compiler_params=pltpu.CompilerParams(vmem_limit_bytes=VMEM_BYTES),
        cost_estimate=pl.CostEstimate(flops=int(us * SCALE * 1.1e9), bytes_accessed=0, transcendentals=0),
    )(*arrays)
    LAST[:] = [result[-1]]
    found, at = {}, 0
    for key, (value, _) in outs.items():
        count = len(aslist(value))
        found[key] = list(result[at : at + count]) if isinstance(value, (list, tuple)) else result[at]
        at += count
    return types.SimpleNamespace(**found)


def vmem(*shape, dtype=BF):
    return pltpu.VMEM(shape, dtype)


ORDER = [((p % 4) << 3) | ((p // 4 % 4) << 1) | (p // HALF) for p in range(FAST)]


def wait_all(buffer, sem):
    pltpu.make_async_copy(buffer, buffer, sem).wait()


def start_weight(dst, parts, first, me, sem):
    columns = dst.shape[-1]
    if len(parts) == 1:
        pltpu.make_async_copy(parts[0].at[:, pl.ds(first, columns)], dst, sem).start()
    else:
        span = dst.shape[0] // FAST
        each = FAST // len(parts)
        for p in range(FAST):
            place = pl.multiple_of((me ^ ORDER[p]) * span, span)
            src = parts[p // each].at[pl.ds((p % each) * span, span), pl.ds(first, columns)]
            pltpu.make_async_copy(src, dst.at[pl.ds(place, span)], sem).start()


def start_grad(src, parts, me, sem):
    if len(parts) == 1:
        pltpu.make_async_copy(src, parts[0], sem).start()
        return
    span = src.shape[0] // FAST
    for p in range(FAST):
        place = pl.multiple_of((me ^ ORDER[p]) * span, span)
        dst = parts[p // HALF].at[pl.ds((p % HALF) * span, span)]
        pltpu.make_async_copy(src.at[pl.ds(place, span)], dst, sem).start()


def grad_shapes(rows, columns, fast):
    return [struct((rows // 2, columns))] * 2 if fast else [struct((rows, columns))]


def take(ref, first=0, columns=None):
    columns = ref.shape[-1] - first if columns is None else columns
    return ref[..., first : first + columns].reshape(-1, columns)


def put(ref, value, first):
    ref[:, first : first + value.shape[1]] = value.astype(BF)


def norm(values):
    centered = values - jnp.mean(values, axis=-1, keepdims=True)
    inverse = lax.rsqrt(jnp.mean(centered * centered, axis=-1, keepdims=True) + 1e-05)
    return centered * inverse, inverse


def norm_back(upstream, normed, inverse, gain_row):
    gain_part = jnp.sum(upstream * normed, axis=0, keepdims=True)
    shift_part = jnp.sum(upstream, axis=0, keepdims=True)
    scaled = upstream * gain_row
    centered = scaled - jnp.mean(scaled, axis=-1, keepdims=True)
    value = inverse * (centered - normed * jnp.mean(scaled * normed, axis=-1, keepdims=True))
    return value, gain_part, shift_part


def lane_masks(dtype):
    lane = lax.broadcasted_iota(jnp.int32, (1, PAIR), 1)
    own = [(lane // HEAD == h).astype(dtype) for h in range(2)]

    def spot(h, k):
        return ((lane // HEAD == 1 - h) & (lane % HEAD == k)).astype(dtype)

    return own, spot


def attend_pair(causal, query, key, value, augq, augk, tri, ctx_out, qa_out, ka_out):
    total = key.shape[0]
    own, spot = lane_masks(F4)
    own_low = [mask.astype(BF) for mask in own]
    eighth = [(mask * HEAD ** (-0.5)).astype(BF) for mask in own]
    wide = jnp.concatenate([value, jnp.ones((total, PAIR), BF)], axis=1)
    keys = []
    for h in range(2):
        keys.append(key * own_low[h] + augk[h])
        ka_out[h] = keys[h]
    units = [(i, h) for i in range(query.shape[0] // TILE) for h in range(2)]
    scores, probs, halves = {}, {}, {}

    def score(i, h):
        rows = slice(i * TILE, (i + 1) * TILE)
        width = (i + 1) * TILE if causal else total
        head = query[rows] * eighth[h] + augq[h, rows]
        s = mt(head, keys[h][:width])
        if causal:
            tail = s[:, width - TILE :] + tri[...]
            s = jnp.concatenate([s[:, : width - TILE], tail], axis=1) if i else tail
        return s, head

    def finish(i, h, low, top, head):
        rows = slice(i * TILE, (i + 1) * TILE)
        both = mm(low, wide[: low.shape[1]])
        sums = both[:, PAIR:]
        halves[h] = both[:, :PAIR] / sums
        rest = -(top + jnp.log(sums))
        high = rest.astype(BF).astype(F4)
        rest = rest - high
        middle = rest.astype(BF).astype(F4)
        extra = high * spot(h, 8) + middle * spot(h, 9) + (rest - middle) * spot(h, 10)
        qa_out[h, rows] = head + extra.astype(BF)
        if h == 1:
            ctx_out[rows] = (halves[0] * own[0] + halves[1] * own[1]).astype(BF)

    count = len(units)
    for t in range(count + 2):
        if t < count:
            scores[t] = score(*units[t])
        if 0 <= t - 2 < count:
            finish(*units[t - 2], *probs.pop(t - 2))
        if 0 <= t - 1 < count:
            s, head = scores.pop(t - 1)
            top = jnp.max(s, axis=1, keepdims=True)
            low = jnp.exp2(s * LOG2E - top * LOG2E).astype(BF)
            probs[t - 1] = (low, top, head)


def self_forward(place, x, parts, augq, augk, tri):
    full, width = x.shape
    heads = width // HEAD

    def body(n):
        pair = pl.program_id(0)

        @pl.when(pair == 0)
        def _():
            start_weight(n.w, n.parts, 0, n.place[0], n.sem)
            wait_all(n.w, n.sem)
            for c in range(0, 3 * width, 512):
                n.qkv[:, c : c + 512] = mm(n.x[...], take(n.w, c, 512)).astype(BF)

        def columns(part):
            return n.qkv[:, pl.ds(pl.multiple_of(part * width + pair * PAIR, PAIR), PAIR)]

        value = columns(2)
        n.value[...] = value
        attend_pair(True, columns(0), columns(1), value, n.augq, n.augk, n.tri, n.ctx, n.qa, n.ka)

    both = pl.BlockSpec((2, full, PAIR), lambda p: (p, 0, 0))
    fixed = pl.BlockSpec((2, full, PAIR), lambda p: (0, 0, 0))
    cols = pl.BlockSpec((full, PAIR), lambda p: (0, p))
    return call(
        body,
        "self_forward",
        dict(
            place=(place, SMEM),
            x=(x, pl.BlockSpec((full, width), lambda p: (0, 0))),
            parts=(parts, ANY),
            augq=(augq, fixed),
            augk=(augk, fixed),
            tri=(tri, pl.BlockSpec((TILE, TILE), lambda p: (0, 0))),
        ),
        dict(
            ctx=(struct((full, width)), cols),
            qa=(struct((heads, full, PAIR)), both),
            ka=(struct((heads, full, PAIR)), both),
            value=(struct((full, width)), cols),
        ),
        dict(
            w=vmem(width, 3 * width),
            qkv=vmem(full, 3 * width),
            sem=pltpu.SemaphoreType.DMA,
        ),
        grid=(heads // 2,),
    )


def unfold_vectors(blocks, vec, bias):
    width, hidden = vec.shape[1], bias.shape[1]
    piece, part = width // FAST, hidden // FAST
    lane = lax.broadcasted_iota(jnp.int32, (PAIR, width), 0)
    col = lax.broadcasted_iota(jnp.int32, (PAIR, width), 1)
    wide = mm(blocks, (lane == col % piece).astype(BF))
    row = lax.broadcasted_iota(jnp.int32, (width, width), 0)
    col = lax.broadcasted_iota(jnp.int32, (width, width), 1)
    wide = jnp.where(row // 16 == col // piece, wide, 0.0).astype(BF)
    line = lax.broadcasted_iota(jnp.int32, (8, width), 0)
    vec[...] = mm((line == lax.broadcasted_iota(jnp.int32, (8, width), 1) % 16).astype(BF), wide)
    owner = lax.broadcasted_iota(jnp.int32, (FAST, width), 0) * 16 + 7
    rows = mm((owner == lax.broadcasted_iota(jnp.int32, (FAST, width), 1)).astype(BF), blocks)
    for j in range(FAST):
        bias[:, j * part : (j + 1) * part] = rows[j : j + 1, :part]


def cross_forward(place, x, mem, parts, ctx, vec, bias, augq, augk, hidden, fast):
    full, width = x.shape
    heads = width // HEAD

    def body(n):
        pair = pl.program_id(0)

        @pl.when(pair == 0)
        def _():
            me = n.place[0]
            start_weight(n.w, n.parts, 0, me, n.sems.at[0])
            if fast:
                start_weight(n.blocks, n.parts, 5 * width, me, n.sems.at[1])
                wait_all(n.blocks, n.sems.at[1])
                unfold_vectors(n.blocks[...], n.vec, n.bias)
            else:
                n.vec[...] = n.vec_in[0][...]
                n.bias[...] = n.bias_in[0][...]
            wait_all(n.w, n.sems.at[0])
            for i in range(0, full, TILE):
                rows = slice(i, i + TILE)
                attn = mm(n.ctx[rows], n.w[:, :width])
                normed, inverse = norm(n.x[rows].astype(F4) + attn)
                n.xhat[rows] = normed
                n.inv[rows] = jnp.broadcast_to(inverse, (TILE, PAIR))
                first = (normed * n.vec[0:1] + n.vec[3:4]).astype(BF)
                n.q[rows] = mm(first, n.w[:, width : 2 * width]).astype(BF)
            for c in range(0, 2 * width, 512):
                n.kv[:, c : c + 512] = mm(n.mem[...], n.w[:, 2 * width + c : 2 * width + c + 512]).astype(BF)

        lanes = pl.ds(pl.multiple_of(pair * PAIR, PAIR), PAIR)
        late = pl.ds(pl.multiple_of(width + pair * PAIR, PAIR), PAIR)
        value = n.kv[:, late]
        n.value[...] = value
        attend_pair(False, n.q[:, lanes], n.kv[:, lanes], value, n.augq, n.augk, None, n.cctx, n.qa, n.ka)

    both = pl.BlockSpec((2, full, PAIR), lambda p: (p, 0, 0))
    fixed = pl.BlockSpec((2, full, PAIR), lambda p: (0, 0, 0))
    cols = pl.BlockSpec((full, PAIR), lambda p: (0, p))

    def still(shape):
        return pl.BlockSpec(shape, lambda p: (0, 0))

    return call(
        body,
        "cross_forward",
        dict(
            place=(place, SMEM),
            x=(x, still((full, width))),
            mem=(mem, still((full, width))),
            parts=(parts, ANY),
            ctx=(ctx, still((full, width))),
            vec_in=([] if fast else [vec], still((8, width))),
            bias_in=([] if fast else [bias], still((1, hidden))),
            augq=(augq, fixed),
            augk=(augk, fixed),
        ),
        dict(
            cctx=(struct((full, width)), cols),
            qa=(struct((heads, full, PAIR)), both),
            ka=(struct((heads, full, PAIR)), both),
            value=(struct((full, width)), cols),
            xhat=(struct((full, width), F4), still((full, width))),
            inv=(struct((full, PAIR), F4), still((full, PAIR))),
            vec=(struct((8, width), F4), still((8, width))),
            bias=(struct((1, hidden), F4), still((1, hidden))),
        ),
        dict(
            w=vmem(width, 4 * width),
            q=vmem(full, width),
            kv=vmem(full, 2 * width),
            blocks=vmem(width, PAIR),
            sems=pltpu.SemaphoreType.DMA((2,)),
        ),
        grid=(heads // 2,),
    )


def middle(place, x, cot, co_parts, ffn_parts, cctx, xhat, vec, bias, fast):
    full, width = x.shape
    hidden = bias.shape[1]
    fold = hidden // width
    late = hidden + width

    def body(n):
        me = n.place[0]
        start_weight(n.co, n.co_parts, 4 * width, me, n.sems.at[0])
        if fast:
            whole = n.ffn_parts[0]
            pltpu.make_async_copy(whole.at[:, :, pl.ds(0, hidden)], n.up, n.sems.at[1]).start()
            for k in range(fold):
                src = whole.at[:, :, pl.ds(hidden + k * width, width)]
                pltpu.make_async_copy(src, n.down.at[:, k], n.sems.at[2]).start()
        else:
            start_weight(n.up, n.ffn_parts[:1], 0, me, n.sems.at[1])
            start_weight(n.down, n.ffn_parts[1:], 0, me, n.sems.at[2])
        n.vec_sum[...] = jnp.zeros(n.vec_sum.shape, F4)
        n.bias_sum[...] = jnp.zeros(n.bias_sum.shape, F4)
        wait_all(n.co, n.sems.at[0])
        wait_all(n.up, n.sems.at[1])
        wait_all(n.down, n.sems.at[2])
        vec = n.vec

        def tile(i, carry):
            rows = pl.ds(pl.multiple_of(i * TILE, TILE), TILE)
            first = n.xhat[rows] * vec[0:1] + vec[3:4]
            normed_one, inverse_one = norm(first + mm(n.cctx[rows], n.co[...]))
            second = normed_one * vec[1:2] + vec[4:5]
            low = second.astype(BF)
            n.second[rows] = low
            pre = mm(low, take(n.up)) + n.bias[...]
            slope = GELU_A * GELU_B * (pre * pre) + GELU_A
            t = jnp.tanh(pre * slope)
            half = 0.5 * t + 0.5
            hid = (pre * half).astype(BF)
            n.hid[rows] = hid
            d_gelu = half + (0.5 - 0.5 * t * t) * pre * (3.0 * slope - 2.0 * GELU_A)
            ffn = mm(hid, take(n.down)) + vec[6:7]
            normed_two, inverse_two = norm(second + ffn + n.x[rows].astype(F4))
            n.out[rows] = (normed_two * vec[2:3] + vec[5:6]).astype(BF)
            d_three, gain_two, shift_two = norm_back(
                n.cot[rows].astype(F4), normed_two, inverse_two, vec[2:3]
            )
            n.d3[rows] = d_three
            df = d_three.astype(BF)
            n.df[rows] = df
            d_pre = (mt(df, take(n.down)) * d_gelu).astype(BF)
            n.d_pre[rows] = d_pre
            n.bias_sum[...] += jnp.sum(d_pre.astype(F4), axis=0, keepdims=True)
            d_second = d_three + mt(d_pre, take(n.up))
            d_two, gain_one, shift_one = norm_back(d_second, normed_one, inverse_one, vec[1:2])
            n.d2[rows] = d_two
            dc = d_two.astype(BF)
            n.dc[rows] = dc
            n.dcctx[rows] = mt(dc, n.co[...]).astype(BF)
            n.vec_sum[1:2] += gain_one
            n.vec_sum[2:3] += gain_two
            n.vec_sum[4:5] += shift_one
            n.vec_sum[5:6] += shift_two
            n.vec_sum[6:7] += jnp.sum(d_three, axis=0, keepdims=True)
            return carry

        lax.fori_loop(0, full // TILE, tile, 0)
        for c in range(0, hidden, 512):
            part = tm(n.hid[:, c : c + 512], n.df[...]).astype(BF)
            if fast:
                rows = width // FAST
                part = part.reshape(512 // (fold * rows), fold, rows, width)
                top = c // fold
                for a in range(fold):
                    n.grad[top : top + 512 // fold, late + a * width : late + (a + 1) * width] = part[
                        :, a
                    ].reshape(512 // fold, width)
            else:
                n.grad_down[c : c + 512] = part
        for c in range(0, hidden, 512):
            n.grad[:, c : c + 512] = tm(n.second[...], n.d_pre[:, c : c + 512]).astype(BF)
        n.grad[:, hidden : hidden + width] = tm(n.cctx[...], n.dc[...]).astype(BF)
        if fast:
            start_grad(n.grad, n.grads, me, n.sems.at[0])
        else:
            start_grad(n.grad, n.grads[:1], me, n.sems.at[0])
            start_grad(n.grad_down, n.grads[1:], me, n.sems.at[1])
            wait_all(n.grad_down, n.sems.at[1])
        wait_all(n.grad, n.sems.at[0])

    if fast:
        grads = grad_shapes(width, late + fold * width, fast)
        scratch = dict(
            up=vmem(FAST, width // FAST, hidden),
            down=vmem(FAST, fold, width // FAST, width),
            grad=vmem(width, late + fold * width),
        )
    else:
        grads = [struct((width, late)), struct((hidden, width))]
        scratch = dict(
            up=vmem(width, hidden), down=vmem(hidden, width), grad=vmem(width, late), grad_down=vmem(hidden, width)
        )
    return call(
        body,
        "middle",
        dict(
            place=(place, SMEM),
            x=(x, WHOLE),
            cot=(cot, WHOLE),
            co_parts=(co_parts, ANY),
            ffn_parts=(ffn_parts, ANY),
            cctx=(cctx, WHOLE),
            xhat=(xhat, WHOLE),
            vec=(vec, WHOLE),
            bias=(bias, WHOLE),
        ),
        dict(
            out=(struct((full, width)), WHOLE),
            d3=(struct((full, width), F4), WHOLE),
            d2=(struct((full, width), F4), WHOLE),
            dcctx=(struct((full, width)), WHOLE),
            vec_sum=(struct((8, width), F4), WHOLE),
            bias_sum=(struct((1, hidden), F4), WHOLE),
            grads=(grads, ANY),
        ),
        dict(
            scratch,
            co=vmem(width, width),
            second=vmem(full, width),
            hid=vmem(full, hidden),
            d_pre=vmem(full, hidden),
            df=vmem(full, width),
            dc=vmem(full, width),
            sems=pltpu.SemaphoreType.DMA((3,)),
        ),
    )


def attend_pair_back(causal, qa, ka, value, ctx, dctx, tri, dq, dk, dv):
    own, spot = lane_masks(F4)
    total = value.shape[0]
    blocks = total // TILE
    upstream = dctx[...].astype(F4)
    product = upstream * ctx[...].astype(F4)
    row = lax.broadcasted_iota(jnp.int32, (PAIR, PAIR), 0) // HEAD
    col = lax.broadcasted_iota(jnp.int32, (PAIR, PAIR), 1) // HEAD
    swap = jnp.where(row != col, -1.0, 0.0).astype(BF)
    high = product.astype(BF)
    delta = mm(high, swap) + mm((product - high.astype(F4)).astype(BF), swap)
    delta_high = delta.astype(BF).astype(F4)
    delta_low = delta - delta_high
    values = value[...].astype(F4)
    d_query, d_key, d_value = [], [], []
    for h in range(2):
        spots = spot(h, 0) + spot(h, 1)
        do = (upstream * own[h] + delta_high * spot(h, 0) + delta_low * spot(h, 1)).astype(BF)
        va = (values * own[h] + spots).astype(BF)
        query, key = qa[h], ka[h]
        query_t = query.T[h * HEAD : (h + 1) * HEAD]
        do_t = do.T[h * HEAD : (h + 1) * HEAD]
        keys, vals, sums = [], [], [None] * blocks
        for j in range(blocks):
            start = j * TILE if causal else 0
            key_j, va_j = key[j * TILE : (j + 1) * TILE], va[j * TILE : (j + 1) * TILE]
            s = mt(query[start:], key_j)
            if causal:
                head = s[:TILE] + tri[...]
                s = jnp.concatenate([head, s[TILE:]], axis=0) if j < blocks - 1 else head
            prob = jnp.exp2(s * LOG2E)
            ds = (prob * mt(do[start:], va_j)).astype(BF)
            vals.append(mm(do_t[:, start:], prob.astype(BF)))
            keys.append(mm(query_t[:, start:], ds))
            back = mm(ds, key_j)
            for i in range(start // TILE, blocks):
                part = back[i * TILE - start : (i + 1) * TILE - start]
                sums[i] = part if sums[i] is None else sums[i] + part
        d_query.append(jnp.concatenate(sums, axis=0))
        d_key.append(jnp.concatenate(keys, axis=1))
        d_value.append(jnp.concatenate(vals, axis=1))
    dq[...] = ((d_query[0] * own[0] + d_query[1] * own[1]) * HEAD ** (-0.5)).astype(BF)
    dk[...] = jnp.concatenate(d_key, axis=0).T.astype(BF)
    dv[...] = jnp.concatenate(d_value, axis=0).T.astype(BF)


def attend_back(causal, qa, ka, value, ctx, dctx, tri, first, count):
    full = value.shape[0]

    def body(n):
        attend_pair_back(causal, n.qa, n.ka, n.value, n.ctx, n.dctx, n.tri, n.dq, n.dk, n.dv)

    both = pl.BlockSpec((2, full, PAIR), lambda p: (p + first, 0, 0))
    cols = pl.BlockSpec((full, PAIR), lambda p: (0, p + first))
    made = (struct((full, count * PAIR)), pl.BlockSpec((full, PAIR), lambda p: (0, p)))
    result = call(
        body,
        "self_back" if causal else "cross_back",
        dict(
            qa=(qa, both),
            ka=(ka, both),
            value=(value, cols),
            ctx=(ctx, cols),
            dctx=(dctx, cols),
            tri=(tri, pl.BlockSpec((TILE, TILE), lambda p: (0, 0))),
        ),
        dict(dq=made, dk=made, dv=made),
        {},
        grid=(count,),
    )
    return [result.dq, result.dk, result.dv]


def columns_of(parts, rows):
    return jnp.concatenate([part[rows] for part in parts], axis=1)


def cross_grads(place, mem, parts, dq, dk, dv, ctx, xhat, inv, d2, d3, vec, vec_mid, bias_mid, fast, after):
    full, width = mem.shape
    extra = PAIR if fast else 0

    def body(n):
        me = n.place[0]
        vec = n.vec
        start_weight(n.w, n.parts, 0, me, n.sems.at[0])
        n.vec_sum[...] = n.vec_mid[...]
        wait_all(n.w, n.sems.at[0])

        def tile(i, carry):
            rows = pl.ds(pl.multiple_of(i * TILE, TILE), TILE)
            normed = n.xhat[rows]
            n.first[rows] = (normed * vec[0:1] + vec[3:4]).astype(BF)
            d_first = n.d2[rows] + mt(columns_of(n.dq, rows), n.w[:, width : 2 * width])
            inverse = jnp.concatenate([n.inv[rows]] * (width // PAIR), axis=1)
            d_one, gain, shift = norm_back(d_first, normed, inverse, vec[0:1])
            n.d13[rows] = n.d3[rows] + d_one
            da = d_one.astype(BF)
            n.da[rows] = da
            n.dctx[rows] = mt(da, n.w[:, :width]).astype(BF)
            n.vec_sum[0:1] += gain
            n.vec_sum[3:4] += shift
            back = mt(columns_of(n.dk, rows), n.w[:, 2 * width : 3 * width])
            back = back + mt(columns_of(n.dv, rows), n.w[:, 3 * width :])
            n.mg[rows] = back.astype(BF)
            return carry

        lax.fori_loop(0, full // TILE, tile, 0)
        everything = slice(None)
        put(n.grad, tm(n.ctx[...], n.da[...]), 0)
        put(n.grad, tm(n.first[...], columns_of(n.dq, everything)), width)
        put(n.grad, tm(n.mem[...], columns_of(n.dk, everything)), 2 * width)
        put(n.grad, tm(n.mem[...], columns_of(n.dv, everything)), 3 * width)
        if fast:
            piece = width // FAST
            row = lax.broadcasted_iota(jnp.int32, (width, width), 0)
            col = lax.broadcasted_iota(jnp.int32, (width, width), 1)
            line = lax.broadcasted_iota(jnp.int32, (width, 8), 0) % piece
            pick_line = (line == lax.broadcasted_iota(jnp.int32, (width, 8), 1)).astype(BF)
            spread = mm(pick_line, n.vec_sum[...].astype(BF))
            spread = jnp.where(row // piece == col // piece, spread, 0.0).astype(BF)
            lane = lax.broadcasted_iota(jnp.int32, (width, PAIR), 1)
            fold = (lax.broadcasted_iota(jnp.int32, (width, PAIR), 0) % piece == lane).astype(BF)
            owner = lax.broadcasted_iota(jnp.int32, (width, FAST), 0)
            wanted = lax.broadcasted_iota(jnp.int32, (width, FAST), 1) * piece + 8
            put(n.grad, mm(spread, fold) + mm((owner == wanted).astype(BF), n.bias_mid[...]), 4 * width)
        start_grad(n.grad, n.grads, me, n.sems.at[1])
        wait_all(n.grad, n.sems.at[1])

    return call(
        body,
        "cross_grads",
        dict(
            place=(place, SMEM),
            mem=(mem, WHOLE),
            parts=(parts, ANY),
            dq=(dq, WHOLE),
            dk=(dk, WHOLE),
            dv=(dv, WHOLE),
            ctx=(ctx, WHOLE),
            xhat=(xhat, WHOLE),
            inv=(inv, WHOLE),
            d2=(d2, WHOLE),
            d3=(d3, WHOLE),
            vec=(vec, WHOLE),
            vec_mid=(vec_mid, WHOLE),
            bias_mid=(bias_mid, WHOLE),
        ),
        dict(
            mg=(struct((full, width)), WHOLE),
            d13=(struct((full, width), F4), WHOLE),
            dctx=(struct((full, width)), WHOLE),
            vec_sum=(struct((8, width), F4), WHOLE),
            grads=(grad_shapes(width, 4 * width + extra, fast), ANY),
        ),
        dict(
            w=vmem(width, 4 * width),
            first=vmem(full, width),
            da=vmem(full, width),
            grad=vmem(width, 4 * width + extra),
            sems=pltpu.SemaphoreType.DMA((2,)),
        ),
        after=after,
    )


def self_grads(place, x, dq, dk, dv, fast, after):
    full, width = x.shape

    def body(n):
        everything = slice(None)
        for c, d in enumerate((n.dq, n.dk, n.dv)):
            put(n.grad, tm(n.x[...], columns_of(d, everything)), c * width)
        start_grad(n.grad, n.grads, n.place[0], n.sem)
        wait_all(n.grad, n.sem)

    return call(
        body,
        "self_grads",
        dict(place=(place, SMEM), x=(x, WHOLE), dq=(dq, WHOLE), dk=(dk, WHOLE), dv=(dv, WHOLE)),
        dict(grads=(grad_shapes(width, 3 * width, fast), ANY)),
        dict(grad=vmem(width, 3 * width), sem=pltpu.SemaphoreType.DMA),
        after=after,
    ).grads


def input_back(place, parts, dq, dk, dv, d13):
    full, width = d13.shape

    def body(n):
        start_weight(n.w, n.parts, 0, n.place[0], n.sem)
        wait_all(n.w, n.sem)
        for i in range(0, full, TILE):
            rows = slice(i, i + TILE)
            back = n.d13[rows]
            for c, d in enumerate((n.dq, n.dk, n.dv)):
                back = back + mt(columns_of(d, rows), n.w[:, c * width : (c + 1) * width])
            n.ig[rows] = back.astype(BF)

    return call(
        body,
        "input_back",
        dict(
            place=(place, SMEM),
            parts=(parts, ANY),
            dq=(dq, WHOLE),
            dk=(dk, WHOLE),
            dv=(dv, WHOLE),
            d13=(d13, WHOLE),
        ),
        dict(ig=(struct((full, width)), WHOLE)),
        dict(w=vmem(width, 3 * width), sem=pltpu.SemaphoreType.DMA),
    ).ig


def total(arrays, pieces, dtype=BF, steps=1):
    rows, columns = arrays[0].shape
    span = rows // pieces // steps

    def body(n):
        for k, out in enumerate(n.outs):
            value = n.parts[k][...].astype(F4)
            for m in range(1, len(arrays)):
                value = value + n.parts[m * pieces + k][...].astype(F4)
            out[...] = value.astype(dtype)

    def piece(k):
        return pl.BlockSpec((span, columns), lambda i: (k * steps + i, 0))

    parts, specs = [], []
    for array in arrays:
        for k in range(pieces):
            parts.append(array)
            specs.append(piece(k))
    outs = [struct((rows // pieces, columns), dtype)] * pieces
    return call(
        body, "total", dict(parts=(parts, specs)), dict(outs=(outs, piece(0))), {}, grid=(steps,)
    ).outs


def finish(arrays, cuts):
    rows = arrays[0].shape[0]

    def body(n):
        value = n.arrays[0][...].astype(F4)
        for array in n.arrays[1:]:
            value = value + array[...].astype(F4)
        for out, (low, high, *more) in zip(n.outs, cuts):
            if len(more) == 1:
                for k in range((high - low) // more[0]):
                    out[k * rows : (k + 1) * rows] = value[:, low + k * more[0] : low + (k + 1) * more[0]]
            elif more:
                out[...] = value[more[0] : more[1], low:high]
            else:
                out[...] = value[:, low:high]

    outs = []
    for low, high, *more in cuts:
        if len(more) == 1:
            outs.append(struct(((high - low) // more[0] * rows, more[0]), F4))
        else:
            outs.append(struct((more[1] - more[0] if more else rows, high - low), F4))
    return call(body, "total", dict(arrays=(arrays, WHOLE)), dict(outs=(outs, WHOLE)), {}).outs


def to_rows(array):
    seats = lax.axis_size("seq")
    blocks = array.reshape(seats, -1, array.shape[-1])
    return lax.all_to_all(blocks, "seq", split_axis=0, concat_axis=0, tiled=True)


def swap(value, bits):
    return lax.ppermute(value, AXES, [(i, i ^ bits) for i in range(FAST)])


def swap_all(value):
    groups = [list(range(core, FAST, 2)) for core in range(2)]
    return lax.all_to_all(value, AXES, split_axis=0, concat_axis=0, tiled=True, axis_index_groups=groups)


def join(arrays, axis, cuts=(), after=()):
    arrays = list(arrays)
    rows = sum(x.shape[0] for x in arrays) if axis == 0 else arrays[0].shape[0]
    columns = arrays[0].shape[1] if axis == 0 else sum(x.shape[1] for x in arrays)
    edges = [0, *cuts, columns]

    def body(n):
        at = 0
        for x in n.arrays:
            if axis == 1:
                n.outs[0][:, at : at + x.shape[1]] = x[...]
            else:
                for out, low, high in zip(n.outs, edges[:-1], edges[1:]):
                    out[at : at + x.shape[0]] = x[:, low:high]
            at += x.shape[axis]

    outs = [struct((rows, high - low)) for low, high in zip(edges[:-1], edges[1:])]
    return call(body, "join", dict(arrays=(arrays, WHOLE)), dict(outs=(outs, WHOLE)), {}, after=after).outs


def swap_plane(held):
    return [held] + [swap(held, bits) for bits in (2, 4, 6)]


def swap_line(held):
    return [held] + [swap(held, z << 3) for z in (1, 2, 3)]


def swap_cores(parts):
    return parts + [swap(part, 1) for part in parts]


def spread_plane(pieces):
    return [pieces[0]] + [swap(piece, bits) for piece, bits in zip(pieces[1:], (2, 4, 6))]


def spread_line(pieces):
    return [pieces[0]] + [swap(piece, z << 3) for z, piece in enumerate(pieces[1:], 1)]


def on_device(
    inputs,
    memory,
    seg_ids,
    mem_lengths,
    cotangent,
    qkv_weight,
    self_out_weight,
    cross_q_weight,
    cross_kv_weight,
    cross_out_weight,
    ffn_in_weight,
    ffn_in_bias,
    ffn_out_weight,
    norm_gains,
    shift_vectors,
):
    seats = lax.axis_size("seq")
    devices = lax.axis_size("dp") * seats
    span, width = inputs.shape[1:]
    hidden = ffn_in_weight.shape[1]
    full = seats * span
    seat = lax.axis_index("seq")
    me = lax.axis_index("dp") * seats + seat
    LAST.clear()
    rows, piece, bias_piece = qkv_weight.shape[0], norm_gains.shape[1], ffn_in_bias.shape[0]
    fast = devices == FAST and rows == 16 and hidden == 4 * width
    place = me.astype(jnp.int32).reshape(1)
    second_group = [self_out_weight, cross_q_weight, cross_kv_weight, cross_out_weight]
    if fast:
        fold = hidden // width
        block = jnp.concatenate(
            [
                jnp.pad(norm_gains, ((0, 0), (0, PAIR - piece))),
                jnp.pad(shift_vectors, ((0, 0), (0, PAIR - piece))),
                jnp.pad(ffn_in_bias[None], ((0, rows - 8), (0, PAIR - bias_piece))),
            ],
            axis=0,
        )
        (front,) = join([qkv_weight, *second_group, block], 1)
        front = swap_line(front)
        folded = [ffn_in_weight] + [ffn_out_weight[k * rows : (k + 1) * rows] for k in range(fold)]
        (ffn,) = join(folded, 1)
        ffn_parts = [lax.all_gather(ffn, AXES, axis=0, tiled=False)]
        x = to_rows(inputs).reshape(full, width)
        one, two = join(front, 0, (3 * width,))
        qkv_parts = swap_cores(swap_plane(one))
        (two,) = join([two, swap(two, 2)], 0, (), qkv_parts[4:])
        two_y = swap(two, 4)
        vec, bias = None, None
    else:
        x = to_rows(inputs).reshape(full, width)
        qkv_parts = [lax.all_gather(qkv_weight, AXES, axis=0, tiled=True)]
        two_parts = [lax.all_gather(jnp.concatenate(second_group, axis=1), AXES, axis=0, tiled=True)]
        ffn_parts = [lax.all_gather(w, AXES, axis=0, tiled=True) for w in (ffn_in_weight, ffn_out_weight)]
        vec = lax.all_gather(jnp.concatenate([norm_gains, shift_vectors], axis=0), AXES, axis=1, tiled=True)
        vec = jnp.pad(vec.astype(F4), ((0, 1), (0, 0)))
        bias = lax.all_gather(ffn_in_bias, AXES, axis=0, tiled=True).astype(F4)[None]
    mem = to_rows(memory).reshape(full, width)
    cot = to_rows(cotangent).reshape(full, width)

    segments = lax.dynamic_index_in_dim(seg_ids, seat, 0, keepdims=False)
    ends = jnp.cumsum(lax.dynamic_index_in_dim(mem_lengths, seat, 0, keepdims=False))
    places = jnp.arange(full, dtype=jnp.int32)
    mem_segments = jnp.sum((places[:, None] >= ends[None, :]).astype(jnp.int32), axis=1)
    lane = jnp.arange(PAIR, dtype=jnp.int32)
    half = jnp.arange(2, dtype=jnp.int32)[:, None, None]
    free = (lane // HEAD)[None, None] == 1 - half
    number = (lane % HEAD)[None, None]

    def key_side(ids):
        away = jnp.where(ids[None, :, None] == number, 0.0, AWAY)
        ones = jnp.where(number < 11, 1.0, 0.0)
        return jnp.where(free, jnp.where(number < 8, away, ones), 0.0).astype(BF)

    augq = jnp.where(free & (number < 8) & (segments[None, :, None] == number), 1.0, 0.0).astype(BF)
    augk, augm = key_side(segments), key_side(mem_segments)
    corner = jnp.arange(TILE, dtype=jnp.int32)
    tri = jnp.where(corner[None, :] <= corner[:, None], 0.0, AWAY).astype(F4)

    a = self_forward(place, x, qkv_parts, augq, augk, tri)
    if fast:
        (two,) = join([two, two_y], 0, (), [mem])
        two_parts = [two, swap(two, 1)]
    c = cross_forward(place, x, mem, two_parts, a.ctx, vec, bias, augq, augm, hidden, fast)
    vec, bias = c.vec, c.bias
    m = middle(place, x, cot, two_parts, ffn_parts, c.cctx, c.xhat, vec, bias, fast)
    output = to_rows(m.out)
    pairs = width // PAIR
    first_half = pairs // 2

    def cross_part(first, count):
        return attend_back(False, c.qa, c.ka, c.value, c.cctx, m.dcctx, tri, first, count)

    one = cross_part(0, first_half)
    if fast:
        big = spread_plane(total([m.grads[0], swap(m.grads[1], 1)], 4, steps=2))
    two = cross_part(first_half, pairs - first_half)
    dq, dk, dv = zip(one, two)
    bias_mid = jnp.pad(m.bias_sum.reshape(-1, bias_piece), ((0, 0), (0, PAIR - bias_piece))).astype(BF)
    g = cross_grads(
        place, mem, two_parts, dq, dk, dv, a.ctx, c.xhat, c.inv, m.d2, m.d3, vec, m.vec_sum, bias_mid, fast, [output]
    )
    memory_grad = to_rows(g.mg)

    def self_part(first, count):
        return attend_back(True, a.qa, a.ka, a.value, a.ctx, g.dctx, tri, first, count)

    if fast:
        two_got = swap(g.grads[1], 1)
        big = spread_line(total(big, 4))
    one = self_part(0, first_half)
    if fast:
        up_sum, co_sum, down_sum = finish(
            big, ((0, hidden), (hidden, hidden + width), (hidden + width, 2 * hidden + width, width))
        )
        two_sum = spread_plane(total([g.grads[0], two_got], 4))
    two = self_part(first_half, pairs - first_half)
    if fast:
        two_sum = spread_line(total(two_sum, 4))
    dq, dk, dv = zip(one, two)
    qkv_g = self_grads(place, x, dq, dk, dv, fast, [memory_grad])
    memory_grad = memory_grad.astype(F4)
    ig = input_back(place, qkv_parts, dq, dk, dv, g.d13)
    if fast:
        qkv_got = swap(qkv_g[1], 1)
        at = 4 * width
        so_sum, cq_sum, ckv_sum, gains_sum, shifts_sum, bias_sum = finish(
            two_sum,
            (
                (0, width),
                (width, 2 * width),
                (2 * width, at),
                (at, at + piece, 0, 3),
                (at, at + piece, 3, 7),
                (at, at + bias_piece, 8, 9),
            ),
        )
        qkv_sum = spread_plane(total([qkv_g[0], qkv_got], 4))
    input_grad = to_rows(ig).astype(F4)
    if fast:
        (qkv_sum,) = finish(spread_line(total(qkv_sum, 4)), ((0, 3 * width),))
    else:

        def scatter(value, dim=0):
            return lax.psum_scatter(value.astype(F4), AXES, scatter_dimension=dim, tiled=True)

        upco_sum, down_sum, two_sum, qkv_sum = [scatter(v) for v in (*m.grads, *g.grads, *qkv_g)]
        up_sum, co_sum = upco_sum[:, :hidden], upco_sum[:, hidden:]
        so_sum, cq_sum, ckv_sum = two_sum[:, :width], two_sum[:, width : 2 * width], two_sum[:, 2 * width :]
        vec_sum, bias_sum = scatter(g.vec_sum[:7], 1), scatter(m.bias_sum[0])
        gains_sum, shifts_sum = vec_sum[:3], vec_sum[3:]
    return (
        output,
        input_grad,
        memory_grad,
        qkv_sum,
        so_sum,
        cq_sum,
        ckv_sum,
        co_sum,
        up_sum,
        bias_sum.reshape(-1),
        down_sum,
        gains_sum,
        shifts_sum,
    )


def solution(mesh):
    rows = P("dp", "seq", None)
    weight = P(AXES, None)
    vector = P(None, AXES)
    return jax.shard_map(
        on_device,
        mesh=mesh,
        in_specs=(rows, rows, P("dp", None), P("dp", None), rows)
        + (weight,) * 6
        + (P(AXES), weight, vector, vector),
        out_specs=(rows,) * 3 + (weight,) * 6 + (P(AXES), weight, vector, vector),
        check_vma=False,
    )
```

```python
import types

import jax
import jax.numpy as jnp
from jax import lax
from jax.experimental import pallas as pl
from jax.experimental.pallas import tpu as pltpu
from jax.sharding import PartitionSpec as P

HEAD = 64
PAIR = 2 * HEAD
TILE = 256
FAST = 32
HALF = FAST // 2
AXES = ("dp", "seq")
LOG2E = 1.4426950408889634
AWAY = -1e30
GELU_A = 0.7978845608028654
GELU_B = 0.044715
BF = jnp.bfloat16
F4 = jnp.float32
VMEM_BYTES = 58 << 20


def mm(a, b):
    return lax.dot_general(a, b, (((1,), (0,)), ((), ())), preferred_element_type=F4)


def mt(a, b):
    return lax.dot_general(a, b, (((1,), (1,)), ((), ())), preferred_element_type=F4)


def tm(a, b):
    return lax.dot_general(a, b, (((0,), (0,)), ((), ())), preferred_element_type=F4)


def struct(shape, dtype=BF):
    return jax.ShapeDtypeStruct(tuple(shape), dtype)


ANY = pl.BlockSpec(memory_space=pl.ANY)
WHOLE = pl.BlockSpec(memory_space=pltpu.VMEM)
SMEM = pl.BlockSpec(memory_space=pltpu.SMEM)


def aslist(value):
    return list(value) if isinstance(value, (list, tuple)) else [value]


LAST = []
COST = dict(
    self_forward=16,
    cross_forward=22,
    middle=31,
    cross_back=26,
    cross_grads=16,
    self_back=10,
    self_grads=5,
    input_back=6,
    total=2,
)
SCALE = 1.0
SUBS = 2
SKEW = 1


def call(body, name, ins, outs, scratch, grid=(), after=()):
    us = COST.get(name, 1.5)
    ins = dict(ins, after=(LAST + list(after), ANY))
    layout = [(key, len(aslist(value)), isinstance(value, (list, tuple))) for key, (value, _) in ins.items()]
    layout += [(key, len(aslist(value)), isinstance(value, (list, tuple))) for key, (value, _) in outs.items()]
    layout += [(key, 1, False) for key in scratch]

    def kernel(*refs):
        held, at = {}, 0
        for key, count, many in layout:
            held[key] = list(refs[at : at + count]) if many else refs[at]
            at += count
        body(types.SimpleNamespace(**held))

    arrays = [x for value, _ in ins.values() for x in aslist(value)]
    in_specs = []
    for value, spec in ins.values():
        in_specs += spec if isinstance(spec, list) else [spec] * len(aslist(value))
    out_specs = [spec for value, spec in outs.values() for _ in aslist(value)]
    out_shape = [x for value, _ in outs.values() for x in aslist(value)]
    result = pl.pallas_call(
        kernel,
        name=name,
        grid=grid,
        in_specs=in_specs,
        out_specs=out_specs,
        out_shape=out_shape,
        scratch_shapes=list(scratch.values()),
        compiler_params=pltpu.CompilerParams(vmem_limit_bytes=VMEM_BYTES),
        cost_estimate=pl.CostEstimate(flops=int(us * SCALE * 1.1e9), bytes_accessed=0, transcendentals=0),
    )(*arrays)
    LAST[:] = [result[-1]]
    found, at = {}, 0
    for key, (value, _) in outs.items():
        count = len(aslist(value))
        found[key] = list(result[at : at + count]) if isinstance(value, (list, tuple)) else result[at]
        at += count
    return types.SimpleNamespace(**found)


def vmem(*shape, dtype=BF):
    return pltpu.VMEM(shape, dtype)


ORDER = [((p % 4) << 3) | ((p // 4 % 4) << 1) | (p // HALF) for p in range(FAST)]


def wait_all(buffer, sem):
    pltpu.make_async_copy(buffer, buffer, sem).wait()


def start_weight(dst, parts, first, me, sem):
    columns = dst.shape[-1]
    if len(parts) == 1:
        pltpu.make_async_copy(parts[0].at[:, pl.ds(first, columns)], dst, sem).start()
    else:
        span = dst.shape[0] // FAST
        each = FAST // len(parts)
        for p in range(FAST):
            place = pl.multiple_of((me ^ ORDER[p]) * span, span)
            src = parts[p // each].at[pl.ds((p % each) * span, span), pl.ds(first, columns)]
            pltpu.make_async_copy(src, dst.at[pl.ds(place, span)], sem).start()


def start_grad(src, parts, me, sem):
    if len(parts) == 1:
        pltpu.make_async_copy(src, parts[0], sem).start()
        return
    span = src.shape[0] // FAST
    for p in range(FAST):
        place = pl.multiple_of((me ^ ORDER[p]) * span, span)
        dst = parts[p // HALF].at[pl.ds((p % HALF) * span, span)]
        pltpu.make_async_copy(src.at[pl.ds(place, span)], dst, sem).start()


def grad_shapes(rows, columns, fast):
    return [struct((rows // 2, columns))] * 2 if fast else [struct((rows, columns))]


def take(ref, first=0, columns=None):
    columns = ref.shape[-1] - first if columns is None else columns
    return ref[..., first : first + columns].reshape(-1, columns)


def put(ref, value, first):
    ref[:, first : first + value.shape[1]] = value.astype(BF)


def norm(values):
    centered = values - jnp.mean(values, axis=-1, keepdims=True)
    inverse = lax.rsqrt(jnp.mean(centered * centered, axis=-1, keepdims=True) + 1e-05)
    return centered * inverse, inverse


def norm_back(upstream, normed, inverse, gain_row):
    gain_part = jnp.sum(upstream * normed, axis=0, keepdims=True)
    shift_part = jnp.sum(upstream, axis=0, keepdims=True)
    scaled = upstream * gain_row
    centered = scaled - jnp.mean(scaled, axis=-1, keepdims=True)
    value = inverse * (centered - normed * jnp.mean(scaled * normed, axis=-1, keepdims=True))
    return value, gain_part, shift_part


def lane_masks(dtype):
    lane = lax.broadcasted_iota(jnp.int32, (1, PAIR), 1)
    own = [(lane // HEAD == h).astype(dtype) for h in range(2)]

    def spot(h, k):
        return ((lane // HEAD == 1 - h) & (lane % HEAD == k)).astype(dtype)

    return own, spot


def attend_pair(causal, query, key, value, augq, augk, tri, ctx_out, qa_out, ka_out):
    total = key.shape[0]
    own, spot = lane_masks(F4)
    own_low = [mask.astype(BF) for mask in own]
    eighth = [(mask * HEAD ** (-0.5)).astype(BF) for mask in own]
    wide = jnp.concatenate([value, jnp.ones((total, PAIR), BF)], axis=1)
    keys = []
    for h in range(2):
        keys.append(key * own_low[h] + augk[h])
        ka_out[h] = keys[h]
    units = [(i, h) for i in range(query.shape[0] // TILE) for h in range(2)]
    scores, probs, halves = {}, {}, {}

    def score(i, h):
        rows = slice(i * TILE, (i + 1) * TILE)
        width = (i + 1) * TILE if causal else total
        head = query[rows] * eighth[h] + augq[h, rows]
        s = mt(head, keys[h][:width])
        if causal:
            tail = s[:, width - TILE :] + tri[...]
            s = jnp.concatenate([s[:, : width - TILE], tail], axis=1) if i else tail
        return s, head

    def finish(i, h, low, top, head):
        rows = slice(i * TILE, (i + 1) * TILE)
        both = mm(low, wide[: low.shape[1]])
        sums = both[:, PAIR:]
        halves[h] = both[:, :PAIR] / sums
        rest = -(top + jnp.log(sums))
        high = rest.astype(BF).astype(F4)
        rest = rest - high
        middle = rest.astype(BF).astype(F4)
        extra = high * spot(h, 8) + middle * spot(h, 9) + (rest - middle) * spot(h, 10)
        qa_out[h, rows] = head + extra.astype(BF)
        if h == 1:
            ctx_out[rows] = (halves[0] * own[0] + halves[1] * own[1]).astype(BF)

    count = len(units)
    for t in range(count + 2):
        if t < count:
            scores[t] = score(*units[t])
        if 0 <= t - 2 < count:
            finish(*units[t - 2], *probs.pop(t - 2))
        if 0 <= t - 1 < count:
            s, head = scores.pop(t - 1)
            top = jnp.max(s, axis=1, keepdims=True)
            low = jnp.exp2(s * LOG2E - top * LOG2E).astype(BF)
            probs[t - 1] = (low, top, head)


def self_forward(place, x, parts, augq, augk, tri):
    full, width = x.shape
    heads = width // HEAD

    def body(n):
        pair = pl.program_id(0)

        @pl.when(pair == 0)
        def _():
            start_weight(n.w, n.parts, 0, n.place[0], n.sem)
            wait_all(n.w, n.sem)
            for c in range(0, 3 * width, 512):
                n.qkv[:, c : c + 512] = mm(n.x[...], take(n.w, c, 512)).astype(BF)

        def columns(part):
            return n.qkv[:, pl.ds(pl.multiple_of(part * width + pair * PAIR, PAIR), PAIR)]

        value = columns(2)
        n.value[...] = value
        attend_pair(True, columns(0), columns(1), value, n.augq, n.augk, n.tri, n.ctx, n.qa, n.ka)

    both = pl.BlockSpec((2, full, PAIR), lambda p: (p, 0, 0))
    fixed = pl.BlockSpec((2, full, PAIR), lambda p: (0, 0, 0))
    cols = pl.BlockSpec((full, PAIR), lambda p: (0, p))
    return call(
        body,
        "self_forward",
        dict(
            place=(place, SMEM),
            x=(x, pl.BlockSpec((full, width), lambda p: (0, 0))),
            parts=(parts, ANY),
            augq=(augq, fixed),
            augk=(augk, fixed),
            tri=(tri, pl.BlockSpec((TILE, TILE), lambda p: (0, 0))),
        ),
        dict(
            ctx=(struct((full, width)), cols),
            qa=(struct((heads, full, PAIR)), both),
            ka=(struct((heads, full, PAIR)), both),
            value=(struct((full, width)), cols),
        ),
        dict(
            w=vmem(width, 3 * width),
            qkv=vmem(full, 3 * width),
            sem=pltpu.SemaphoreType.DMA,
        ),
        grid=(heads // 2,),
    )


def unfold_vectors(blocks, vec, bias):
    width, hidden = vec.shape[1], bias.shape[1]
    piece, part = width // FAST, hidden // FAST
    lane = lax.broadcasted_iota(jnp.int32, (PAIR, width), 0)
    col = lax.broadcasted_iota(jnp.int32, (PAIR, width), 1)
    wide = mm(blocks, (lane == col % piece).astype(BF))
    row = lax.broadcasted_iota(jnp.int32, (width, width), 0)
    col = lax.broadcasted_iota(jnp.int32, (width, width), 1)
    wide = jnp.where(row // 16 == col // piece, wide, 0.0).astype(BF)
    line = lax.broadcasted_iota(jnp.int32, (8, width), 0)
    vec[...] = mm((line == lax.broadcasted_iota(jnp.int32, (8, width), 1) % 16).astype(BF), wide)
    owner = lax.broadcasted_iota(jnp.int32, (FAST, width), 0) * 16 + 7
    rows = mm((owner == lax.broadcasted_iota(jnp.int32, (FAST, width), 1)).astype(BF), blocks)
    for j in range(FAST):
        bias[:, j * part : (j + 1) * part] = rows[j : j + 1, :part]


def cross_forward(place, x, mem, parts, ctx, vec, bias, augq, augk, hidden, fast):
    full, width = x.shape
    heads = width // HEAD

    def body(n):
        pair = pl.program_id(0)

        @pl.when(pair == 0)
        def _():
            me = n.place[0]
            start_weight(n.w, n.parts, 0, me, n.sems.at[0])
            if fast:
                start_weight(n.blocks, n.parts, 5 * width, me, n.sems.at[1])
                wait_all(n.blocks, n.sems.at[1])
                unfold_vectors(n.blocks[...], n.vec, n.bias)
            else:
                n.vec[...] = n.vec_in[0][...]
                n.bias[...] = n.bias_in[0][...]
            wait_all(n.w, n.sems.at[0])
            for i in range(0, full, TILE):
                rows = slice(i, i + TILE)
                attn = mm(n.ctx[rows], n.w[:, :width])
                normed, inverse = norm(n.x[rows].astype(F4) + attn)
                n.xhat[rows] = normed
                n.inv[rows] = jnp.broadcast_to(inverse, (TILE, PAIR))
                first = (normed * n.vec[0:1] + n.vec[3:4]).astype(BF)
                n.q[rows] = mm(first, n.w[:, width : 2 * width]).astype(BF)
            for c in range(0, 2 * width, 512):
                n.kv[:, c : c + 512] = mm(n.mem[...], n.w[:, 2 * width + c : 2 * width + c + 512]).astype(BF)

        lanes = pl.ds(pl.multiple_of(pair * PAIR, PAIR), PAIR)
        late = pl.ds(pl.multiple_of(width + pair * PAIR, PAIR), PAIR)
        value = n.kv[:, late]
        n.value[...] = value
        attend_pair(False, n.q[:, lanes], n.kv[:, lanes], value, n.augq, n.augk, None, n.cctx, n.qa, n.ka)

    both = pl.BlockSpec((2, full, PAIR), lambda p: (p, 0, 0))
    fixed = pl.BlockSpec((2, full, PAIR), lambda p: (0, 0, 0))
    cols = pl.BlockSpec((full, PAIR), lambda p: (0, p))

    def still(shape):
        return pl.BlockSpec(shape, lambda p: (0, 0))

    return call(
        body,
        "cross_forward",
        dict(
            place=(place, SMEM),
            x=(x, still((full, width))),
            mem=(mem, still((full, width))),
            parts=(parts, ANY),
            ctx=(ctx, still((full, width))),
            vec_in=([] if fast else [vec], still((8, width))),
            bias_in=([] if fast else [bias], still((1, hidden))),
            augq=(augq, fixed),
            augk=(augk, fixed),
        ),
        dict(
            cctx=(struct((full, width)), cols),
            qa=(struct((heads, full, PAIR)), both),
            ka=(struct((heads, full, PAIR)), both),
            value=(struct((full, width)), cols),
            xhat=(struct((full, width), F4), still((full, width))),
            inv=(struct((full, PAIR), F4), still((full, PAIR))),
            vec=(struct((8, width), F4), still((8, width))),
            bias=(struct((1, hidden), F4), still((1, hidden))),
        ),
        dict(
            w=vmem(width, 4 * width),
            q=vmem(full, width),
            kv=vmem(full, 2 * width),
            blocks=vmem(width, PAIR),
            sems=pltpu.SemaphoreType.DMA((2,)),
        ),
        grid=(heads // 2,),
    )


def middle(place, x, cot, co_parts, ffn_parts, cctx, xhat, vec, bias, fast):
    full, width = x.shape
    hidden = bias.shape[1]
    fold = hidden // width
    late = hidden + width
    block = SUBS * TILE

    def body(n):
        me = n.place[0]
        step = pl.program_id(0)

        @pl.when(step == 0)
        def _():
            start_weight(n.co, n.co_parts, 4 * width, me, n.sems.at[0])
            if fast:
                whole = n.ffn_parts[0]
                pltpu.make_async_copy(whole.at[:, :, pl.ds(0, hidden)], n.up, n.sems.at[1]).start()
                for k in range(fold):
                    src = whole.at[:, :, pl.ds(hidden + k * width, width)]
                    pltpu.make_async_copy(src, n.down.at[:, k], n.sems.at[2]).start()
            else:
                start_weight(n.up, n.ffn_parts[:1], 0, me, n.sems.at[1])
                start_weight(n.down, n.ffn_parts[1:], 0, me, n.sems.at[2])
            n.vec_sum[...] = jnp.zeros(n.vec_sum.shape, F4)
            n.bias_sum[...] = jnp.zeros(n.bias_sum.shape, F4)
            wait_all(n.co, n.sems.at[0])
            wait_all(n.up, n.sems.at[1])
            wait_all(n.down, n.sems.at[2])

        vec = n.vec

        def tile_steps(k):
            rows = slice(k * TILE, (k + 1) * TILE)
            kept = pl.ds(pl.multiple_of(step * block + k * TILE, TILE), TILE)
            v = types.SimpleNamespace()

            def enter():
                context = n.cctx[rows]
                n.context[kept] = context
                v.first = n.xhat[rows] * vec[0:1] + vec[3:4] + mm(context, n.co[...])

            def norm_one():
                v.normed_one, v.inverse_one = norm(v.first)
                v.second = v.normed_one * vec[1:2] + vec[4:5]
                v.low = v.second.astype(BF)
                n.second[kept] = v.low

            def rise():
                v.pre = mm(v.low, take(n.up)) + n.bias[...]

            def gelu():
                pre = v.pre
                slope = GELU_A * GELU_B * (pre * pre) + GELU_A
                t = jnp.tanh(pre * slope)
                half = 0.5 * t + 0.5
                v.hid = (pre * half).astype(BF)
                n.hid[kept] = v.hid
                v.d_gelu = half + (0.5 - 0.5 * t * t) * pre * (3.0 * slope - 2.0 * GELU_A)

            def fall():
                v.ffn = mm(v.hid, take(n.down)) + vec[6:7]

            def norm_two():
                normed, inverse = norm(v.second + v.ffn + n.x[rows].astype(F4))
                n.out[rows] = (normed * vec[2:3] + vec[5:6]).astype(BF)
                v.d_three, gain, shift = norm_back(n.cot[rows].astype(F4), normed, inverse, vec[2:3])
                n.d3[rows] = v.d_three
                v.df = v.d_three.astype(BF)
                n.df[kept] = v.df
                n.vec_sum[2:3] += gain
                n.vec_sum[5:6] += shift
                n.vec_sum[6:7] += jnp.sum(v.d_three, axis=0, keepdims=True)

            def back_down():
                v.d_hid = mt(v.df, take(n.down))

            def back_gelu():
                d_pre = v.d_hid * v.d_gelu
                v.d_pre = d_pre.astype(BF)
                n.d_pre[kept] = v.d_pre
                n.bias_sum[...] += jnp.sum(d_pre, axis=0, keepdims=True)

            def back_up():
                v.d_second = v.d_three + mt(v.d_pre, take(n.up))

            def norm_one_back():
                d_two, gain, shift = norm_back(v.d_second, v.normed_one, v.inverse_one, vec[1:2])
                n.d2[rows] = d_two
                v.dc = d_two.astype(BF)
                n.dc[kept] = v.dc
                n.vec_sum[1:2] += gain
                n.vec_sum[4:5] += shift

            def leave():
                n.dcctx[rows] = mt(v.dc, n.co[...]).astype(BF)

            return [
                enter, norm_one, rise, gelu, fall, norm_two, back_down, back_gelu, back_up, norm_one_back, leave
            ]

        tiles = [tile_steps(k) for k in range(SUBS)]
        for t in range(len(tiles[0]) + SKEW * (SUBS - 1)):
            for k, steps in enumerate(tiles):
                if 0 <= t - SKEW * k < len(steps):
                    steps[t - SKEW * k]()

        @pl.when(step == full // block - 1)
        def _():
            for c in range(0, hidden, 512):
                part = tm(n.hid[:, c : c + 512], n.df[...]).astype(BF)
                if fast:
                    rows = width // FAST
                    part = part.reshape(512 // (fold * rows), fold, rows, width)
                    top = c // fold
                    for a in range(fold):
                        n.grad[top : top + 512 // fold, late + a * width : late + (a + 1) * width] = part[
                            :, a
                        ].reshape(512 // fold, width)
                else:
                    n.grad_down[c : c + 512] = part
            if fast:
                edge = pl.ds(late, fold * width)
                first = pltpu.make_async_copy(n.grad.at[:, edge], n.grads[0].at[:, edge], n.sems.at[0])
                edge = pl.ds(0, late)
                last = pltpu.make_async_copy(n.grad.at[:, edge], n.grads[0].at[:, edge], n.sems.at[1])
            else:
                first = pltpu.make_async_copy(n.grad_down, n.grads[1], n.sems.at[0])
                last = pltpu.make_async_copy(n.grad, n.grads[0], n.sems.at[1])
            first.start()
            for c in range(0, hidden, 512):
                n.grad[:, c : c + 512] = tm(n.second[...], n.d_pre[:, c : c + 512]).astype(BF)
            n.grad[:, hidden : hidden + width] = tm(n.context[...], n.dc[...]).astype(BF)
            last.start()
            share = hidden // n.bias_rows.shape[0]
            n.bias_rows[...] = jnp.zeros(n.bias_rows.shape, BF)
            for j in range(n.bias_rows.shape[0]):
                n.bias_rows[j : j + 1, :share] = n.bias_sum[:, j * share : (j + 1) * share].astype(BF)
            first.wait()
            last.wait()

    if fast:
        grads = [struct((width, late + fold * width))]
        scratch = dict(
            up=vmem(FAST, width // FAST, hidden),
            down=vmem(FAST, fold, width // FAST, width),
            grad=vmem(width, late + fold * width),
        )
    else:
        grads = [struct((width, late)), struct((hidden, width))]
        scratch = dict(
            up=vmem(width, hidden), down=vmem(hidden, width), grad=vmem(width, late), grad_down=vmem(hidden, width)
        )
    tile = pl.BlockSpec((block, width), lambda i: (i, 0))

    def still(shape):
        return pl.BlockSpec(shape, lambda i: (0, 0))

    return call(
        body,
        "middle",
        dict(
            place=(place, SMEM),
            x=(x, tile),
            cot=(cot, tile),
            co_parts=(co_parts, ANY),
            ffn_parts=(ffn_parts, ANY),
            cctx=(cctx, tile),
            xhat=(xhat, tile),
            vec=(vec, still(vec.shape)),
            bias=(bias, still(bias.shape)),
        ),
        dict(
            out=(struct((full, width)), tile),
            d3=(struct((full, width), F4), tile),
            d2=(struct((full, width), F4), tile),
            dcctx=(struct((full, width)), tile),
            vec_sum=(struct((8, width), F4), still((8, width))),
            bias_sum=(struct((1, hidden), F4), still((1, hidden))),
            bias_rows=(struct((FAST, PAIR)), still((FAST, PAIR))),
            grads=(grads, ANY),
        ),
        dict(
            scratch,
            co=vmem(width, width),
            context=vmem(full, width),
            second=vmem(full, width),
            hid=vmem(full, hidden),
            d_pre=vmem(full, hidden),
            df=vmem(full, width),
            dc=vmem(full, width),
            sems=pltpu.SemaphoreType.DMA((3,)),
        ),
        grid=(full // block,),
    )


def attend_pair_back(causal, qa, ka, value, ctx, dctx, tri, dq, dk, dv):
    own, spot = lane_masks(F4)
    total = value.shape[0]
    blocks = total // TILE
    upstream = dctx[...].astype(F4)
    product = upstream * ctx[...].astype(F4)
    row = lax.broadcasted_iota(jnp.int32, (PAIR, PAIR), 0) // HEAD
    col = lax.broadcasted_iota(jnp.int32, (PAIR, PAIR), 1) // HEAD
    swap = jnp.where(row != col, -1.0, 0.0).astype(BF)
    high = product.astype(BF)
    delta = mm(high, swap) + mm((product - high.astype(F4)).astype(BF), swap)
    delta_high = delta.astype(BF).astype(F4)
    delta_low = delta - delta_high
    values = value[...].astype(F4)
    d_query, d_key, d_value = [], [], []
    for h in range(2):
        spots = spot(h, 0) + spot(h, 1)
        do = (upstream * own[h] + delta_high * spot(h, 0) + delta_low * spot(h, 1)).astype(BF)
        va = (values * own[h] + spots).astype(BF)
        query, key = qa[h], ka[h]
        query_t = query.T[h * HEAD : (h + 1) * HEAD]
        do_t = do.T[h * HEAD : (h + 1) * HEAD]
        keys, vals, sums = [], [], [None] * blocks
        for j in range(blocks):
            start = j * TILE if causal else 0
            key_j, va_j = key[j * TILE : (j + 1) * TILE], va[j * TILE : (j + 1) * TILE]
            s = mt(query[start:], key_j)
            if causal:
                head = s[:TILE] + tri[...]
                s = jnp.concatenate([head, s[TILE:]], axis=0) if j < blocks - 1 else head
            prob = jnp.exp2(s * LOG2E)
            ds = (prob * mt(do[start:], va_j)).astype(BF)
            vals.append(mm(do_t[:, start:], prob.astype(BF)))
            keys.append(mm(query_t[:, start:], ds))
            back = mm(ds, key_j)
            for i in range(start // TILE, blocks):
                part = back[i * TILE - start : (i + 1) * TILE - start]
                sums[i] = part if sums[i] is None else sums[i] + part
        d_query.append(jnp.concatenate(sums, axis=0))
        d_key.append(jnp.concatenate(keys, axis=1))
        d_value.append(jnp.concatenate(vals, axis=1))
    dq[...] = ((d_query[0] * own[0] + d_query[1] * own[1]) * HEAD ** (-0.5)).astype(BF)
    dk[...] = jnp.concatenate(d_key, axis=0).T.astype(BF)
    dv[...] = jnp.concatenate(d_value, axis=0).T.astype(BF)


def attend_back(causal, qa, ka, value, ctx, dctx, tri, first, count):
    full = value.shape[0]

    def body(n):
        attend_pair_back(causal, n.qa, n.ka, n.value, n.ctx, n.dctx, n.tri, n.dq, n.dk, n.dv)

    both = pl.BlockSpec((2, full, PAIR), lambda p: (p + first, 0, 0))
    cols = pl.BlockSpec((full, PAIR), lambda p: (0, p + first))
    made = (struct((full, count * PAIR)), pl.BlockSpec((full, PAIR), lambda p: (0, p)))
    result = call(
        body,
        "self_back" if causal else "cross_back",
        dict(
            qa=(qa, both),
            ka=(ka, both),
            value=(value, cols),
            ctx=(ctx, cols),
            dctx=(dctx, cols),
            tri=(tri, pl.BlockSpec((TILE, TILE), lambda p: (0, 0))),
        ),
        dict(dq=made, dk=made, dv=made),
        {},
        grid=(count,),
    )
    return [result.dq, result.dk, result.dv]


def columns_of(parts, rows):
    return jnp.concatenate([part[rows] for part in parts], axis=1)


def cross_grads(place, mem, parts, dq, dk, dv, ctx, xhat, inv, d2, d3, vec, vec_mid, bias_mid, fast, after):
    full, width = mem.shape
    extra = PAIR if fast else 0

    def body(n):
        me = n.place[0]
        vec = n.vec
        start_weight(n.w, n.parts, 0, me, n.sems.at[0])
        n.vec_sum[...] = n.vec_mid[...]
        wait_all(n.w, n.sems.at[0])

        def tile(i, carry):
            rows = pl.ds(pl.multiple_of(i * TILE, TILE), TILE)
            normed = n.xhat[rows]
            n.first[rows] = (normed * vec[0:1] + vec[3:4]).astype(BF)
            d_first = n.d2[rows] + mt(columns_of(n.dq, rows), n.w[:, width : 2 * width])
            inverse = jnp.concatenate([n.inv[rows]] * (width // PAIR), axis=1)
            d_one, gain, shift = norm_back(d_first, normed, inverse, vec[0:1])
            n.d13[rows] = n.d3[rows] + d_one
            da = d_one.astype(BF)
            n.da[rows] = da
            n.dctx[rows] = mt(da, n.w[:, :width]).astype(BF)
            n.vec_sum[0:1] += gain
            n.vec_sum[3:4] += shift
            back = mt(columns_of(n.dk, rows), n.w[:, 2 * width : 3 * width])
            back = back + mt(columns_of(n.dv, rows), n.w[:, 3 * width :])
            n.mg[rows] = back.astype(BF)
            return carry

        lax.fori_loop(0, full // TILE, tile, 0)
        everything = slice(None)
        put(n.grad, tm(n.ctx[...], n.da[...]), 0)
        put(n.grad, tm(n.first[...], columns_of(n.dq, everything)), width)
        put(n.grad, tm(n.mem[...], columns_of(n.dk, everything)), 2 * width)
        put(n.grad, tm(n.mem[...], columns_of(n.dv, everything)), 3 * width)
        if fast:
            piece = width // FAST
            row = lax.broadcasted_iota(jnp.int32, (width, width), 0)
            col = lax.broadcasted_iota(jnp.int32, (width, width), 1)
            line = lax.broadcasted_iota(jnp.int32, (width, 8), 0) % piece
            pick_line = (line == lax.broadcasted_iota(jnp.int32, (width, 8), 1)).astype(BF)
            spread = mm(pick_line, n.vec_sum[...].astype(BF))
            spread = jnp.where(row // piece == col // piece, spread, 0.0).astype(BF)
            lane = lax.broadcasted_iota(jnp.int32, (width, PAIR), 1)
            fold = (lax.broadcasted_iota(jnp.int32, (width, PAIR), 0) % piece == lane).astype(BF)
            owner = lax.broadcasted_iota(jnp.int32, (width, FAST), 0)
            wanted = lax.broadcasted_iota(jnp.int32, (width, FAST), 1) * piece + 8
            put(n.grad, mm(spread, fold) + mm((owner == wanted).astype(BF), n.bias_mid[...]), 4 * width)
        start_grad(n.grad, n.grads, me, n.sems.at[1])
        wait_all(n.grad, n.sems.at[1])

    return call(
        body,
        "cross_grads",
        dict(
            place=(place, SMEM),
            mem=(mem, WHOLE),
            parts=(parts, ANY),
            dq=(dq, WHOLE),
            dk=(dk, WHOLE),
            dv=(dv, WHOLE),
            ctx=(ctx, WHOLE),
            xhat=(xhat, WHOLE),
            inv=(inv, WHOLE),
            d2=(d2, WHOLE),
            d3=(d3, WHOLE),
            vec=(vec, WHOLE),
            vec_mid=(vec_mid, WHOLE),
            bias_mid=(bias_mid, WHOLE),
        ),
        dict(
            mg=(struct((full, width)), WHOLE),
            d13=(struct((full, width), F4), WHOLE),
            dctx=(struct((full, width)), WHOLE),
            vec_sum=(struct((8, width), F4), WHOLE),
            grads=(grad_shapes(width, 4 * width + extra, fast), ANY),
        ),
        dict(
            w=vmem(width, 4 * width),
            first=vmem(full, width),
            da=vmem(full, width),
            grad=vmem(width, 4 * width + extra),
            sems=pltpu.SemaphoreType.DMA((2,)),
        ),
        after=after,
    )


def self_grads(place, x, dq, dk, dv, fast, after):
    full, width = x.shape

    def body(n):
        everything = slice(None)
        for c, d in enumerate((n.dq, n.dk, n.dv)):
            put(n.grad, tm(n.x[...], columns_of(d, everything)), c * width)
        start_grad(n.grad, n.grads, n.place[0], n.sem)
        wait_all(n.grad, n.sem)

    return call(
        body,
        "self_grads",
        dict(place=(place, SMEM), x=(x, WHOLE), dq=(dq, WHOLE), dk=(dk, WHOLE), dv=(dv, WHOLE)),
        dict(grads=(grad_shapes(width, 3 * width, fast), ANY)),
        dict(grad=vmem(width, 3 * width), sem=pltpu.SemaphoreType.DMA),
        after=after,
    ).grads


def input_back(place, parts, dq, dk, dv, d13, after):
    full, width = d13.shape

    def body(n):
        start_weight(n.w, n.parts, 0, n.place[0], n.sem)
        wait_all(n.w, n.sem)
        for i in range(0, full, TILE):
            rows = slice(i, i + TILE)
            back = n.d13[rows]
            for c, d in enumerate((n.dq, n.dk, n.dv)):
                back = back + mt(columns_of(d, rows), n.w[:, c * width : (c + 1) * width])
            n.ig[rows] = back.astype(BF)

    return call(
        body,
        "input_back",
        dict(
            place=(place, SMEM),
            parts=(parts, ANY),
            dq=(dq, WHOLE),
            dk=(dk, WHOLE),
            dv=(dv, WHOLE),
            d13=(d13, WHOLE),
        ),
        dict(ig=(struct((full, width)), WHOLE)),
        dict(w=vmem(width, 3 * width), sem=pltpu.SemaphoreType.DMA),
        after=after,
    ).ig


def total(groups, pieces, steps=1, after=()):
    rows = groups[0][0].shape[0]
    span = rows // pieces // steps
    widths = [group[0].shape[1] for group in groups]

    def body(n):
        left, at = 0, 0
        for group, columns in zip(groups, widths):
            for k, out in enumerate(n.outs):
                value = n.parts[at + k][...].astype(F4)
                for m in range(1, len(group)):
                    value = value + n.parts[at + m * pieces + k][...].astype(F4)
                out[:, left : left + columns] = value.astype(BF)
            left += columns
            at += len(group) * pieces

    def piece(k, columns):
        return pl.BlockSpec((span, columns), lambda i: (k * steps + i, 0))

    parts, specs = [], []
    for group, columns in zip(groups, widths):
        for array in group:
            for k in range(pieces):
                parts.append(array)
                specs.append(piece(k, columns))
    outs = [struct((rows // pieces, sum(widths)))] * pieces
    return call(
        body, "total", dict(parts=(parts, specs)), dict(outs=(outs, piece(0, sum(widths)))), {}, (steps,), after
    ).outs


def finish(arrays, cuts):
    rows = arrays[0].shape[0]

    def body(n):
        value = n.arrays[0][...].astype(F4)
        for array in n.arrays[1:]:
            value = value + array[...].astype(F4)
        for out, (low, high, *more) in zip(n.outs, cuts):
            if len(more) == 1:
                for k in range((high - low) // more[0]):
                    out[k * rows : (k + 1) * rows] = value[:, low + k * more[0] : low + (k + 1) * more[0]]
            elif more:
                out[...] = value[more[0] : more[1], low:high]
            else:
                out[...] = value[:, low:high]

    outs = []
    for low, high, *more in cuts:
        if len(more) == 1:
            outs.append(struct(((high - low) // more[0] * rows, more[0]), F4))
        else:
            outs.append(struct((more[1] - more[0] if more else rows, high - low), F4))
    return call(body, "total", dict(arrays=(arrays, WHOLE)), dict(outs=(outs, WHOLE)), {}).outs


def to_rows(array):
    seats = lax.axis_size("seq")
    blocks = array.reshape(seats, -1, array.shape[-1])
    return lax.all_to_all(blocks, "seq", split_axis=0, concat_axis=0, tiled=True)


def swap(value, bits):
    return lax.ppermute(value, AXES, [(i, i ^ bits) for i in range(FAST)])


def swap_all(value):
    groups = [list(range(core, FAST, 2)) for core in range(2)]
    return lax.all_to_all(value, AXES, split_axis=0, concat_axis=0, tiled=True, axis_index_groups=groups)


def join(arrays, axis, cuts=(), after=()):
    arrays = list(arrays)
    rows = sum(x.shape[0] for x in arrays) if axis == 0 else arrays[0].shape[0]
    columns = arrays[0].shape[1] if axis == 0 else sum(x.shape[1] for x in arrays)
    edges = [0, *cuts, columns]

    def body(n):
        at = 0
        for x in n.arrays:
            if axis == 1:
                n.outs[0][:, at : at + x.shape[1]] = x[...]
            else:
                for out, low, high in zip(n.outs, edges[:-1], edges[1:]):
                    out[at : at + x.shape[0]] = x[:, low:high]
            at += x.shape[axis]

    outs = [struct((rows, high - low)) for low, high in zip(edges[:-1], edges[1:])]
    return call(body, "join", dict(arrays=(arrays, WHOLE)), dict(outs=(outs, WHOLE)), {}, after=after).outs


def swap_plane(held):
    return [held] + [swap(held, bits) for bits in (2, 4, 6)]


def swap_line(held):
    return [held] + [swap(held, z << 3) for z in (1, 2, 3)]


def swap_cores(parts):
    return parts + [swap(part, 1) for part in parts]


def spread_plane(pieces):
    return [pieces[0]] + [swap(piece, bits) for piece, bits in zip(pieces[1:], (2, 4, 6))]


def spread_line(pieces):
    return [pieces[0]] + [swap(piece, z << 3) for z, piece in enumerate(pieces[1:], 1)]


def on_device(
    inputs,
    memory,
    seg_ids,
    mem_lengths,
    cotangent,
    qkv_weight,
    self_out_weight,
    cross_q_weight,
    cross_kv_weight,
    cross_out_weight,
    ffn_in_weight,
    ffn_in_bias,
    ffn_out_weight,
    norm_gains,
    shift_vectors,
):
    seats = lax.axis_size("seq")
    devices = lax.axis_size("dp") * seats
    span, width = inputs.shape[1:]
    hidden = ffn_in_weight.shape[1]
    full = seats * span
    seat = lax.axis_index("seq")
    me = lax.axis_index("dp") * seats + seat
    LAST.clear()
    rows, piece, bias_piece = qkv_weight.shape[0], norm_gains.shape[1], ffn_in_bias.shape[0]
    fast = devices == FAST and rows == 16 and hidden == 4 * width
    place = me.astype(jnp.int32).reshape(1)
    second_group = [self_out_weight, cross_q_weight, cross_kv_weight, cross_out_weight]
    if fast:
        fold = hidden // width
        block = jnp.concatenate(
            [
                jnp.pad(norm_gains, ((0, 0), (0, PAIR - piece))),
                jnp.pad(shift_vectors, ((0, 0), (0, PAIR - piece))),
                jnp.pad(ffn_in_bias[None], ((0, rows - 8), (0, PAIR - bias_piece))),
            ],
            axis=0,
        )
        folded = [ffn_in_weight] + [ffn_out_weight[k * rows : (k + 1) * rows] for k in range(fold)]
        (ffn,) = join(folded, 1)
        ffn_parts = [lax.all_gather(ffn, AXES, axis=0, tiled=False)]
        x = to_rows(inputs).reshape(full, width)
        (one,) = join(swap_line(qkv_weight), 0)
        one = swap_plane(one)
        (two,) = join([*second_group, block], 1, (), [x])
        two = swap_line(two)
        (one,) = join(one, 0, (), two[1:])
        qkv_parts = [one, swap(one, 1)]
        mem = to_rows(memory).reshape(full, width)
        (two,) = join(two, 0, (), [mem])
        two = swap_plane(two)
        vec, bias = None, None
    else:
        x = to_rows(inputs).reshape(full, width)
        qkv_parts = [lax.all_gather(qkv_weight, AXES, axis=0, tiled=True)]
        two_parts = [lax.all_gather(jnp.concatenate(second_group, axis=1), AXES, axis=0, tiled=True)]
        ffn_parts = [lax.all_gather(w, AXES, axis=0, tiled=True) for w in (ffn_in_weight, ffn_out_weight)]
        vec = lax.all_gather(jnp.concatenate([norm_gains, shift_vectors], axis=0), AXES, axis=1, tiled=True)
        vec = jnp.pad(vec.astype(F4), ((0, 1), (0, 0)))
        bias = lax.all_gather(ffn_in_bias, AXES, axis=0, tiled=True).astype(F4)[None]
        mem = to_rows(memory).reshape(full, width)
    cot = to_rows(cotangent).reshape(full, width)

    segments = lax.dynamic_index_in_dim(seg_ids, seat, 0, keepdims=False)
    ends = jnp.cumsum(lax.dynamic_index_in_dim(mem_lengths, seat, 0, keepdims=False))
    places = jnp.arange(full, dtype=jnp.int32)
    mem_segments = jnp.sum((places[:, None] >= ends[None, :]).astype(jnp.int32), axis=1)
    lane = jnp.arange(PAIR, dtype=jnp.int32)
    half = jnp.arange(2, dtype=jnp.int32)[:, None, None]
    free = (lane // HEAD)[None, None] == 1 - half
    number = (lane % HEAD)[None, None]

    def key_side(ids):
        away = jnp.where(ids[None, :, None] == number, 0.0, AWAY)
        ones = jnp.where(number < 11, 1.0, 0.0)
        return jnp.where(free, jnp.where(number < 8, away, ones), 0.0).astype(BF)

    augq = jnp.where(free & (number < 8) & (segments[None, :, None] == number), 1.0, 0.0).astype(BF)
    augk, augm = key_side(segments), key_side(mem_segments)
    corner = jnp.arange(TILE, dtype=jnp.int32)
    tri = jnp.where(corner[None, :] <= corner[:, None], 0.0, AWAY).astype(F4)

    a = self_forward(place, x, qkv_parts, augq, augk, tri)
    if fast:
        (two,) = join(two, 0)
        two_parts = [two, swap(two, 1)]
    c = cross_forward(place, x, mem, two_parts, a.ctx, vec, bias, augq, augm, hidden, fast)
    vec, bias = c.vec, c.bias
    m = middle(place, x, cot, two_parts, ffn_parts, c.cctx, c.xhat, vec, bias, fast)
    output = to_rows(m.out)
    pairs = width // PAIR
    first_half = pairs // 2

    if fast:
        big = lax.psum_scatter(m.grads[0], AXES, scatter_dimension=0, tiled=True)
    dq, dk, dv = zip(attend_back(False, c.qa, c.ka, c.value, c.cctx, m.dcctx, tri, 0, pairs))
    g = cross_grads(
        place, mem, two_parts, dq, dk, dv, a.ctx, c.xhat, c.inv, m.d2, m.d3, vec, m.vec_sum, m.bias_rows, fast, [output]
    )
    memory_grad = to_rows(g.mg)

    def self_part(first, count):
        return attend_back(True, a.qa, a.ka, a.value, a.ctx, g.dctx, tri, first, count)

    if fast:
        two_got = swap(g.grads[1], 1)
    one = self_part(0, first_half)
    if fast:
        two_sum = spread_plane(total([[g.grads[0], two_got]], 4))
    two = self_part(first_half, pairs - first_half)
    dq, dk, dv = zip(one, two)
    ig = input_back(place, qkv_parts, dq, dk, dv, g.d13, two_sum[1:] if fast else [])
    input_grad = to_rows(ig)
    qkv_g = self_grads(place, x, dq, dk, dv, fast, [memory_grad])
    memory_grad = memory_grad.astype(F4)
    if fast:
        qkv_sum = spread_plane(total([[qkv_g[0], swap(qkv_g[1], 1)]], 4, 1, [input_grad]))
        at = 7 * width
        qkv_sum, so_sum, cq_sum, ckv_sum, gains_sum, shifts_sum, bias_sum = finish(
            spread_line(total([qkv_sum, two_sum], 4)),
            (
                (0, 3 * width),
                (3 * width, 4 * width),
                (4 * width, 5 * width),
                (5 * width, at),
                (at, at + piece, 0, 3),
                (at, at + piece, 3, 7),
                (at, at + bias_piece, 8, 9),
            ),
        )
        up_sum, co_sum, down_sum = finish(
            [big], ((0, hidden), (hidden, hidden + width), (hidden + width, 2 * hidden + width, width))
        )
    else:

        def scatter(value, dim=0):
            return lax.psum_scatter(value.astype(F4), AXES, scatter_dimension=dim, tiled=True)

        upco_sum, down_sum, two_sum, qkv_sum = [scatter(v) for v in (*m.grads, *g.grads, *qkv_g)]
        up_sum, co_sum = upco_sum[:, :hidden], upco_sum[:, hidden:]
        so_sum, cq_sum, ckv_sum = two_sum[:, :width], two_sum[:, width : 2 * width], two_sum[:, 2 * width :]
        vec_sum, bias_sum = scatter(g.vec_sum[:7], 1), scatter(m.bias_sum[0])
        gains_sum, shifts_sum = vec_sum[:3], vec_sum[3:]
    return (
        output,
        input_grad.astype(F4),
        memory_grad,
        qkv_sum,
        so_sum,
        cq_sum,
        ckv_sum,
        co_sum,
        up_sum,
        bias_sum.reshape(-1),
        down_sum,
        gains_sum,
        shifts_sum,
    )


def solution(mesh):
    rows = P("dp", "seq", None)
    weight = P(AXES, None)
    vector = P(None, AXES)
    return jax.shard_map(
        on_device,
        mesh=mesh,
        in_specs=(rows, rows, P("dp", None), P("dp", None), rows)
        + (weight,) * 6
        + (P(AXES), weight, vector, vector),
        out_specs=(rows,) * 3 + (weight,) * 6 + (P(AXES), weight, vector, vector),
        check_vma=False,
    )
```

```python
import types

import jax
import jax.numpy as jnp
from jax import lax
from jax.experimental import pallas as pl
from jax.experimental.pallas import tpu as pltpu
from jax.sharding import PartitionSpec as P

HEAD = 64
PAIR = 2 * HEAD
TILE = 256
FAST = 32
HALF = FAST // 2
AXES = ("dp", "seq")
LOG2E = 1.4426950408889634
AWAY = -1e30
GELU_A = 0.7978845608028654
GELU_B = 0.044715
BF = jnp.bfloat16
F4 = jnp.float32
VMEM_BYTES = 58 << 20


def mm(a, b):
    return lax.dot_general(a, b, (((1,), (0,)), ((), ())), preferred_element_type=F4)


def mt(a, b):
    return lax.dot_general(a, b, (((1,), (1,)), ((), ())), preferred_element_type=F4)


def tm(a, b):
    return lax.dot_general(a, b, (((0,), (0,)), ((), ())), preferred_element_type=F4)


def struct(shape, dtype=BF):
    return jax.ShapeDtypeStruct(tuple(shape), dtype)


ANY = pl.BlockSpec(memory_space=pl.ANY)
WHOLE = pl.BlockSpec(memory_space=pltpu.VMEM)
SMEM = pl.BlockSpec(memory_space=pltpu.SMEM)


def aslist(value):
    return list(value) if isinstance(value, (list, tuple)) else [value]


LAST = []
COST = dict(
    self_forward=16,
    cross_forward=22,
    middle=31,
    cross_back=34,
    self_back=8,
    self_grads=4,
    total=2,
)
SCALE = 1.0
SUBS = 2
SKEW = 1


def call(body, name, ins, outs, scratch, grid=(), after=()):
    us = COST.get(name, 1.5)
    ins = dict(ins, after=(LAST + list(after), ANY))
    layout = [(key, len(aslist(value)), isinstance(value, (list, tuple))) for key, (value, _) in ins.items()]
    layout += [(key, len(aslist(value)), isinstance(value, (list, tuple))) for key, (value, _) in outs.items()]
    layout += [(key, 1, False) for key in scratch]

    def kernel(*refs):
        held, at = {}, 0
        for key, count, many in layout:
            held[key] = list(refs[at : at + count]) if many else refs[at]
            at += count
        body(types.SimpleNamespace(**held))

    arrays = [x for value, _ in ins.values() for x in aslist(value)]
    in_specs = []
    for value, spec in ins.values():
        in_specs += spec if isinstance(spec, list) else [spec] * len(aslist(value))
    out_specs = [spec for value, spec in outs.values() for _ in aslist(value)]
    out_shape = [x for value, _ in outs.values() for x in aslist(value)]
    result = pl.pallas_call(
        kernel,
        name=name,
        grid=grid,
        in_specs=in_specs,
        out_specs=out_specs,
        out_shape=out_shape,
        scratch_shapes=list(scratch.values()),
        compiler_params=pltpu.CompilerParams(vmem_limit_bytes=VMEM_BYTES),
        cost_estimate=pl.CostEstimate(flops=int(us * SCALE * 1.1e9), bytes_accessed=0, transcendentals=0),
    )(*arrays)
    LAST[:] = [result[-1]]
    found, at = {}, 0
    for key, (value, _) in outs.items():
        count = len(aslist(value))
        found[key] = list(result[at : at + count]) if isinstance(value, (list, tuple)) else result[at]
        at += count
    return types.SimpleNamespace(**found)


def vmem(*shape, dtype=BF):
    return pltpu.VMEM(shape, dtype)


ORDER = [((p % 4) << 3) | ((p // 4 % 4) << 1) | (p // HALF) for p in range(FAST)]


def wait_all(buffer, sem):
    pltpu.make_async_copy(buffer, buffer, sem).wait()


def start_weight(dst, parts, first, me, sem):
    columns = dst.shape[-1]
    if len(parts) == 1:
        pltpu.make_async_copy(parts[0].at[:, pl.ds(first, columns)], dst, sem).start()
    else:
        span = dst.shape[0] // FAST
        each = FAST // len(parts)
        for p in range(FAST):
            place = pl.multiple_of((me ^ ORDER[p]) * span, span)
            src = parts[p // each].at[pl.ds((p % each) * span, span), pl.ds(first, columns)]
            pltpu.make_async_copy(src, dst.at[pl.ds(place, span)], sem).start()


def start_grad(src, parts, me, sem):
    if len(parts) == 1:
        pltpu.make_async_copy(src, parts[0], sem).start()
        return
    span = src.shape[0] // FAST
    for p in range(FAST):
        place = pl.multiple_of((me ^ ORDER[p]) * span, span)
        dst = parts[p // HALF].at[pl.ds((p % HALF) * span, span)]
        pltpu.make_async_copy(src.at[pl.ds(place, span)], dst, sem).start()


def grad_shapes(rows, columns, fast):
    return [struct((rows // 2, columns))] * 2 if fast else [struct((rows, columns))]


def take(ref, first=0, columns=None):
    columns = ref.shape[-1] - first if columns is None else columns
    return ref[..., first : first + columns].reshape(-1, columns)


def put(ref, value, first):
    ref[:, first : first + value.shape[1]] = value.astype(BF)


def norm(values):
    centered = values - jnp.mean(values, axis=-1, keepdims=True)
    inverse = lax.rsqrt(jnp.mean(centered * centered, axis=-1, keepdims=True) + 1e-05)
    return centered * inverse, inverse


def norm_back(upstream, normed, inverse, gain_row):
    gain_part = jnp.sum(upstream * normed, axis=0, keepdims=True)
    shift_part = jnp.sum(upstream, axis=0, keepdims=True)
    scaled = upstream * gain_row
    centered = scaled - jnp.mean(scaled, axis=-1, keepdims=True)
    value = inverse * (centered - normed * jnp.mean(scaled * normed, axis=-1, keepdims=True))
    return value, gain_part, shift_part


def lane_masks(dtype):
    lane = lax.broadcasted_iota(jnp.int32, (1, PAIR), 1)
    own = [(lane // HEAD == h).astype(dtype) for h in range(2)]

    def spot(h, k):
        return ((lane // HEAD == 1 - h) & (lane % HEAD == k)).astype(dtype)

    return own, spot


def attend_pair(causal, query, key, value, augq, augk, tri, ctx_out, qa_out, ka_out):
    total = key.shape[0]
    own, spot = lane_masks(F4)
    own_low = [mask.astype(BF) for mask in own]
    eighth = [(mask * HEAD ** (-0.5)).astype(BF) for mask in own]
    wide = jnp.concatenate([value, jnp.ones((total, PAIR), BF)], axis=1)
    keys = []
    for h in range(2):
        keys.append(key * own_low[h] + augk[h])
        ka_out[h] = keys[h]
    units = [(i, h) for i in range(query.shape[0] // TILE) for h in range(2)]
    scores, probs, halves = {}, {}, {}

    def score(i, h):
        rows = slice(i * TILE, (i + 1) * TILE)
        width = (i + 1) * TILE if causal else total
        head = query[rows] * eighth[h] + augq[h, rows]
        s = mt(head, keys[h][:width])
        if causal:
            tail = s[:, width - TILE :] + tri[...]
            s = jnp.concatenate([s[:, : width - TILE], tail], axis=1) if i else tail
        return s, head

    def finish(i, h, low, top, head):
        rows = slice(i * TILE, (i + 1) * TILE)
        both = mm(low, wide[: low.shape[1]])
        sums = both[:, PAIR:]
        halves[h] = both[:, :PAIR] / sums
        rest = -(top + jnp.log(sums))
        high = rest.astype(BF).astype(F4)
        rest = rest - high
        middle = rest.astype(BF).astype(F4)
        extra = high * spot(h, 8) + middle * spot(h, 9) + (rest - middle) * spot(h, 10)
        qa_out[h, rows] = head + extra.astype(BF)
        if h == 1:
            ctx_out[rows] = (halves[0] * own[0] + halves[1] * own[1]).astype(BF)

    count = len(units)
    for t in range(count + 2):
        if t < count:
            scores[t] = score(*units[t])
        if 0 <= t - 2 < count:
            finish(*units[t - 2], *probs.pop(t - 2))
        if 0 <= t - 1 < count:
            s, head = scores.pop(t - 1)
            top = jnp.max(s, axis=1, keepdims=True)
            low = jnp.exp2(s * LOG2E - top * LOG2E).astype(BF)
            probs[t - 1] = (low, top, head)


def self_forward(place, x, parts, augq, augk, tri):
    full, width = x.shape
    heads = width // HEAD

    def body(n):
        pair = pl.program_id(0)

        @pl.when(pair == 0)
        def _():
            start_weight(n.w, n.parts, 0, n.place[0], n.sem)
            wait_all(n.w, n.sem)
            for c in range(0, 3 * width, 512):
                n.qkv[:, c : c + 512] = mm(n.x[...], take(n.w, c, 512)).astype(BF)

        def columns(part):
            return n.qkv[:, pl.ds(pl.multiple_of(part * width + pair * PAIR, PAIR), PAIR)]

        value = columns(2)
        n.value[...] = value
        attend_pair(True, columns(0), columns(1), value, n.augq, n.augk, n.tri, n.ctx, n.qa, n.ka)

    both = pl.BlockSpec((2, full, PAIR), lambda p: (p, 0, 0))
    fixed = pl.BlockSpec((2, full, PAIR), lambda p: (0, 0, 0))
    cols = pl.BlockSpec((full, PAIR), lambda p: (0, p))
    return call(
        body,
        "self_forward",
        dict(
            place=(place, SMEM),
            x=(x, pl.BlockSpec((full, width), lambda p: (0, 0))),
            parts=(parts, ANY),
            augq=(augq, fixed),
            augk=(augk, fixed),
            tri=(tri, pl.BlockSpec((TILE, TILE), lambda p: (0, 0))),
        ),
        dict(
            ctx=(struct((full, width)), cols),
            qa=(struct((heads, full, PAIR)), both),
            ka=(struct((heads, full, PAIR)), both),
            value=(struct((full, width)), cols),
        ),
        dict(
            w=vmem(width, 3 * width),
            qkv=vmem(full, 3 * width),
            sem=pltpu.SemaphoreType.DMA,
        ),
        grid=(heads // 2,),
    )


def unfold_vectors(blocks, vec, bias):
    width, hidden = vec.shape[1], bias.shape[1]
    piece, part = width // FAST, hidden // FAST
    lane = lax.broadcasted_iota(jnp.int32, (PAIR, width), 0)
    col = lax.broadcasted_iota(jnp.int32, (PAIR, width), 1)
    wide = mm(blocks, (lane == col % piece).astype(BF))
    row = lax.broadcasted_iota(jnp.int32, (width, width), 0)
    col = lax.broadcasted_iota(jnp.int32, (width, width), 1)
    wide = jnp.where(row // 16 == col // piece, wide, 0.0).astype(BF)
    line = lax.broadcasted_iota(jnp.int32, (8, width), 0)
    vec[...] = mm((line == lax.broadcasted_iota(jnp.int32, (8, width), 1) % 16).astype(BF), wide)
    owner = lax.broadcasted_iota(jnp.int32, (FAST, width), 0) * 16 + 7
    rows = mm((owner == lax.broadcasted_iota(jnp.int32, (FAST, width), 1)).astype(BF), blocks)
    for j in range(FAST):
        bias[:, j * part : (j + 1) * part] = rows[j : j + 1, :part]


def cross_forward(place, x, mem, parts, ctx, vec, bias, augq, augk, hidden, fast):
    full, width = x.shape
    heads = width // HEAD

    def body(n):
        pair = pl.program_id(0)

        @pl.when(pair == 0)
        def _():
            me = n.place[0]
            start_weight(n.w, n.parts, 0, me, n.sems.at[0])
            if fast:
                start_weight(n.blocks, n.parts, 5 * width, me, n.sems.at[1])
                wait_all(n.blocks, n.sems.at[1])
                unfold_vectors(n.blocks[...], n.vec, n.bias)
            else:
                n.vec[...] = n.vec_in[0][...]
                n.bias[...] = n.bias_in[0][...]
            wait_all(n.w, n.sems.at[0])
            for i in range(0, full, TILE):
                rows = slice(i, i + TILE)
                attn = mm(n.ctx[rows], n.w[:, :width])
                normed, inverse = norm(n.x[rows].astype(F4) + attn)
                n.xhat[rows] = normed.astype(BF)
                n.inv[rows] = jnp.broadcast_to(inverse, (TILE, PAIR))
                first = (normed * n.vec[0:1] + n.vec[3:4]).astype(BF)
                n.q[rows] = mm(first, n.w[:, width : 2 * width]).astype(BF)
            for c in range(0, 2 * width, 512):
                n.kv[:, c : c + 512] = mm(n.mem[...], n.w[:, 2 * width + c : 2 * width + c + 512]).astype(BF)

        lanes = pl.ds(pl.multiple_of(pair * PAIR, PAIR), PAIR)
        late = pl.ds(pl.multiple_of(width + pair * PAIR, PAIR), PAIR)
        value = n.kv[:, late]
        n.value[...] = value
        attend_pair(False, n.q[:, lanes], n.kv[:, lanes], value, n.augq, n.augk, None, n.cctx, n.qa, n.ka)

    both = pl.BlockSpec((2, full, PAIR), lambda p: (p, 0, 0))
    fixed = pl.BlockSpec((2, full, PAIR), lambda p: (0, 0, 0))
    cols = pl.BlockSpec((full, PAIR), lambda p: (0, p))

    def still(shape):
        return pl.BlockSpec(shape, lambda p: (0, 0))

    return call(
        body,
        "cross_forward",
        dict(
            place=(place, SMEM),
            x=(x, still((full, width))),
            mem=(mem, still((full, width))),
            parts=(parts, ANY),
            ctx=(ctx, still((full, width))),
            vec_in=([] if fast else [vec], still((8, width))),
            bias_in=([] if fast else [bias], still((1, hidden))),
            augq=(augq, fixed),
            augk=(augk, fixed),
        ),
        dict(
            cctx=(struct((full, width)), cols),
            qa=(struct((heads, full, PAIR)), both),
            ka=(struct((heads, full, PAIR)), both),
            value=(struct((full, width)), cols),
            xhat=(struct((full, width)), still((full, width))),
            inv=(struct((full, PAIR), F4), still((full, PAIR))),
            vec=(struct((8, width), F4), still((8, width))),
            bias=(struct((1, hidden), F4), still((1, hidden))),
        ),
        dict(
            w=vmem(width, 4 * width),
            q=vmem(full, width),
            kv=vmem(full, 2 * width),
            blocks=vmem(width, PAIR),
            sems=pltpu.SemaphoreType.DMA((2,)),
        ),
        grid=(heads // 2,),
    )


def middle(place, x, cot, co_parts, ffn_parts, cctx, xhat, vec, bias, fast):
    full, width = x.shape
    hidden = bias.shape[1]
    fold = hidden // width
    late = hidden + width
    block = SUBS * TILE

    def body(n):
        me = n.place[0]
        step = pl.program_id(0)

        @pl.when(step == 0)
        def _():
            start_weight(n.co, n.co_parts, 4 * width, me, n.sems.at[0])
            if fast:
                whole = n.ffn_parts[0]
                pltpu.make_async_copy(whole.at[:, :, pl.ds(0, hidden)], n.up, n.sems.at[1]).start()
                for k in range(fold):
                    src = whole.at[:, :, pl.ds(hidden + k * width, width)]
                    pltpu.make_async_copy(src, n.down.at[:, k], n.sems.at[2]).start()
            else:
                start_weight(n.up, n.ffn_parts[:1], 0, me, n.sems.at[1])
                start_weight(n.down, n.ffn_parts[1:], 0, me, n.sems.at[2])
            n.vec_sum[...] = jnp.zeros(n.vec_sum.shape, F4)
            n.bias_sum[...] = jnp.zeros(n.bias_sum.shape, F4)
            wait_all(n.co, n.sems.at[0])
            wait_all(n.up, n.sems.at[1])
            wait_all(n.down, n.sems.at[2])

        vec = n.vec

        def tile_steps(k):
            rows = slice(k * TILE, (k + 1) * TILE)
            kept = pl.ds(pl.multiple_of(step * block + k * TILE, TILE), TILE)
            v = types.SimpleNamespace()

            def enter():
                context = n.cctx[rows]
                n.context[kept] = context
                v.first = n.xhat[rows].astype(F4) * vec[0:1] + vec[3:4] + mm(context, n.co[...])

            def norm_one():
                v.normed_one, v.inverse_one = norm(v.first)
                v.second = v.normed_one * vec[1:2] + vec[4:5]
                v.low = v.second.astype(BF)
                n.second[kept] = v.low

            def rise():
                v.pre = mm(v.low, take(n.up)) + n.bias[...]

            def gelu():
                pre = v.pre
                slope = GELU_A * GELU_B * (pre * pre) + GELU_A
                t = jnp.tanh(pre * slope)
                half = 0.5 * t + 0.5
                v.hid = (pre * half).astype(BF)
                n.hid[kept] = v.hid
                v.d_gelu = half + (0.5 - 0.5 * t * t) * pre * (3.0 * slope - 2.0 * GELU_A)

            def fall():
                v.ffn = mm(v.hid, take(n.down)) + vec[6:7]

            def norm_two():
                normed, inverse = norm(v.second + v.ffn + n.x[rows].astype(F4))
                n.out[rows] = (normed * vec[2:3] + vec[5:6]).astype(BF)
                v.d_three, gain, shift = norm_back(n.cot[rows].astype(F4), normed, inverse, vec[2:3])
                v.df = v.d_three.astype(BF)
                n.d3[rows] = v.df
                n.df[kept] = v.df
                n.vec_sum[2:3] += gain
                n.vec_sum[5:6] += shift
                n.vec_sum[6:7] += jnp.sum(v.d_three, axis=0, keepdims=True)

            def back_down():
                v.d_hid = mt(v.df, take(n.down))

            def back_gelu():
                d_pre = v.d_hid * v.d_gelu
                v.d_pre = d_pre.astype(BF)
                n.d_pre[kept] = v.d_pre
                n.bias_sum[...] += jnp.sum(d_pre, axis=0, keepdims=True)

            def back_up():
                v.d_second = v.d_three + mt(v.d_pre, take(n.up))

            def norm_one_back():
                d_two, gain, shift = norm_back(v.d_second, v.normed_one, v.inverse_one, vec[1:2])
                v.dc = d_two.astype(BF)
                n.d2[rows] = v.dc
                n.dc[kept] = v.dc
                n.vec_sum[1:2] += gain
                n.vec_sum[4:5] += shift

            def leave():
                n.dcctx[rows] = mt(v.dc, n.co[...]).astype(BF)

            return [
                enter, norm_one, rise, gelu, fall, norm_two, back_down, back_gelu, back_up, norm_one_back, leave
            ]

        tiles = [tile_steps(k) for k in range(SUBS)]
        for t in range(len(tiles[0]) + SKEW * (SUBS - 1)):
            for k, steps in enumerate(tiles):
                if 0 <= t - SKEW * k < len(steps):
                    steps[t - SKEW * k]()

        @pl.when(step == full // block - 1)
        def _():
            for c in range(0, hidden, 512):
                part = tm(n.hid[:, c : c + 512], n.df[...]).astype(BF)
                if fast:
                    rows = width // FAST
                    part = part.reshape(512 // (fold * rows), fold, rows, width)
                    top = c // fold
                    for a in range(fold):
                        n.grad[top : top + 512 // fold, late + a * width : late + (a + 1) * width] = part[
                            :, a
                        ].reshape(512 // fold, width)
                else:
                    n.grad_down[c : c + 512] = part
            if fast:
                edge = pl.ds(late, fold * width)
                first = pltpu.make_async_copy(n.grad.at[:, edge], n.grads[0].at[:, edge], n.sems.at[0])
                edge = pl.ds(0, late)
                last = pltpu.make_async_copy(n.grad.at[:, edge], n.grads[0].at[:, edge], n.sems.at[1])
            else:
                first = pltpu.make_async_copy(n.grad_down, n.grads[1], n.sems.at[0])
                last = pltpu.make_async_copy(n.grad, n.grads[0], n.sems.at[1])
            first.start()
            for c in range(0, hidden, 512):
                n.grad[:, c : c + 512] = tm(n.second[...], n.d_pre[:, c : c + 512]).astype(BF)
            n.grad[:, hidden : hidden + width] = tm(n.context[...], n.dc[...]).astype(BF)
            last.start()
            share = hidden // n.bias_rows.shape[0]
            n.bias_rows[...] = jnp.zeros(n.bias_rows.shape, BF)
            for j in range(n.bias_rows.shape[0]):
                n.bias_rows[j : j + 1, :share] = n.bias_sum[:, j * share : (j + 1) * share].astype(BF)
            first.wait()
            last.wait()

    if fast:
        grads = [struct((width, late + fold * width))]
        scratch = dict(
            up=vmem(FAST, width // FAST, hidden),
            down=vmem(FAST, fold, width // FAST, width),
            grad=vmem(width, late + fold * width),
        )
    else:
        grads = [struct((width, late)), struct((hidden, width))]
        scratch = dict(
            up=vmem(width, hidden), down=vmem(hidden, width), grad=vmem(width, late), grad_down=vmem(hidden, width)
        )
    tile = pl.BlockSpec((block, width), lambda i: (i, 0))

    def still(shape):
        return pl.BlockSpec(shape, lambda i: (0, 0))

    return call(
        body,
        "middle",
        dict(
            place=(place, SMEM),
            x=(x, tile),
            cot=(cot, tile),
            co_parts=(co_parts, ANY),
            ffn_parts=(ffn_parts, ANY),
            cctx=(cctx, tile),
            xhat=(xhat, tile),
            vec=(vec, still(vec.shape)),
            bias=(bias, still(bias.shape)),
        ),
        dict(
            out=(struct((full, width)), tile),
            d3=(struct((full, width)), tile),
            d2=(struct((full, width)), tile),
            dcctx=(struct((full, width)), tile),
            vec_sum=(struct((8, width), F4), still((8, width))),
            bias_sum=(struct((1, hidden), F4), still((1, hidden))),
            bias_rows=(struct((FAST, PAIR)), still((FAST, PAIR))),
            grads=(grads, ANY),
        ),
        dict(
            scratch,
            co=vmem(width, width),
            context=vmem(full, width),
            second=vmem(full, width),
            hid=vmem(full, hidden),
            d_pre=vmem(full, hidden),
            df=vmem(full, width),
            dc=vmem(full, width),
            sems=pltpu.SemaphoreType.DMA((3,)),
        ),
        grid=(full // block,),
    )


def attend_pair_back(causal, qa, ka, value, ctx, dctx, tri, dq, dk, dv):
    own, spot = lane_masks(F4)
    total = value.shape[0]
    blocks = total // TILE
    upstream = dctx[...].astype(F4)
    product = upstream * ctx[...].astype(F4)
    row = lax.broadcasted_iota(jnp.int32, (PAIR, PAIR), 0) // HEAD
    col = lax.broadcasted_iota(jnp.int32, (PAIR, PAIR), 1) // HEAD
    swap = jnp.where(row != col, -1.0, 0.0).astype(BF)
    high = product.astype(BF)
    delta = mm(high, swap) + mm((product - high.astype(F4)).astype(BF), swap)
    delta_high = delta.astype(BF).astype(F4)
    delta_low = delta - delta_high
    values = value[...].astype(F4)
    d_query, d_key, d_value = [], [], []
    for h in range(2):
        spots = spot(h, 0) + spot(h, 1)
        do = (upstream * own[h] + delta_high * spot(h, 0) + delta_low * spot(h, 1)).astype(BF)
        va = (values * own[h] + spots).astype(BF)
        query, key = qa[h], ka[h]
        query_t = query.T[h * HEAD : (h + 1) * HEAD]
        do_t = do.T[h * HEAD : (h + 1) * HEAD]
        keys, vals, sums = [], [], [None] * blocks
        for j in range(blocks):
            start = j * TILE if causal else 0
            key_j, va_j = key[j * TILE : (j + 1) * TILE], va[j * TILE : (j + 1) * TILE]
            s = mt(query[start:], key_j)
            if causal:
                head = s[:TILE] + tri[...]
                s = jnp.concatenate([head, s[TILE:]], axis=0) if j < blocks - 1 else head
            prob = jnp.exp2(s * LOG2E)
            ds = (prob * mt(do[start:], va_j)).astype(BF)
            vals.append(mm(do_t[:, start:], prob.astype(BF)))
            keys.append(mm(query_t[:, start:], ds))
            back = mm(ds, key_j)
            for i in range(start // TILE, blocks):
                part = back[i * TILE - start : (i + 1) * TILE - start]
                sums[i] = part if sums[i] is None else sums[i] + part
        d_query.append(jnp.concatenate(sums, axis=0))
        d_key.append(jnp.concatenate(keys, axis=1))
        d_value.append(jnp.concatenate(vals, axis=1))
    dq[...] = ((d_query[0] * own[0] + d_query[1] * own[1]) * HEAD ** (-0.5)).astype(BF)
    dk[...] = jnp.concatenate(d_key, axis=0).T.astype(BF)
    dv[...] = jnp.concatenate(d_value, axis=0).T.astype(BF)


def cross_back(place, mem, parts, att, dcctx, tri, ctx, d2, d3, vec, vec_mid, bias_mid, fast, after):
    full, width = mem.shape
    extra = PAIR if fast else 0
    pairs, tiles = width // PAIR, full // TILE

    def body(n):
        me = n.place[0]
        step = pl.program_id(0)
        vec = n.vec
        loads = [(n.ctx, n.kept_ctx), (n.mem, n.kept_mem), (n.xhat, n.kept_xhat), (n.inv, n.kept_inv)]
        loads += [(n.d2, n.kept_d2), (n.d3, n.kept_d3)]

        @pl.when(step == 0)
        def _():
            n.vec_sum[...] = n.vec_mid[...]
            start_weight(n.w, n.parts, 0, me, n.sems.at[0])
            for k, (src, dst) in enumerate(loads):
                pltpu.make_async_copy(src, dst, n.sems.at[k + 1]).start()

        @pl.when(step < pairs)
        def _():
            lanes = pl.ds(pl.multiple_of(jnp.minimum(step, pairs - 1) * PAIR, PAIR), PAIR)
            attend_pair_back(
                False,
                n.qa,
                n.ka,
                n.value,
                n.cctx,
                n.dcctx,
                n.tri,
                n.dq.at[:, lanes],
                n.dk.at[:, lanes],
                n.dv.at[:, lanes],
            )

        @pl.when(step == pairs)
        def _():
            wait_all(n.w, n.sems.at[0])
            for k, (src, dst) in enumerate(loads):
                pltpu.make_async_copy(src, dst, n.sems.at[k + 1]).wait()

        @pl.when(step >= pairs)
        def _():
            rows = pl.ds(pl.multiple_of(jnp.maximum(step - pairs, 0) * TILE, TILE), TILE)
            normed = n.kept_xhat[rows].astype(F4)
            n.first[rows] = (normed * vec[0:1] + vec[3:4]).astype(BF)
            d_first = n.kept_d2[rows].astype(F4) + mt(n.dq[rows], n.w[:, width : 2 * width])
            back = mt(n.dk[rows], n.w[:, 2 * width : 3 * width]) + mt(n.dv[rows], n.w[:, 3 * width :])
            n.mg[...] = back.astype(BF)
            inverse = jnp.concatenate([n.kept_inv[rows]] * (width // PAIR), axis=1)
            d_one, gain, shift = norm_back(d_first, normed, inverse, vec[0:1])
            n.d13[...] = (n.kept_d3[rows].astype(F4) + d_one).astype(BF)
            da = d_one.astype(BF)
            n.da[rows] = da
            n.dctx[...] = mt(da, n.w[:, :width]).astype(BF)
            n.vec_sum[0:1] += gain
            n.vec_sum[3:4] += shift

        @pl.when(step == pairs + tiles - 1)
        def _():
            put(n.grad, tm(n.kept_mem[...], n.dk[...]), 2 * width)
            put(n.grad, tm(n.kept_mem[...], n.dv[...]), 3 * width)
            put(n.grad, tm(n.kept_ctx[...], n.da[...]), 0)
            put(n.grad, tm(n.first[...], n.dq[...]), width)
            if fast:
                piece = width // FAST
                row = lax.broadcasted_iota(jnp.int32, (width, width), 0)
                col = lax.broadcasted_iota(jnp.int32, (width, width), 1)
                line = lax.broadcasted_iota(jnp.int32, (width, 8), 0) % piece
                pick_line = (line == lax.broadcasted_iota(jnp.int32, (width, 8), 1)).astype(BF)
                spread = mm(pick_line, n.vec_sum[...].astype(BF))
                spread = jnp.where(row // piece == col // piece, spread, 0.0).astype(BF)
                lane = lax.broadcasted_iota(jnp.int32, (width, PAIR), 1)
                fold = (lax.broadcasted_iota(jnp.int32, (width, PAIR), 0) % piece == lane).astype(BF)
                owner = lax.broadcasted_iota(jnp.int32, (width, FAST), 0)
                wanted = lax.broadcasted_iota(jnp.int32, (width, FAST), 1) * piece + 8
                put(n.grad, mm(spread, fold) + mm((owner == wanted).astype(BF), n.bias_mid[...]), 4 * width)
            start_grad(n.grad, n.grads, me, n.sems.at[0])
            wait_all(n.grad, n.sems.at[0])

    def pair(i):
        return jnp.minimum(i, pairs - 1)

    both = pl.BlockSpec((2, full, PAIR), lambda i: (pair(i), 0, 0))
    cols = pl.BlockSpec((full, PAIR), lambda i: (0, pair(i)))
    tile = pl.BlockSpec((TILE, width), lambda i: (jnp.maximum(i - pairs, 0), 0))

    def still(array):
        return (array, pl.BlockSpec(array.shape, lambda i: (0, 0)))

    return call(
        body,
        "cross_back",
        dict(
            place=(place, SMEM),
            qa=(att.qa, both),
            ka=(att.ka, both),
            value=(att.value, cols),
            cctx=(att.cctx, cols),
            dcctx=(dcctx, cols),
            tri=still(tri),
            parts=(parts, ANY),
            mem=(mem, ANY),
            ctx=(ctx, ANY),
            xhat=(att.xhat, ANY),
            inv=(att.inv, ANY),
            d2=(d2, ANY),
            d3=(d3, ANY),
            vec=still(vec),
            vec_mid=still(vec_mid),
            bias_mid=still(bias_mid),
        ),
        dict(
            mg=(struct((full, width)), tile),
            d13=(struct((full, width)), tile),
            dctx=(struct((full, width)), tile),
            vec_sum=still(struct((8, width), F4)),
            grads=(grad_shapes(width, 4 * width + extra, fast), ANY),
        ),
        dict(
            w=vmem(width, 4 * width),
            dq=vmem(full, width),
            dk=vmem(full, width),
            dv=vmem(full, width),
            kept_ctx=vmem(full, width),
            kept_mem=vmem(full, width),
            kept_xhat=vmem(full, width),
            kept_inv=vmem(full, PAIR, dtype=F4),
            kept_d2=vmem(full, width),
            kept_d3=vmem(full, width),
            first=vmem(full, width),
            da=vmem(full, width),
            grad=vmem(width, 4 * width + extra),
            sems=pltpu.SemaphoreType.DMA((7,)),
        ),
        grid=(pairs + tiles,),
        after=after,
    )


def self_back(att, dctx, tri, mg):
    full, width = att.value.shape

    def body(n):
        attend_pair_back(True, n.qa, n.ka, n.value, n.ctx, n.dctx, n.tri, n.dq, n.dk, n.dv)
        n.mg[...] = n.mg_in[...]

    both = pl.BlockSpec((2, full, PAIR), lambda p: (p, 0, 0))
    cols = pl.BlockSpec((full, PAIR), lambda p: (0, p))
    made = (struct((full, width)), cols)
    part = pl.BlockSpec((full // (width // PAIR), width), lambda p: (p, 0))
    return call(
        body,
        "self_back",
        dict(
            mg_in=(mg, part),
            qa=(att.qa, both),
            ka=(att.ka, both),
            value=(att.value, cols),
            ctx=(att.ctx, cols),
            dctx=(dctx, cols),
            tri=(tri, pl.BlockSpec((TILE, TILE), lambda p: (0, 0))),
        ),
        dict(dq=made, dk=made, dv=made, mg=(struct((full, width)), part)),
        {},
        grid=(width // PAIR,),
    )


def self_grads(place, x, parts, d, d13, fast, after):
    full, width = x.shape

    def body(n):
        me = n.place[0]
        start_weight(n.w, n.parts, 0, me, n.sems.at[0])
        late = [
            pltpu.make_async_copy(src, dst, n.sems.at[k + 2])
            for k, (src, dst) in enumerate([(n.dk, n.late_dk), (n.dv, n.late_dv), (n.d13, n.late_d13)])
        ]
        for copy in late:
            copy.start()
        put(n.grad, tm(n.x[...], n.dq[...]), 0)
        late[0].wait()
        put(n.grad, tm(n.x[...], n.late_dk[...]), width)
        late[1].wait()
        put(n.grad, tm(n.x[...], n.late_dv[...]), 2 * width)
        start_grad(n.grad, n.grads, me, n.sems.at[1])
        wait_all(n.w, n.sems.at[0])
        late[2].wait()
        for i in range(0, full, TILE):
            rows = slice(i, i + TILE)
            back = n.late_d13[rows].astype(F4)
            for c, d in enumerate((n.dq, n.late_dk, n.late_dv)):
                back = back + mt(d[rows], n.w[:, c * width : (c + 1) * width])
            n.ig[rows] = back.astype(BF)
        wait_all(n.grad, n.sems.at[1])

    return call(
        body,
        "self_grads",
        dict(
            place=(place, SMEM),
            x=(x, WHOLE),
            parts=(parts, ANY),
            dq=(d.dq, WHOLE),
            dk=(d.dk, ANY),
            dv=(d.dv, ANY),
            d13=(d13, ANY),
        ),
        dict(ig=(struct((full, width)), WHOLE), grads=(grad_shapes(width, 3 * width, fast), ANY)),
        dict(
            w=vmem(width, 3 * width),
            grad=vmem(width, 3 * width),
            late_dk=vmem(full, width),
            late_dv=vmem(full, width),
            late_d13=vmem(full, width),
            sems=pltpu.SemaphoreType.DMA((5,)),
        ),
        after=after,
    )


def total(groups, pieces, steps=1, after=()):
    rows = groups[0][0].shape[0]
    span = rows // pieces // steps
    widths = [group[0].shape[1] for group in groups]

    def body(n):
        left, at = 0, 0
        for group, columns in zip(groups, widths):
            for k, out in enumerate(n.outs):
                value = n.parts[at + k][...].astype(F4)
                for m in range(1, len(group)):
                    value = value + n.parts[at + m * pieces + k][...].astype(F4)
                out[:, left : left + columns] = value.astype(BF)
            left += columns
            at += len(group) * pieces

    def piece(k, columns):
        return pl.BlockSpec((span, columns), lambda i: (k * steps + i, 0))

    parts, specs = [], []
    for group, columns in zip(groups, widths):
        for array in group:
            for k in range(pieces):
                parts.append(array)
                specs.append(piece(k, columns))
    outs = [struct((rows // pieces, sum(widths)))] * pieces
    return call(
        body, "total", dict(parts=(parts, specs)), dict(outs=(outs, piece(0, sum(widths)))), {}, (steps,), after
    ).outs


def finish(arrays, cuts):
    rows = arrays[0].shape[0]

    def body(n):
        value = n.arrays[0][...].astype(F4)
        for array in n.arrays[1:]:
            value = value + array[...].astype(F4)
        for out, (low, high, *more) in zip(n.outs, cuts):
            if len(more) == 1:
                for k in range((high - low) // more[0]):
                    out[k * rows : (k + 1) * rows] = value[:, low + k * more[0] : low + (k + 1) * more[0]]
            elif more:
                out[...] = value[more[0] : more[1], low:high]
            else:
                out[...] = value[:, low:high]

    outs = []
    for low, high, *more in cuts:
        if len(more) == 1:
            outs.append(struct(((high - low) // more[0] * rows, more[0]), F4))
        else:
            outs.append(struct((more[1] - more[0] if more else rows, high - low), F4))
    return call(body, "total", dict(arrays=(arrays, WHOLE)), dict(outs=(outs, WHOLE)), {}).outs


def to_rows(array):
    seats = lax.axis_size("seq")
    blocks = array.reshape(seats, -1, array.shape[-1])
    return lax.all_to_all(blocks, "seq", split_axis=0, concat_axis=0, tiled=True)


def pack_front(weights, gains, shifts, bias):
    rows = weights[0].shape[0]

    def body(n):
        at = 0
        for weight in n.weights:
            n.out[:, at : at + weight.shape[1]] = weight[...]
            at += weight.shape[1]
        block = jnp.zeros((rows, PAIR), F4)
        row = lax.broadcasted_iota(jnp.int32, (rows, PAIR), 0)
        for k, (source, line) in enumerate([(n.gains, k) for k in range(3)] + [(n.shifts, k) for k in range(4)]):
            piece = source[line : line + 1].astype(F4)
            piece = jnp.concatenate([piece, jnp.zeros((1, PAIR - piece.shape[1]), F4)], axis=1)
            block = jnp.where(row == k, piece, block)
        piece = n.bias[...].astype(F4)
        piece = jnp.concatenate([piece, jnp.zeros((1, PAIR - piece.shape[1]), F4)], axis=1)
        n.out[:, at:] = jnp.where(row == 7, piece, block).astype(BF)

    columns = sum(weight.shape[1] for weight in weights) + PAIR
    return call(
        body,
        "pack",
        dict(weights=(weights, WHOLE), gains=(gains, WHOLE), shifts=(shifts, WHOLE), bias=(bias, WHOLE)),
        dict(out=(struct((rows, columns)), WHOLE)),
        {},
    ).out


def held(array, after=()):
    def kernel(*refs):
        pass

    others = LAST + list(after)
    result = pl.pallas_call(
        kernel,
        name="held",
        in_specs=[ANY] * (1 + len(others)),
        out_specs=ANY,
        out_shape=struct(array.shape, array.dtype),
        input_output_aliases={0: 0},
        cost_estimate=pl.CostEstimate(flops=1000000, bytes_accessed=0, transcendentals=0),
    )(array, *others)
    LAST[:] = [result]
    return result


def pack_ffn(up, down):
    rows, hidden = up.shape
    width = down.shape[1]

    def body(n):
        n.out[:, :hidden] = n.up[...]
        for k in range(down.shape[0] // rows):
            n.out[:, hidden + k * width : hidden + (k + 1) * width] = n.down[k * rows : (k + 1) * rows]

    out = struct((rows, hidden + down.shape[0] // rows * width))
    return call(body, "pack", dict(up=(up, WHOLE), down=(down, WHOLE)), dict(out=(out, WHOLE)), {}).out


def swap(value, bits):
    return lax.ppermute(value, AXES, [(i, i ^ bits) for i in range(FAST)])


def swap_all(value):
    groups = [list(range(core, FAST, 2)) for core in range(2)]
    return lax.all_to_all(value, AXES, split_axis=0, concat_axis=0, tiled=True, axis_index_groups=groups)


def join(arrays, axis, cuts=(), after=()):
    arrays = list(arrays)
    rows = sum(x.shape[0] for x in arrays) if axis == 0 else arrays[0].shape[0]
    columns = arrays[0].shape[1] if axis == 0 else sum(x.shape[1] for x in arrays)
    edges = [0, *cuts, columns]

    def body(n):
        at = 0
        for x in n.arrays:
            if axis == 1:
                n.outs[0][:, at : at + x.shape[1]] = x[...]
            else:
                for out, low, high in zip(n.outs, edges[:-1], edges[1:]):
                    out[at : at + x.shape[0]] = x[:, low:high]
            at += x.shape[axis]

    outs = [struct((rows, high - low)) for low, high in zip(edges[:-1], edges[1:])]
    return call(body, "join", dict(arrays=(arrays, WHOLE)), dict(outs=(outs, WHOLE)), {}, after=after).outs


def swap_plane(held):
    return [held] + [swap(held, bits) for bits in (2, 4, 6)]


def swap_line(held):
    return [held] + [swap(held, z << 3) for z in (1, 2, 3)]


def swap_cores(parts):
    return parts + [swap(part, 1) for part in parts]


def spread_plane(pieces):
    return [pieces[0]] + [swap(piece, bits) for piece, bits in zip(pieces[1:], (2, 4, 6))]


def spread_line(pieces):
    return [pieces[0]] + [swap(piece, z << 3) for z, piece in enumerate(pieces[1:], 1)]


def on_device(
    inputs,
    memory,
    seg_ids,
    mem_lengths,
    cotangent,
    qkv_weight,
    self_out_weight,
    cross_q_weight,
    cross_kv_weight,
    cross_out_weight,
    ffn_in_weight,
    ffn_in_bias,
    ffn_out_weight,
    norm_gains,
    shift_vectors,
):
    seats = lax.axis_size("seq")
    devices = lax.axis_size("dp") * seats
    span, width = inputs.shape[1:]
    hidden = ffn_in_weight.shape[1]
    full = seats * span
    seat = lax.axis_index("seq")
    me = lax.axis_index("dp") * seats + seat
    LAST.clear()
    rows, piece, bias_piece = qkv_weight.shape[0], norm_gains.shape[1], ffn_in_bias.shape[0]
    fast = devices == FAST and rows == 16 and hidden == 4 * width
    place = me.astype(jnp.int32).reshape(1)
    second_group = [self_out_weight, cross_q_weight, cross_kv_weight, cross_out_weight]
    if fast:
        front = pack_front([qkv_weight, *second_group], norm_gains, shift_vectors, ffn_in_bias[None])
        front = swap_line(front)
        ffn_parts = [lax.all_gather(pack_ffn(ffn_in_weight, ffn_out_weight), AXES, axis=0, tiled=False)]
        x = to_rows(inputs).reshape(full, width)
        one, two = join(front, 0, (3 * width,))
        (one,) = join(swap_plane(one), 0, (), [x])
        qkv_parts = [one, swap(one, 1)]
        two = swap_plane(two)
        vec, bias = None, None
    else:
        x = to_rows(inputs).reshape(full, width)
        qkv_parts = [lax.all_gather(qkv_weight, AXES, axis=0, tiled=True)]
        two_parts = [lax.all_gather(jnp.concatenate(second_group, axis=1), AXES, axis=0, tiled=True)]
        ffn_parts = [lax.all_gather(w, AXES, axis=0, tiled=True) for w in (ffn_in_weight, ffn_out_weight)]
        vec = lax.all_gather(jnp.concatenate([norm_gains, shift_vectors], axis=0), AXES, axis=1, tiled=True)
        vec = jnp.pad(vec.astype(F4), ((0, 1), (0, 0)))
        bias = lax.all_gather(ffn_in_bias, AXES, axis=0, tiled=True).astype(F4)[None]
    mem = to_rows(memory).reshape(full, width)
    cot = to_rows(cotangent).reshape(full, width)

    segments = lax.dynamic_index_in_dim(seg_ids, seat, 0, keepdims=False)
    ends = jnp.cumsum(lax.dynamic_index_in_dim(mem_lengths, seat, 0, keepdims=False))
    places = jnp.arange(full, dtype=jnp.int32)
    mem_segments = jnp.sum((places[:, None] >= ends[None, :]).astype(jnp.int32), axis=1)
    lane = jnp.arange(PAIR, dtype=jnp.int32)
    half = jnp.arange(2, dtype=jnp.int32)[:, None, None]
    free = (lane // HEAD)[None, None] == 1 - half
    number = (lane % HEAD)[None, None]

    def key_side(ids):
        away = jnp.where(ids[None, :, None] == number, 0.0, AWAY)
        ones = jnp.where(number < 11, 1.0, 0.0)
        return jnp.where(free, jnp.where(number < 8, away, ones), 0.0).astype(BF)

    augq = jnp.where(free & (number < 8) & (segments[None, :, None] == number), 1.0, 0.0).astype(BF)
    augk, augm = key_side(segments), key_side(mem_segments)
    corner = jnp.arange(TILE, dtype=jnp.int32)
    tri = jnp.where(corner[None, :] <= corner[:, None], 0.0, AWAY).astype(F4)

    a = self_forward(place, x, qkv_parts, augq, augk, tri)
    if fast:
        (two,) = join(two, 0, (), [mem])
        two_parts = [two, swap(two, 1)]
    c = cross_forward(place, x, mem, two_parts, a.ctx, vec, bias, augq, augm, hidden, fast)
    vec, bias = c.vec, c.bias
    m = middle(place, x, cot, two_parts, ffn_parts, c.cctx, c.xhat, vec, bias, fast)
    output = to_rows(m.out)

    if fast:
        big = lax.psum_scatter(m.grads[0], AXES, scatter_dimension=0, tiled=True)
    g = cross_back(
        place, mem, two_parts, c, m.dcctx, tri, a.ctx, m.d2, m.d3, vec, m.vec_sum, m.bias_rows, fast, []
    )
    two_sum = []
    if fast:
        two_sum = spread_plane(total([[g.grads[0], swap(held(g.grads[1], [output]), 1)]], 4))
    d = self_back(a, g.dctx, tri, g.mg)
    memory_grad = to_rows(d.mg)
    s = self_grads(place, x, qkv_parts, d, g.d13, fast, two_sum[1:])
    if fast:
        qkv_sum = spread_plane(total([[s.grads[0], swap(s.grads[1], 1)]], 4))
    if fast:
        line = spread_line(total([qkv_sum, two_sum], 4, 1, [memory_grad]))
    input_grad = to_rows(held(s.ig))
    memory_grad = memory_grad.astype(F4)
    if fast:
        up_sum, co_sum, down_sum = finish(
            [big], ((0, hidden), (hidden, hidden + width), (hidden + width, 2 * hidden + width, width))
        )
        at = 7 * width
        qkv_sum, so_sum, cq_sum, ckv_sum, gains_sum, shifts_sum, bias_sum = finish(
            line,
            (
                (0, 3 * width),
                (3 * width, 4 * width),
                (4 * width, 5 * width),
                (5 * width, at),
                (at, at + piece, 0, 3),
                (at, at + piece, 3, 7),
                (at, at + bias_piece, 8, 9),
            ),
        )
    else:

        def scatter(value, dim=0):
            return lax.psum_scatter(value.astype(F4), AXES, scatter_dimension=dim, tiled=True)

        upco_sum, down_sum, two_sum, qkv_sum = [scatter(v) for v in (*m.grads, *g.grads, *s.grads)]
        up_sum, co_sum = upco_sum[:, :hidden], upco_sum[:, hidden:]
        so_sum, cq_sum, ckv_sum = two_sum[:, :width], two_sum[:, width : 2 * width], two_sum[:, 2 * width :]
        vec_sum, bias_sum = scatter(g.vec_sum[:7], 1), scatter(m.bias_sum[0])
        gains_sum, shifts_sum = vec_sum[:3], vec_sum[3:]
    return (
        output,
        input_grad.astype(F4),
        memory_grad,
        qkv_sum,
        so_sum,
        cq_sum,
        ckv_sum,
        co_sum,
        up_sum,
        bias_sum.reshape(-1),
        down_sum,
        gains_sum,
        shifts_sum,
    )


def solution(mesh):
    rows = P("dp", "seq", None)
    weight = P(AXES, None)
    vector = P(None, AXES)
    return jax.shard_map(
        on_device,
        mesh=mesh,
        in_specs=(rows, rows, P("dp", None), P("dp", None), rows)
        + (weight,) * 6
        + (P(AXES), weight, vector, vector),
        out_specs=(rows,) * 3 + (weight,) * 6 + (P(AXES), weight, vector, vector),
        check_vma=False,
    )
```

```python
import types

import jax
import jax.numpy as jnp
from jax import lax
from jax.experimental import pallas as pl
from jax.experimental.pallas import tpu as pltpu
from jax.sharding import PartitionSpec as P

HEAD = 64
PAIR = 2 * HEAD
TILE = 256
FAST = 32
HALF = FAST // 2
AXES = ("dp", "seq")
LOG2E = 1.4426950408889634
AWAY = -1e30
GELU_A = 0.7978845608028654
GELU_B = 0.044715
BF = jnp.bfloat16
F4 = jnp.float32
VMEM_BYTES = 58 << 20


def mm(a, b):
    return lax.dot_general(a, b, (((1,), (0,)), ((), ())), preferred_element_type=F4)


def mt(a, b):
    return lax.dot_general(a, b, (((1,), (1,)), ((), ())), preferred_element_type=F4)


def tm(a, b):
    return lax.dot_general(a, b, (((0,), (0,)), ((), ())), preferred_element_type=F4)


def struct(shape, dtype=BF):
    return jax.ShapeDtypeStruct(tuple(shape), dtype)


ANY = pl.BlockSpec(memory_space=pl.ANY)
HBM = pl.BlockSpec(memory_space=pltpu.HBM)
WHOLE = pl.BlockSpec(memory_space=pltpu.VMEM)
SMEM = pl.BlockSpec(memory_space=pltpu.SMEM)


def aslist(value):
    return list(value) if isinstance(value, (list, tuple)) else [value]


LAST = []
COST = dict(
    self_forward=16,
    cross_forward=22,
    middle=31,
    cross_back=34,
    self_back=8,
    self_grads=0.2,
    total=2,
)
SCALE = 1.0
SUBS = 2
SKEW = 1


def call(body, name, ins, outs, scratch, grid=(), after=()):
    us = COST.get(name, 1.5)
    ins = dict(ins, after=(LAST + list(after), HBM))
    layout = [(key, len(aslist(value)), isinstance(value, (list, tuple))) for key, (value, _) in ins.items()]
    layout += [(key, len(aslist(value)), isinstance(value, (list, tuple))) for key, (value, _) in outs.items()]
    layout += [(key, 1, False) for key in scratch]

    def kernel(*refs):
        held, at = {}, 0
        for key, count, many in layout:
            held[key] = list(refs[at : at + count]) if many else refs[at]
            at += count
        body(types.SimpleNamespace(**held))

    arrays = [x for value, _ in ins.values() for x in aslist(value)]
    in_specs = []
    for value, spec in ins.values():
        in_specs += spec if isinstance(spec, list) else [spec] * len(aslist(value))
    out_specs = [spec for value, spec in outs.values() for _ in aslist(value)]
    out_shape = [x for value, _ in outs.values() for x in aslist(value)]
    result = pl.pallas_call(
        kernel,
        name=name,
        grid=grid,
        in_specs=in_specs,
        out_specs=out_specs,
        out_shape=out_shape,
        scratch_shapes=list(scratch.values()),
        compiler_params=pltpu.CompilerParams(vmem_limit_bytes=VMEM_BYTES),
        cost_estimate=pl.CostEstimate(flops=int(us * SCALE * 1.1e9), bytes_accessed=0, transcendentals=0),
    )(*arrays)
    LAST[:] = [result[-1]]
    found, at = {}, 0
    for key, (value, _) in outs.items():
        count = len(aslist(value))
        found[key] = list(result[at : at + count]) if isinstance(value, (list, tuple)) else result[at]
        at += count
    return types.SimpleNamespace(**found)


def vmem(*shape, dtype=BF):
    return pltpu.VMEM(shape, dtype)


ORDER = [((p % 4) << 3) | ((p // 4 % 4) << 1) | (p // HALF) for p in range(FAST)]


def wait_all(buffer, sem):
    pltpu.make_async_copy(buffer, buffer, sem).wait()


def start_weight(dst, parts, first, me, sem):
    columns = dst.shape[-1]
    if len(parts) == 1:
        pltpu.make_async_copy(parts[0].at[:, pl.ds(first, columns)], dst, sem).start()
    else:
        span = dst.shape[0] // FAST
        each = FAST // len(parts)
        for p in range(FAST):
            place = pl.multiple_of((me ^ ORDER[p]) * span, span)
            src = parts[p // each].at[pl.ds((p % each) * span, span), pl.ds(first, columns)]
            pltpu.make_async_copy(src, dst.at[pl.ds(place, span)], sem).start()


def start_grad(src, parts, me, sem):
    if len(parts) == 1:
        pltpu.make_async_copy(src, parts[0], sem).start()
        return
    span = src.shape[0] // FAST
    for p in range(FAST):
        place = pl.multiple_of((me ^ ORDER[p]) * span, span)
        dst = parts[p // HALF].at[pl.ds((p % HALF) * span, span)]
        pltpu.make_async_copy(src.at[pl.ds(place, span)], dst, sem).start()


def grad_shapes(rows, columns, fast):
    return [struct((rows // 2, columns))] * 2 if fast else [struct((rows, columns))]


def take(ref, first=0, columns=None):
    columns = ref.shape[-1] - first if columns is None else columns
    return ref[..., first : first + columns].reshape(-1, columns)


def put(ref, value, first):
    ref[:, first : first + value.shape[1]] = value.astype(BF)


def norm(values):
    centered = values - jnp.mean(values, axis=-1, keepdims=True)
    inverse = lax.rsqrt(jnp.mean(centered * centered, axis=-1, keepdims=True) + 1e-05)
    return centered * inverse, inverse


def norm_back(upstream, normed, inverse, gain_row):
    gain_part = jnp.sum(upstream * normed, axis=0, keepdims=True)
    shift_part = jnp.sum(upstream, axis=0, keepdims=True)
    scaled = upstream * gain_row
    centered = scaled - jnp.mean(scaled, axis=-1, keepdims=True)
    value = inverse * (centered - normed * jnp.mean(scaled * normed, axis=-1, keepdims=True))
    return value, gain_part, shift_part


def lane_masks(dtype):
    lane = lax.broadcasted_iota(jnp.int32, (1, PAIR), 1)
    own = [(lane // HEAD == h).astype(dtype) for h in range(2)]

    def spot(h, k):
        return ((lane // HEAD == 1 - h) & (lane % HEAD == k)).astype(dtype)

    return own, spot


def attend_pair(causal, query, key, value, augq, augk, tri, ctx_out, qa_out, ka_out):
    total = key.shape[0]
    own, spot = lane_masks(F4)
    lane = lax.broadcasted_iota(jnp.int32, (TILE, PAIR), 1) % HEAD
    own_low = [mask.astype(BF) for mask in own]
    eighth = [(mask * HEAD ** (-0.5)).astype(BF) for mask in own]
    wide = jnp.concatenate([value, jnp.ones((total, PAIR), BF)], axis=1)
    keys = []
    for h in range(2):
        keys.append(key * own_low[h] + augk[h])
        ka_out[h] = keys[h]
    units = [(i, h) for i in range(query.shape[0] // TILE) for h in range(2)]
    scores, probs, halves = {}, {}, {}

    def score(i, h):
        rows = slice(i * TILE, (i + 1) * TILE)
        width = (i + 1) * TILE if causal else total
        head = query[rows] * eighth[h] + augq[h, rows]
        s = mt(head, keys[h][:width])
        if causal:
            tail = s[:, width - TILE :] + tri[...]
            s = jnp.concatenate([s[:, : width - TILE], tail], axis=1) if i else tail
        return s, head

    def finish(i, h, low, top, head):
        rows = slice(i * TILE, (i + 1) * TILE)
        both = mm(low, wide[: low.shape[1]])
        sums = both[:, PAIR:]
        halves[h] = both[:, :PAIR] / sums
        rest = -(top + jnp.log(sums))
        high = rest.astype(BF).astype(F4)
        rest = rest - high
        middle = rest.astype(BF).astype(F4)
        extra = jnp.where(lane == 8, high, jnp.where(lane == 9, middle, rest - middle))
        qa_out[h, rows] = head + (extra * (spot(h, 8) + spot(h, 9) + spot(h, 10))).astype(BF)
        if h == 1:
            ctx_out[rows] = (halves[0] * own[0] + halves[1] * own[1]).astype(BF)

    count = len(units)
    for t in range(count + 2):
        if t < count:
            scores[t] = score(*units[t])
        if 0 <= t - 2 < count:
            finish(*units[t - 2], *probs.pop(t - 2))
        if 0 <= t - 1 < count:
            s, head = scores.pop(t - 1)
            top = jnp.max(s, axis=1, keepdims=True)
            low = jnp.exp2(s * LOG2E - top * LOG2E).astype(BF)
            probs[t - 1] = (low, top, head)


def self_forward(place, x, parts, augq, augk, tri):
    full, width = x.shape
    heads = width // HEAD

    def body(n):
        pair = pl.program_id(0)

        @pl.when(pair == 0)
        def _():
            start_weight(n.w, n.parts, 0, n.place[0], n.sem)
            wait_all(n.w, n.sem)
            for c in range(0, 3 * width, 512):
                n.qkv[:, c : c + 512] = mm(n.x[...], take(n.w, c, 512)).astype(BF)

        def columns(part):
            return n.qkv[:, pl.ds(pl.multiple_of(part * width + pair * PAIR, PAIR), PAIR)]

        value = columns(2)
        n.value[...] = value
        attend_pair(True, columns(0), columns(1), value, n.augq, n.augk, n.tri, n.ctx, n.qa, n.ka)

    both = pl.BlockSpec((2, full, PAIR), lambda p: (p, 0, 0))
    fixed = pl.BlockSpec((2, full, PAIR), lambda p: (0, 0, 0))
    cols = pl.BlockSpec((full, PAIR), lambda p: (0, p))
    return call(
        body,
        "self_forward",
        dict(
            place=(place, SMEM),
            x=(x, pl.BlockSpec((full, width), lambda p: (0, 0))),
            parts=(parts, HBM),
            augq=(augq, fixed),
            augk=(augk, fixed),
            tri=(tri, pl.BlockSpec((TILE, TILE), lambda p: (0, 0))),
        ),
        dict(
            ctx=(struct((full, width)), cols),
            qa=(struct((heads, full, PAIR)), both),
            ka=(struct((heads, full, PAIR)), both),
            value=(struct((full, width)), cols),
        ),
        dict(
            w=vmem(width, 3 * width),
            qkv=vmem(full, 3 * width),
            sem=pltpu.SemaphoreType.DMA,
        ),
        grid=(heads // 2,),
    )


def unfold_vectors(blocks, vec, bias):
    width, hidden = vec.shape[1], bias.shape[1]
    piece, part = width // FAST, hidden // FAST
    lane = lax.broadcasted_iota(jnp.int32, (PAIR, width), 0)
    col = lax.broadcasted_iota(jnp.int32, (PAIR, width), 1)
    wide = mm(blocks, (lane == col % piece).astype(BF))
    row = lax.broadcasted_iota(jnp.int32, (width, width), 0)
    col = lax.broadcasted_iota(jnp.int32, (width, width), 1)
    wide = jnp.where(row // 16 == col // piece, wide, 0.0).astype(BF)
    line = lax.broadcasted_iota(jnp.int32, (8, width), 0)
    vec[...] = mm((line == lax.broadcasted_iota(jnp.int32, (8, width), 1) % 16).astype(BF), wide)
    owner = lax.broadcasted_iota(jnp.int32, (FAST, width), 0) * 16 + 7
    rows = mm((owner == lax.broadcasted_iota(jnp.int32, (FAST, width), 1)).astype(BF), blocks)
    for j in range(FAST):
        bias[:, j * part : (j + 1) * part] = rows[j : j + 1, :part]


def cross_forward(place, x, mem, parts, ctx, vec, bias, augq, augk, hidden, fast):
    full, width = x.shape
    heads = width // HEAD

    def body(n):
        pair = pl.program_id(0)

        @pl.when(pair == 0)
        def _():
            me = n.place[0]
            start_weight(n.w, n.parts, 0, me, n.sems.at[0])
            x_copy = pltpu.make_async_copy(n.x, n.x_kept, n.sems.at[2])
            mem_copy = pltpu.make_async_copy(n.mem, n.mem_kept, n.sems.at[3])
            x_copy.start()
            mem_copy.start()
            if fast:
                start_weight(n.blocks, n.parts, 4 * width, me, n.sems.at[1])
                wait_all(n.blocks, n.sems.at[1])
                unfold_vectors(n.blocks[...], n.vec, n.bias)
            else:
                n.vec[...] = n.vec_in[0][...]
                n.bias[...] = n.bias_in[0][...]
            wait_all(n.w, n.sems.at[0])
            x_copy.wait()
            for i in range(0, full, TILE):
                rows = slice(i, i + TILE)
                attn = mm(n.ctx[rows], n.w[:, :width])
                normed, inverse = norm(n.x_kept[rows].astype(F4) + attn)
                n.xhat[rows] = normed.astype(BF)
                n.inv[rows] = jnp.broadcast_to(inverse, (TILE, PAIR))
                first = (normed * n.vec[0:1] + n.vec[3:4]).astype(BF)
                n.q[rows] = mm(first, n.w[:, width : 2 * width]).astype(BF)
            mem_copy.wait()
            for c in range(0, 2 * width, 512):
                n.kv[:, c : c + 512] = mm(n.mem_kept[...], n.w[:, 2 * width + c : 2 * width + c + 512]).astype(BF)

        lanes = pl.ds(pl.multiple_of(pair * PAIR, PAIR), PAIR)
        late = pl.ds(pl.multiple_of(width + pair * PAIR, PAIR), PAIR)
        value = n.kv[:, late]
        n.value[...] = value
        attend_pair(False, n.q[:, lanes], n.kv[:, lanes], value, n.augq, n.augk, None, n.cctx, n.qa, n.ka)

    both = pl.BlockSpec((2, full, PAIR), lambda p: (p, 0, 0))
    fixed = pl.BlockSpec((2, full, PAIR), lambda p: (0, 0, 0))
    cols = pl.BlockSpec((full, PAIR), lambda p: (0, p))

    def still(shape):
        return pl.BlockSpec(shape, lambda p: (0, 0))

    return call(
        body,
        "cross_forward",
        dict(
            place=(place, SMEM),
            x=(x, HBM),
            mem=(mem, HBM),
            parts=(parts, HBM),
            ctx=(ctx, still((full, width))),
            vec_in=([] if fast else [vec], still((8, width))),
            bias_in=([] if fast else [bias], still((1, hidden))),
            augq=(augq, fixed),
            augk=(augk, fixed),
        ),
        dict(
            cctx=(struct((full, width)), cols),
            qa=(struct((heads, full, PAIR)), both),
            ka=(struct((heads, full, PAIR)), both),
            value=(struct((full, width)), cols),
            xhat=(struct((full, width)), still((full, width))),
            inv=(struct((full, PAIR), F4), still((full, PAIR))),
            vec=(struct((8, width), F4), still((8, width))),
            bias=(struct((1, hidden), F4), still((1, hidden))),
        ),
        dict(
            w=vmem(width, 4 * width),
            q=vmem(full, width),
            kv=vmem(full, 2 * width),
            blocks=vmem(width, PAIR),
            x_kept=vmem(full, width),
            mem_kept=vmem(full, width),
            sems=pltpu.SemaphoreType.DMA((4,)),
        ),
        grid=(heads // 2,),
    )


def middle(place, x, cot, co_parts, ffn_parts, cctx, xhat, vec, bias, fast):
    full, width = x.shape
    hidden = bias.shape[1]
    fold = hidden // width
    late = hidden + width
    block = SUBS * TILE

    def body(n):
        me = n.place[0]
        step = pl.program_id(0)

        @pl.when(step == 0)
        def _():
            if fast:
                whole = n.ffn_parts[0]
                pltpu.make_async_copy(whole.at[:, :, pl.ds(2 * hidden, width)], n.co, n.sems.at[0]).start()
                pltpu.make_async_copy(whole.at[:, :, pl.ds(0, hidden)], n.up, n.sems.at[1]).start()
                for k in range(fold):
                    src = whole.at[:, :, pl.ds(hidden + k * width, width)]
                    pltpu.make_async_copy(src, n.down.at[:, k], n.sems.at[2]).start()
            else:
                start_weight(n.co, n.co_parts, 4 * width, me, n.sems.at[0])
                start_weight(n.up, n.ffn_parts[:1], 0, me, n.sems.at[1])
                start_weight(n.down, n.ffn_parts[1:], 0, me, n.sems.at[2])
            pltpu.make_async_copy(n.x, n.x_kept, n.sems.at[3]).start()
            pltpu.make_async_copy(n.cot, n.cot_kept, n.sems.at[4]).start()
            n.vec_sum[...] = jnp.zeros(n.vec_sum.shape, F4)
            n.bias_sum[...] = jnp.zeros(n.bias_sum.shape, F4)
            wait_all(n.co, n.sems.at[0])
            wait_all(n.up, n.sems.at[1])
            wait_all(n.down, n.sems.at[2])
            wait_all(n.x_kept, n.sems.at[3])
            wait_all(n.cot_kept, n.sems.at[4])

        vec = n.vec

        def tile_steps(k):
            rows = slice(k * TILE, (k + 1) * TILE)
            kept = pl.ds(pl.multiple_of(step * block + k * TILE, TILE), TILE)
            v = types.SimpleNamespace()

            def enter():
                context = n.cctx[rows]
                n.context[kept] = context
                v.first = n.xhat[rows].astype(F4) * vec[0:1] + vec[3:4] + mm(context, take(n.co))

            def norm_one():
                v.normed_one, v.inverse_one = norm(v.first)
                v.second = v.normed_one * vec[1:2] + vec[4:5]
                v.low = v.second.astype(BF)
                n.second[kept] = v.low

            def rise():
                v.pre = mm(v.low, take(n.up)) + n.bias[...]

            def gelu():
                pre = v.pre
                slope = GELU_A * GELU_B * (pre * pre) + GELU_A
                t = jnp.tanh(pre * slope)
                half = 0.5 * t + 0.5
                v.hid = (pre * half).astype(BF)
                n.hid[kept] = v.hid
                v.d_gelu = half + (0.5 - 0.5 * t * t) * pre * (3.0 * slope - 2.0 * GELU_A)

            def fall():
                v.ffn = mm(v.hid, take(n.down)) + vec[6:7]

            def norm_two():
                normed, inverse = norm(v.second + v.ffn + n.x_kept[kept].astype(F4))
                n.out[rows] = (normed * vec[2:3] + vec[5:6]).astype(BF)
                v.d_three, gain, shift = norm_back(n.cot_kept[kept].astype(F4), normed, inverse, vec[2:3])
                v.df = v.d_three.astype(BF)
                n.d3[rows] = v.df
                n.df[kept] = v.df
                n.vec_sum[2:3] += gain
                n.vec_sum[5:6] += shift
                n.vec_sum[6:7] += jnp.sum(v.d_three, axis=0, keepdims=True)

            def back_down():
                v.d_hid = mt(v.df, take(n.down))

            def back_gelu():
                d_pre = v.d_hid * v.d_gelu
                v.d_pre = d_pre.astype(BF)
                n.d_pre[kept] = v.d_pre
                n.bias_sum[...] += jnp.sum(d_pre, axis=0, keepdims=True)

            def back_up():
                v.d_second = v.d_three + mt(v.d_pre, take(n.up))

            def norm_one_back():
                d_two, gain, shift = norm_back(v.d_second, v.normed_one, v.inverse_one, vec[1:2])
                v.dc = d_two.astype(BF)
                n.d2[rows] = v.dc
                n.dc[kept] = v.dc
                n.vec_sum[1:2] += gain
                n.vec_sum[4:5] += shift

            def leave():
                n.dcctx[rows] = mt(v.dc, take(n.co)).astype(BF)

            return [
                enter, norm_one, rise, gelu, fall, norm_two, back_down, back_gelu, back_up, norm_one_back, leave
            ]

        tiles = [tile_steps(k) for k in range(SUBS)]
        for t in range(len(tiles[0]) + SKEW * (SUBS - 1)):
            for k, steps in enumerate(tiles):
                if 0 <= t - SKEW * k < len(steps):
                    steps[t - SKEW * k]()

        @pl.when(step == full // block - 1)
        def _():
            for c in range(0, hidden, 512):
                part = tm(n.hid[:, c : c + 512], n.df[...]).astype(BF)
                if fast:
                    rows = width // FAST
                    part = part.reshape(512 // (fold * rows), fold, rows, width)
                    top = c // fold
                    for a in range(fold):
                        n.grad[top : top + 512 // fold, late + a * width : late + (a + 1) * width] = part[
                            :, a
                        ].reshape(512 // fold, width)
                else:
                    n.grad_down[c : c + 512] = part
            if fast:
                edge = pl.ds(late, fold * width)
                first = pltpu.make_async_copy(n.grad.at[:, edge], n.grads[0].at[:, edge], n.sems.at[0])
                edge = pl.ds(0, late)
                last = pltpu.make_async_copy(n.grad.at[:, edge], n.grads[0].at[:, edge], n.sems.at[1])
            else:
                first = pltpu.make_async_copy(n.grad_down, n.grads[1], n.sems.at[0])
                last = pltpu.make_async_copy(n.grad, n.grads[0], n.sems.at[1])
            first.start()
            for c in range(0, hidden, 512):
                n.grad[:, c : c + 512] = tm(n.second[...], n.d_pre[:, c : c + 512]).astype(BF)
            n.grad[:, hidden : hidden + width] = tm(n.context[...], n.dc[...]).astype(BF)
            last.start()
            share = hidden // n.bias_rows.shape[0]
            n.bias_rows[...] = jnp.zeros(n.bias_rows.shape, BF)
            for j in range(n.bias_rows.shape[0]):
                n.bias_rows[j : j + 1, :share] = n.bias_sum[:, j * share : (j + 1) * share].astype(BF)
            first.wait()
            last.wait()

    if fast:
        grads = [struct((width, late + fold * width))]
        scratch = dict(
            co=vmem(FAST, width // FAST, width),
            up=vmem(FAST, width // FAST, hidden),
            down=vmem(FAST, fold, width // FAST, width),
            grad=vmem(width, late + fold * width),
        )
    else:
        grads = [struct((width, late)), struct((hidden, width))]
        scratch = dict(
            co=vmem(width, width),
            up=vmem(width, hidden),
            down=vmem(hidden, width),
            grad=vmem(width, late),
            grad_down=vmem(hidden, width),
        )
    tile = pl.BlockSpec((block, width), lambda i: (i, 0))

    def still(shape):
        return pl.BlockSpec(shape, lambda i: (0, 0))

    return call(
        body,
        "middle",
        dict(
            place=(place, SMEM),
            x=(x, HBM),
            cot=(cot, HBM),
            co_parts=(co_parts, HBM),
            ffn_parts=(ffn_parts, HBM),
            cctx=(cctx, tile),
            xhat=(xhat, tile),
            vec=(vec, still(vec.shape)),
            bias=(bias, still(bias.shape)),
        ),
        dict(
            out=(struct((full, width)), tile),
            d3=(struct((full, width)), tile),
            d2=(struct((full, width)), tile),
            dcctx=(struct((full, width)), tile),
            vec_sum=(struct((8, width), F4), still((8, width))),
            bias_sum=(struct((1, hidden), F4), still((1, hidden))),
            bias_rows=(struct((FAST, PAIR)), still((FAST, PAIR))),
            grads=(grads, ANY),
        ),
        dict(
            scratch,
            context=vmem(full, width),
            second=vmem(full, width),
            hid=vmem(full, hidden),
            d_pre=vmem(full, hidden),
            df=vmem(full, width),
            dc=vmem(full, width),
            x_kept=vmem(full, width),
            cot_kept=vmem(full, width),
            sems=pltpu.SemaphoreType.DMA((5,)),
        ),
        grid=(full // block,),
    )


def attend_pair_back(causal, qa, ka, value, ctx, dctx, tri, dq, dk, dv):
    own, spot = lane_masks(F4)
    total = value.shape[0]
    blocks = total // TILE
    upstream = dctx[...].astype(F4)
    product = upstream * ctx[...].astype(F4)
    row = lax.broadcasted_iota(jnp.int32, (PAIR, PAIR), 0) // HEAD
    col = lax.broadcasted_iota(jnp.int32, (PAIR, PAIR), 1) // HEAD
    swap = jnp.where(row != col, -1.0, 0.0).astype(BF)
    high = product.astype(BF)
    delta = mm(high, swap) + mm((product - high.astype(F4)).astype(BF), swap)
    delta_high = delta.astype(BF).astype(F4)
    delta_low = delta - delta_high
    values = value[...].astype(F4)
    d_query, d_key, d_value = [], [], []
    for h in range(2):
        spots = spot(h, 0) + spot(h, 1)
        do = (upstream * own[h] + delta_high * spot(h, 0) + delta_low * spot(h, 1)).astype(BF)
        va = (values * own[h] + spots).astype(BF)
        query, key = qa[h], ka[h]
        query_t = query.T[h * HEAD : (h + 1) * HEAD]
        do_t = do.T[h * HEAD : (h + 1) * HEAD]
        keys, vals, sums = [], [], [None] * blocks
        for j in range(blocks):
            start = j * TILE if causal else 0
            key_j, va_j = key[j * TILE : (j + 1) * TILE], va[j * TILE : (j + 1) * TILE]
            s = mt(query[start:], key_j)
            if causal:
                head = s[:TILE] + tri[...]
                s = jnp.concatenate([head, s[TILE:]], axis=0) if j < blocks - 1 else head
            prob = jnp.exp2(s * LOG2E)
            ds = (prob * mt(do[start:], va_j)).astype(BF)
            vals.append(mm(do_t[:, start:], prob.astype(BF)))
            keys.append(mm(query_t[:, start:], ds))
            back = mm(ds, key_j)
            for i in range(start // TILE, blocks):
                part = back[i * TILE - start : (i + 1) * TILE - start]
                sums[i] = part if sums[i] is None else sums[i] + part
        d_query.append(jnp.concatenate(sums, axis=0))
        d_key.append(jnp.concatenate(keys, axis=1))
        d_value.append(jnp.concatenate(vals, axis=1))
    dq[...] = ((d_query[0] * own[0] + d_query[1] * own[1]) * HEAD ** (-0.5)).astype(BF)
    dk[...] = jnp.concatenate(d_key, axis=0).T.astype(BF)
    dv[...] = jnp.concatenate(d_value, axis=0).T.astype(BF)


def cross_back(place, mem, parts, att, dcctx, tri, ctx, d2, d3, vec, vec_mid, bias_mid, fast, after):
    full, width = mem.shape
    extra = PAIR if fast else 0
    pairs, tiles = width // PAIR, full // TILE

    def body(n):
        me = n.place[0]
        step = pl.program_id(0)
        vec = n.vec
        loads = [(n.ctx, n.kept_ctx), (n.mem, n.kept_mem), (n.xhat, n.kept_xhat), (n.inv, n.kept_inv)]
        loads += [(n.d2, n.kept_d2), (n.d3, n.kept_d3)]

        @pl.when(step == 0)
        def _():
            n.vec_sum[...] = n.vec_mid[...]
            start_weight(n.w, n.parts, 0, me, n.sems.at[0])
            for k, (src, dst) in enumerate(loads):
                pltpu.make_async_copy(src, dst, n.sems.at[k + 1]).start()

        @pl.when(step < pairs)
        def _():
            lanes = pl.ds(pl.multiple_of(jnp.minimum(step, pairs - 1) * PAIR, PAIR), PAIR)
            attend_pair_back(
                False,
                n.qa,
                n.ka,
                n.value,
                n.cctx,
                n.dcctx,
                n.tri,
                n.dq.at[:, lanes],
                n.dk.at[:, lanes],
                n.dv.at[:, lanes],
            )

        @pl.when(step == pairs)
        def _():
            wait_all(n.w, n.sems.at[0])
            for k, (src, dst) in enumerate(loads):
                pltpu.make_async_copy(src, dst, n.sems.at[k + 1]).wait()

        @pl.when(step >= pairs)
        def _():
            rows = pl.ds(pl.multiple_of(jnp.maximum(step - pairs, 0) * TILE, TILE), TILE)
            normed = n.kept_xhat[rows].astype(F4)
            n.first[rows] = (normed * vec[0:1] + vec[3:4]).astype(BF)
            d_first = n.kept_d2[rows].astype(F4) + mt(n.dq[rows], n.w[:, width : 2 * width])
            back = mt(n.dk[rows], n.w[:, 2 * width : 3 * width]) + mt(n.dv[rows], n.w[:, 3 * width :])
            n.mg[...] = back.astype(BF)
            inverse = jnp.concatenate([n.kept_inv[rows]] * (width // PAIR), axis=1)
            d_one, gain, shift = norm_back(d_first, normed, inverse, vec[0:1])
            n.d13[...] = (n.kept_d3[rows].astype(F4) + d_one).astype(BF)
            da = d_one.astype(BF)
            n.da[rows] = da
            n.dctx[...] = mt(da, n.w[:, :width]).astype(BF)
            n.vec_sum[0:1] += gain
            n.vec_sum[3:4] += shift

        @pl.when(step == pairs + tiles - 1)
        def _():
            put(n.grad, tm(n.kept_mem[...], n.dk[...]), 2 * width)
            put(n.grad, tm(n.kept_mem[...], n.dv[...]), 3 * width)
            put(n.grad, tm(n.kept_ctx[...], n.da[...]), 0)
            put(n.grad, tm(n.first[...], n.dq[...]), width)
            if fast:
                piece = width // FAST
                row = lax.broadcasted_iota(jnp.int32, (width, width), 0)
                col = lax.broadcasted_iota(jnp.int32, (width, width), 1)
                line = lax.broadcasted_iota(jnp.int32, (width, 8), 0) % piece
                pick_line = (line == lax.broadcasted_iota(jnp.int32, (width, 8), 1)).astype(BF)
                spread = mm(pick_line, n.vec_sum[...].astype(BF))
                spread = jnp.where(row // piece == col // piece, spread, 0.0).astype(BF)
                lane = lax.broadcasted_iota(jnp.int32, (width, PAIR), 1)
                fold = (lax.broadcasted_iota(jnp.int32, (width, PAIR), 0) % piece == lane).astype(BF)
                owner = lax.broadcasted_iota(jnp.int32, (width, FAST), 0)
                wanted = lax.broadcasted_iota(jnp.int32, (width, FAST), 1) * piece + 8
                put(n.grad, mm(spread, fold) + mm((owner == wanted).astype(BF), n.bias_mid[...]), 4 * width)
            start_grad(n.grad, n.grads, me, n.sems.at[0])
            wait_all(n.grad, n.sems.at[0])

    def pair(i):
        return jnp.minimum(i, pairs - 1)

    both = pl.BlockSpec((2, full, PAIR), lambda i: (pair(i), 0, 0))
    cols = pl.BlockSpec((full, PAIR), lambda i: (0, pair(i)))
    tile = pl.BlockSpec((TILE, width), lambda i: (jnp.maximum(i - pairs, 0), 0))

    def still(array):
        return (array, pl.BlockSpec(array.shape, lambda i: (0, 0)))

    return call(
        body,
        "cross_back",
        dict(
            place=(place, SMEM),
            qa=(att.qa, both),
            ka=(att.ka, both),
            value=(att.value, cols),
            cctx=(att.cctx, cols),
            dcctx=(dcctx, cols),
            tri=still(tri),
            parts=(parts, HBM),
            mem=(mem, HBM),
            ctx=(ctx, HBM),
            xhat=(att.xhat, HBM),
            inv=(att.inv, HBM),
            d2=(d2, HBM),
            d3=(d3, HBM),
            vec=still(vec),
            vec_mid=still(vec_mid),
            bias_mid=still(bias_mid),
        ),
        dict(
            mg=(struct((full, width)), tile),
            d13=(struct((full, width)), tile),
            dctx=(struct((full, width)), tile),
            vec_sum=still(struct((8, width), F4)),
            grads=(grad_shapes(width, 4 * width + extra, fast), ANY),
        ),
        dict(
            w=vmem(width, 4 * width),
            dq=vmem(full, width),
            dk=vmem(full, width),
            dv=vmem(full, width),
            kept_ctx=vmem(full, width),
            kept_mem=vmem(full, width),
            kept_xhat=vmem(full, width),
            kept_inv=vmem(full, PAIR, dtype=F4),
            kept_d2=vmem(full, width),
            kept_d3=vmem(full, width),
            first=vmem(full, width),
            da=vmem(full, width),
            grad=vmem(width, 4 * width + extra),
            sems=pltpu.SemaphoreType.DMA((7,)),
        ),
        grid=(pairs + tiles,),
        after=after,
    )


def self_back(att, dctx, tri):
    full, width = att.value.shape

    def body(n):
        attend_pair_back(True, n.qa, n.ka, n.value, n.ctx, n.dctx, n.tri, n.dq, n.dk, n.dv)

    both = pl.BlockSpec((2, full, PAIR), lambda p: (p, 0, 0))
    cols = pl.BlockSpec((full, PAIR), lambda p: (0, p))
    made = (struct((full, width)), cols)
    return call(
        body,
        "self_back",
        dict(

            qa=(att.qa, both),
            ka=(att.ka, both),
            value=(att.value, cols),
            ctx=(att.ctx, cols),
            dctx=(dctx, cols),
            tri=(tri, pl.BlockSpec((TILE, TILE), lambda p: (0, 0))),
        ),
        dict(dq=made, dk=made, dv=made),
        {},
        grid=(width // PAIR,),
    )


def self_grads(place, x, parts, d, d13, fast, after):
    full, width = x.shape

    def body(n):
        me = n.place[0]
        start_weight(n.w, n.parts, 0, me, n.sems.at[0])
        late = [
            pltpu.make_async_copy(src, dst, n.sems.at[k + 2])
            for k, (src, dst) in enumerate([(n.dk, n.late_dk), (n.dv, n.late_dv), (n.d13, n.late_d13)])
        ]
        for copy in late:
            copy.start()
        put(n.grad, tm(n.x[...], n.dq[...]), 0)
        late[0].wait()
        put(n.grad, tm(n.x[...], n.late_dk[...]), width)
        late[1].wait()
        put(n.grad, tm(n.x[...], n.late_dv[...]), 2 * width)
        start_grad(n.grad, n.grads, me, n.sems.at[1])
        wait_all(n.w, n.sems.at[0])
        late[2].wait()
        for i in range(0, full, TILE):
            rows = slice(i, i + TILE)
            back = n.late_d13[rows].astype(F4)
            for c, d in enumerate((n.dq, n.late_dk, n.late_dv)):
                back = back + mt(d[rows], n.w[:, c * width : (c + 1) * width])
            n.ig[rows] = back.astype(BF)
        wait_all(n.grad, n.sems.at[1])

    return call(
        body,
        "self_grads",
        dict(
            place=(place, SMEM),
            x=(x, WHOLE),
            parts=(parts, HBM),
            dq=(d.dq, WHOLE),
            dk=(d.dk, HBM),
            dv=(d.dv, HBM),
            d13=(d13, HBM),
        ),
        dict(ig=(struct((full, width)), WHOLE), grads=(grad_shapes(width, 3 * width, fast), ANY)),
        dict(
            w=vmem(width, 3 * width),
            grad=vmem(width, 3 * width),
            late_dk=vmem(full, width),
            late_dv=vmem(full, width),
            late_d13=vmem(full, width),
            sems=pltpu.SemaphoreType.DMA((5,)),
        ),
        after=after,
    )


def total(groups, pieces, steps=1, after=()):
    rows = groups[0][0].shape[0]
    span = rows // pieces // steps
    widths = [group[0].shape[1] for group in groups]

    def body(n):
        left, at = 0, 0
        for group, columns in zip(groups, widths):
            for k, out in enumerate(n.outs):
                value = n.parts[at + k][...].astype(F4)
                for m in range(1, len(group)):
                    value = value + n.parts[at + m * pieces + k][...].astype(F4)
                out[:, left : left + columns] = value.astype(BF)
            left += columns
            at += len(group) * pieces

    def piece(k, columns):
        return pl.BlockSpec((span, columns), lambda i: (k * steps + i, 0))

    parts, specs = [], []
    for group, columns in zip(groups, widths):
        for array in group:
            for k in range(pieces):
                parts.append(array)
                specs.append(piece(k, columns))
    outs = [struct((rows // pieces, sum(widths)))] * pieces
    return call(
        body, "total", dict(parts=(parts, specs)), dict(outs=(outs, piece(0, sum(widths)))), {}, (steps,), after
    ).outs


def finish(arrays, cuts):
    rows = arrays[0].shape[0]

    def body(n):
        value = n.arrays[0][...].astype(F4)
        for array in n.arrays[1:]:
            value = value + array[...].astype(F4)
        for out, (low, high, *more) in zip(n.outs, cuts):
            if len(more) == 1:
                for k in range((high - low) // more[0]):
                    out[k * rows : (k + 1) * rows] = value[:, low + k * more[0] : low + (k + 1) * more[0]]
            elif more:
                out[...] = value[more[0] : more[1], low:high]
            else:
                out[...] = value[:, low:high]

    outs = []
    for low, high, *more in cuts:
        if len(more) == 1:
            outs.append(struct(((high - low) // more[0] * rows, more[0]), F4))
        else:
            outs.append(struct((more[1] - more[0] if more else rows, high - low), F4))
    return call(body, "total", dict(arrays=(arrays, WHOLE)), dict(outs=(outs, WHOLE)), {}).outs


def widen(array, dtype):
    def body(n):
        n.out[...] = n.array[...].astype(dtype)

    block = pl.BlockSpec((1,) + array.shape[1:], lambda i: (i, 0, 0))
    return call(
        body,
        "widen",
        dict(array=(array, block)),
        dict(out=(struct(array.shape, dtype), block)),
        {},
        grid=(array.shape[0],),
    ).out


def to_rows(array):
    seats = lax.axis_size("seq")
    blocks = array.reshape(seats, -1, array.shape[-1])
    return lax.all_to_all(blocks, "seq", split_axis=0, concat_axis=0, tiled=True)


def pack(weights, gains, shifts, bias, up, down, co):
    rows, hidden = up.shape
    width = co.shape[1]

    def body(n):
        at = 0
        for weight in n.weights:
            n.front[:, at : at + weight.shape[1]] = weight[...]
            at += weight.shape[1]
        block = jnp.zeros((rows, PAIR), F4)
        row = lax.broadcasted_iota(jnp.int32, (rows, PAIR), 0)
        lines = [(n.gains, k) for k in range(3)] + [(n.shifts, k) for k in range(4)] + [(n.bias, 0)]
        for k, (source, line) in enumerate(lines):
            piece = source[line : line + 1].astype(F4)
            piece = jnp.concatenate([piece, jnp.zeros((1, PAIR - piece.shape[1]), F4)], axis=1)
            block = jnp.where(row == k, piece, block)
        n.front[:, at:] = block.astype(BF)
        n.late[:, :hidden] = n.up[...]
        n.late[:, 2 * hidden :] = n.co[...]
        for k in range(hidden // width):
            n.late[:, hidden + k * width : hidden + (k + 1) * width] = n.down[k * rows : (k + 1) * rows]

    columns = sum(weight.shape[1] for weight in weights) + PAIR
    return call(
        body,
        "pack",
        dict(
            weights=(weights, WHOLE),
            gains=(gains, WHOLE),
            shifts=(shifts, WHOLE),
            bias=(bias, WHOLE),
            up=(up, WHOLE),
            down=(down, WHOLE),
            co=(co, WHOLE),
        ),
        dict(front=(struct((rows, columns)), WHOLE), late=(struct((rows, 2 * hidden + width)), WHOLE)),
        {},
    )


def held(array, after=()):
    def kernel(*refs):
        pass

    others = [other for other in LAST + list(after) if other is not array]
    result = pl.pallas_call(
        kernel,
        name="held",
        in_specs=[HBM] * (1 + len(others)),
        out_specs=HBM,
        out_shape=struct(array.shape, array.dtype),
        input_output_aliases={0: 0},
        cost_estimate=pl.CostEstimate(flops=1000000, bytes_accessed=0, transcendentals=0),
    )(array, *others)
    LAST[:] = [result]
    return result


def swap(value, bits):
    return lax.ppermute(value, AXES, [(i, i ^ bits) for i in range(FAST)])


def swap_all(value):
    groups = [list(range(core, FAST, 2)) for core in range(2)]
    return lax.all_to_all(value, AXES, split_axis=0, concat_axis=0, tiled=True, axis_index_groups=groups)


def join(arrays, cuts=(), after=()):
    arrays = list(arrays)
    rows, columns = sum(x.shape[0] for x in arrays), arrays[0].shape[1]
    edges = [0, *cuts, columns]

    def body(n):
        at, copies = 0, []
        for x in n.arrays:
            for out, low, high in zip(n.outs, edges[:-1], edges[1:]):
                src = x.at[:, pl.ds(low, high - low)]
                dst = out.at[pl.ds(at, x.shape[0])]
                copies.append(pltpu.make_async_copy(src, dst, n.sems.at[len(copies)]))
            at += x.shape[0]
        for copy in copies:
            copy.start()
        for copy in copies:
            copy.wait()

    outs = [struct((rows, high - low)) for low, high in zip(edges[:-1], edges[1:])]
    sems = pltpu.SemaphoreType.DMA((len(arrays) * len(outs),))
    return call(
        body, "join", dict(arrays=(arrays, HBM)), dict(outs=(outs, WHOLE)), dict(sems=sems), after=after
    ).outs


def swap_plane(held):
    return [held] + [swap(held, bits) for bits in (2, 4, 6)]


def swap_line(held):
    return [held] + [swap(held, z << 3) for z in (1, 2, 3)]


def swap_cores(parts):
    return parts + [swap(part, 1) for part in parts]


def spread_plane(pieces):
    return [pieces[0]] + [swap(piece, bits) for piece, bits in zip(pieces[1:], (2, 4, 6))]


def spread_line(pieces):
    return [pieces[0]] + [swap(piece, z << 3) for z, piece in enumerate(pieces[1:], 1)]


def on_device(
    inputs,
    memory,
    seg_ids,
    mem_lengths,
    cotangent,
    qkv_weight,
    self_out_weight,
    cross_q_weight,
    cross_kv_weight,
    cross_out_weight,
    ffn_in_weight,
    ffn_in_bias,
    ffn_out_weight,
    norm_gains,
    shift_vectors,
):
    seats = lax.axis_size("seq")
    devices = lax.axis_size("dp") * seats
    span, width = inputs.shape[1:]
    hidden = ffn_in_weight.shape[1]
    full = seats * span
    seat = lax.axis_index("seq")
    me = lax.axis_index("dp") * seats + seat
    LAST.clear()
    rows, piece, bias_piece = qkv_weight.shape[0], norm_gains.shape[1], ffn_in_bias.shape[0]
    fast = devices == FAST and rows == 16 and hidden == 4 * width
    place = me.astype(jnp.int32).reshape(1)
    second_group = [self_out_weight, cross_q_weight, cross_kv_weight, cross_out_weight]
    if fast:
        packed = pack(
            [qkv_weight, *second_group[:3]],
            norm_gains,
            shift_vectors,
            ffn_in_bias[None],
            ffn_in_weight,
            ffn_out_weight,
            cross_out_weight,
        )
        front = swap_line(packed.front)
        ffn_parts = [lax.all_gather(packed.late, AXES, axis=0, tiled=False)]
        x = to_rows(inputs).reshape(full, width)
        one, two = join(front, (3 * width,))
        (one,) = join(swap_plane(one), (), [x])
        qkv_parts = [one, swap(one, 1)]
        two = swap_plane(two)
        vec, bias = None, None
    else:
        x = to_rows(inputs).reshape(full, width)
        qkv_parts = [lax.all_gather(qkv_weight, AXES, axis=0, tiled=True)]
        two_parts = [lax.all_gather(jnp.concatenate(second_group, axis=1), AXES, axis=0, tiled=True)]
        ffn_parts = [lax.all_gather(w, AXES, axis=0, tiled=True) for w in (ffn_in_weight, ffn_out_weight)]
        vec = lax.all_gather(jnp.concatenate([norm_gains, shift_vectors], axis=0), AXES, axis=1, tiled=True)
        vec = jnp.pad(vec.astype(F4), ((0, 1), (0, 0)))
        bias = lax.all_gather(ffn_in_bias, AXES, axis=0, tiled=True).astype(F4)[None]
    mem = to_rows(memory).reshape(full, width)
    cot = to_rows(cotangent).reshape(full, width)

    segments = lax.dynamic_index_in_dim(seg_ids, seat, 0, keepdims=False)
    ends = jnp.cumsum(lax.dynamic_index_in_dim(mem_lengths, seat, 0, keepdims=False))
    places = jnp.arange(full, dtype=jnp.int32)
    mem_segments = jnp.sum((places[:, None] >= ends[None, :]).astype(jnp.int32), axis=1)
    lane = jnp.arange(PAIR, dtype=jnp.int32)
    half = jnp.arange(2, dtype=jnp.int32)[:, None, None]
    free = (lane // HEAD)[None, None] == 1 - half
    number = (lane % HEAD)[None, None]

    def key_side(ids):
        away = jnp.where(ids[None, :, None] == number, 0.0, AWAY)
        ones = jnp.where(number < 11, 1.0, 0.0)
        return jnp.where(free, jnp.where(number < 8, away, ones), 0.0).astype(BF)

    augq = jnp.where(free & (number < 8) & (segments[None, :, None] == number), 1.0, 0.0).astype(BF)
    augk, augm = key_side(segments), key_side(mem_segments)
    corner = jnp.arange(TILE, dtype=jnp.int32)
    tri = jnp.where(corner[None, :] <= corner[:, None], 0.0, AWAY).astype(F4)

    a = self_forward(place, x, qkv_parts, augq, augk, tri)
    if fast:
        (two,) = join(two, (), [mem])
        two_parts = [two, swap(two, 1)]
    c = cross_forward(place, x, mem, two_parts, a.ctx, vec, bias, augq, augm, hidden, fast)
    vec, bias = c.vec, c.bias
    m = middle(place, x, cot, [] if fast else two_parts, ffn_parts, c.cctx, c.xhat, vec, bias, fast)
    output = to_rows(m.out)

    if fast:
        big = lax.psum_scatter(m.grads[0], AXES, scatter_dimension=0, tiled=True)
    g = cross_back(
        place, mem, two_parts, c, m.dcctx, tri, a.ctx, m.d2, m.d3, vec, m.vec_sum, m.bias_rows, fast, []
    )
    two_sum = []
    if fast:
        two_sum = spread_plane(total([[g.grads[0], swap(held(g.grads[1], [output]), 1)]], 4))
    memory_grad = to_rows(g.mg)
    d = self_back(a, g.dctx, tri)
    s = self_grads(place, x, qkv_parts, d, g.d13, fast, [memory_grad])
    if fast:
        qkv_got = swap(held(s.grads[1], two_sum[1:]), 1)
        qkv_sum = spread_plane(total([[s.grads[0], qkv_got]], 4))
    memory_grad = widen(memory_grad, F4)
    output = widen(output, BF)
    if fast:
        line = spread_line(total([qkv_sum, two_sum], 4))
    input_grad = to_rows(held(s.ig))
    if fast:
        at = 7 * width
        qkv_sum, so_sum, cq_sum, ckv_sum, gains_sum, shifts_sum, bias_sum = finish(
            line,
            (
                (0, 3 * width),
                (3 * width, 4 * width),
                (4 * width, 5 * width),
                (5 * width, at),
                (at, at + piece, 0, 3),
                (at, at + piece, 3, 7),
                (at, at + bias_piece, 8, 9),
            ),
        )
        up_sum, co_sum, down_sum = finish(
            [big], ((0, hidden), (hidden, hidden + width), (hidden + width, 2 * hidden + width, width))
        )
    else:

        def scatter(value, dim=0):
            return lax.psum_scatter(value.astype(F4), AXES, scatter_dimension=dim, tiled=True)

        upco_sum, down_sum, two_sum, qkv_sum = [scatter(v) for v in (*m.grads, *g.grads, *s.grads)]
        up_sum, co_sum = upco_sum[:, :hidden], upco_sum[:, hidden:]
        so_sum, cq_sum, ckv_sum = two_sum[:, :width], two_sum[:, width : 2 * width], two_sum[:, 2 * width :]
        vec_sum, bias_sum = scatter(g.vec_sum[:7], 1), scatter(m.bias_sum[0])
        gains_sum, shifts_sum = vec_sum[:3], vec_sum[3:]
    return (
        output,
        input_grad.astype(F4),
        memory_grad,
        qkv_sum,
        so_sum,
        cq_sum,
        ckv_sum,
        co_sum,
        up_sum,
        bias_sum.reshape(-1),
        down_sum,
        gains_sum,
        shifts_sum,
    )


def solution(mesh):
    rows = P("dp", "seq", None)
    weight = P(AXES, None)
    vector = P(None, AXES)
    return jax.shard_map(
        on_device,
        mesh=mesh,
        in_specs=(rows, rows, P("dp", None), P("dp", None), rows)
        + (weight,) * 6
        + (P(AXES), weight, vector, vector),
        out_specs=(rows,) * 3 + (weight,) * 6 + (P(AXES), weight, vector, vector),
        check_vma=False,
    )
```

```python
import types

import jax
import jax.numpy as jnp
from jax import lax
from jax.experimental import pallas as pl
from jax.experimental.pallas import tpu as pltpu
from jax.sharding import PartitionSpec as P

HEAD = 64
PAIR = 2 * HEAD
TILE = 256
FAST = 32
HALF = FAST // 2
AXES = ("dp", "seq")
LOG2E = 1.4426950408889634
AWAY = -1e30
GELU_A = 0.7978845608028654
GELU_B = 0.044715
BF = jnp.bfloat16
F4 = jnp.float32
VMEM_BYTES = 58 << 20
SMALL_BYTES = 20 << 20


def mm(a, b):
    return lax.dot_general(a, b, (((1,), (0,)), ((), ())), preferred_element_type=F4)


def mt(a, b):
    return lax.dot_general(a, b, (((1,), (1,)), ((), ())), preferred_element_type=F4)


def tm(a, b):
    return lax.dot_general(a, b, (((0,), (0,)), ((), ())), preferred_element_type=F4)


def struct(shape, dtype=BF):
    return jax.ShapeDtypeStruct(tuple(shape), dtype)


ANY = pl.BlockSpec(memory_space=pl.ANY)
HBM = pl.BlockSpec(memory_space=pltpu.HBM)
WHOLE = pl.BlockSpec(memory_space=pltpu.VMEM)
SMEM = pl.BlockSpec(memory_space=pltpu.SMEM)


def aslist(value):
    return list(value) if isinstance(value, (list, tuple)) else [value]


LAST = []
COST = dict(
    self_forward=16,
    cross_forward=22,
    middle=31,
    cross_back=34,
    self_back=8,
    self_grads=0.2,
    total=2,
)
SMALL = ("total", "widen")
SCALE = 1.0
SUBS = 2
SKEW = 1


def call(body, name, ins, outs, scratch, grid=(), after=()):
    us = COST.get(name, 1.5)
    ins = dict(ins, after=(LAST + list(after), HBM))
    layout = [(key, len(aslist(value)), isinstance(value, (list, tuple))) for key, (value, _) in ins.items()]
    layout += [(key, len(aslist(value)), isinstance(value, (list, tuple))) for key, (value, _) in outs.items()]
    layout += [(key, 1, False) for key in scratch]

    def kernel(*refs):
        held, at = {}, 0
        for key, count, many in layout:
            held[key] = list(refs[at : at + count]) if many else refs[at]
            at += count
        body(types.SimpleNamespace(**held))

    arrays = [x for value, _ in ins.values() for x in aslist(value)]
    in_specs = []
    for value, spec in ins.values():
        in_specs += spec if isinstance(spec, list) else [spec] * len(aslist(value))
    out_specs = [spec for value, spec in outs.values() for _ in aslist(value)]
    out_shape = [x for value, _ in outs.values() for x in aslist(value)]
    result = pl.pallas_call(
        kernel,
        name=name,
        grid=grid,
        in_specs=in_specs,
        out_specs=out_specs,
        out_shape=out_shape,
        scratch_shapes=list(scratch.values()),
        compiler_params=pltpu.CompilerParams(vmem_limit_bytes=SMALL_BYTES if name in SMALL else VMEM_BYTES),
        cost_estimate=pl.CostEstimate(flops=int(us * SCALE * 1.1e9), bytes_accessed=0, transcendentals=0),
    )(*arrays)
    LAST[:] = [result[-1]]
    found, at = {}, 0
    for key, (value, _) in outs.items():
        count = len(aslist(value))
        found[key] = list(result[at : at + count]) if isinstance(value, (list, tuple)) else result[at]
        at += count
    return types.SimpleNamespace(**found)


def vmem(*shape, dtype=BF):
    return pltpu.VMEM(shape, dtype)


ORDER = [((p % 4) << 3) | ((p // 4 % 4) << 1) | (p // HALF) for p in range(FAST)]


def wait_all(buffer, sem):
    pltpu.make_async_copy(buffer, buffer, sem).wait()


def start_weight(dst, parts, first, me, sem):
    columns = dst.shape[-1]
    if len(parts) == 1:
        pltpu.make_async_copy(parts[0].at[:, pl.ds(first, columns)], dst, sem).start()
    else:
        span = dst.shape[0] // FAST
        each = FAST // len(parts)
        for p in range(FAST):
            place = pl.multiple_of((me ^ ORDER[p]) * span, span)
            src = parts[p // each].at[pl.ds((p % each) * span, span), pl.ds(first, columns)]
            pltpu.make_async_copy(src, dst.at[pl.ds(place, span)], sem).start()


def start_grad(src, parts, me, sem):
    if len(parts) == 1:
        pltpu.make_async_copy(src, parts[0], sem).start()
        return
    span = src.shape[0] // FAST
    for p in range(FAST):
        place = pl.multiple_of((me ^ ORDER[p]) * span, span)
        dst = parts[p // HALF].at[pl.ds((p % HALF) * span, span)]
        pltpu.make_async_copy(src.at[pl.ds(place, span)], dst, sem).start()


def grad_shapes(rows, columns, fast):
    return [struct((rows // 2, columns))] * 2 if fast else [struct((rows, columns))]


def take(ref, first=0, columns=None):
    columns = ref.shape[-1] - first if columns is None else columns
    return ref[..., first : first + columns].reshape(-1, columns)


def put(ref, value, first):
    ref[:, first : first + value.shape[1]] = value.astype(BF)


def norm(values):
    centered = values - jnp.mean(values, axis=-1, keepdims=True)
    inverse = lax.rsqrt(jnp.mean(centered * centered, axis=-1, keepdims=True) + 1e-05)
    return centered * inverse, inverse


def norm_back(upstream, normed, inverse, gain_row):
    gain_part = jnp.sum(upstream * normed, axis=0, keepdims=True)
    shift_part = jnp.sum(upstream, axis=0, keepdims=True)
    scaled = upstream * gain_row
    centered = scaled - jnp.mean(scaled, axis=-1, keepdims=True)
    value = inverse * (centered - normed * jnp.mean(scaled * normed, axis=-1, keepdims=True))
    return value, gain_part, shift_part


def lane_masks(dtype):
    lane = lax.broadcasted_iota(jnp.int32, (1, PAIR), 1)
    own = [(lane // HEAD == h).astype(dtype) for h in range(2)]

    def spot(h, k):
        return ((lane // HEAD == 1 - h) & (lane % HEAD == k)).astype(dtype)

    return own, spot


def attend_pair(causal, query, key, value, augq, augk, tri, ctx_out, qa_out, ka_out):
    total = key.shape[0]
    own, spot = lane_masks(F4)
    lane = lax.broadcasted_iota(jnp.int32, (TILE, PAIR), 1) % HEAD
    own_low = [mask.astype(BF) for mask in own]
    eighth = [(mask * HEAD ** (-0.5)).astype(BF) for mask in own]
    wide = jnp.concatenate([value, jnp.ones((total, PAIR), BF)], axis=1)
    keys = []
    for h in range(2):
        keys.append(key * own_low[h] + augk[h])
        ka_out[h] = keys[h]
    units = [(i, h) for i in range(query.shape[0] // TILE) for h in range(2)]
    scores, probs, halves = {}, {}, {}

    def score(i, h):
        rows = slice(i * TILE, (i + 1) * TILE)
        width = (i + 1) * TILE if causal else total
        head = query[rows] * eighth[h] + augq[h, rows]
        s = mt(head, keys[h][:width])
        if causal:
            tail = s[:, width - TILE :] + tri[...]
            s = jnp.concatenate([s[:, : width - TILE], tail], axis=1) if i else tail
        return s, head

    def finish(i, h, low, top, head):
        rows = slice(i * TILE, (i + 1) * TILE)
        both = mm(low, wide[: low.shape[1]])
        sums = both[:, PAIR:]
        halves[h] = both[:, :PAIR] / sums
        rest = -(top + jnp.log(sums))
        high = rest.astype(BF).astype(F4)
        rest = rest - high
        middle = rest.astype(BF).astype(F4)
        extra = jnp.where(lane == 8, high, jnp.where(lane == 9, middle, rest - middle))
        qa_out[h, rows] = head + (extra * (spot(h, 8) + spot(h, 9) + spot(h, 10))).astype(BF)
        if h == 1:
            ctx_out[rows] = (halves[0] * own[0] + halves[1] * own[1]).astype(BF)

    count = len(units)
    for t in range(count + 2):
        if t < count:
            scores[t] = score(*units[t])
        if 0 <= t - 2 < count:
            finish(*units[t - 2], *probs.pop(t - 2))
        if 0 <= t - 1 < count:
            s, head = scores.pop(t - 1)
            top = jnp.max(s, axis=1, keepdims=True)
            low = jnp.exp2(s * LOG2E - top * LOG2E).astype(BF)
            probs[t - 1] = (low, top, head)


def self_forward(place, x, parts, augq, augk, tri):
    full, width = x.shape
    heads = width // HEAD

    def body(n):
        pair = pl.program_id(0)

        @pl.when(pair == 0)
        def _():
            start_weight(n.w, n.parts, 0, n.place[0], n.sem)
            wait_all(n.w, n.sem)
            for c in range(0, 3 * width, 512):
                n.qkv[:, c : c + 512] = mm(n.x[...], take(n.w, c, 512)).astype(BF)

        def columns(part):
            return n.qkv[:, pl.ds(pl.multiple_of(part * width + pair * PAIR, PAIR), PAIR)]

        value = columns(2)
        n.value[...] = value
        attend_pair(True, columns(0), columns(1), value, n.augq, n.augk, n.tri, n.ctx, n.qa, n.ka)

    both = pl.BlockSpec((2, full, PAIR), lambda p: (p, 0, 0))
    fixed = pl.BlockSpec((2, full, PAIR), lambda p: (0, 0, 0))
    cols = pl.BlockSpec((full, PAIR), lambda p: (0, p))
    return call(
        body,
        "self_forward",
        dict(
            place=(place, SMEM),
            x=(x, pl.BlockSpec((full, width), lambda p: (0, 0))),
            parts=(parts, HBM),
            augq=(augq, fixed),
            augk=(augk, fixed),
            tri=(tri, pl.BlockSpec((TILE, TILE), lambda p: (0, 0))),
        ),
        dict(
            ctx=(struct((full, width)), cols),
            qa=(struct((heads, full, PAIR)), both),
            ka=(struct((heads, full, PAIR)), both),
            value=(struct((full, width)), cols),
        ),
        dict(
            w=vmem(width, 3 * width),
            qkv=vmem(full, 3 * width),
            sem=pltpu.SemaphoreType.DMA,
        ),
        grid=(heads // 2,),
    )


def unfold_vectors(blocks, vec, bias):
    width, hidden = vec.shape[1], bias.shape[1]
    piece, part = width // FAST, hidden // FAST
    lane = lax.broadcasted_iota(jnp.int32, (PAIR, width), 0)
    col = lax.broadcasted_iota(jnp.int32, (PAIR, width), 1)
    wide = mm(blocks, (lane == col % piece).astype(BF))
    row = lax.broadcasted_iota(jnp.int32, (width, width), 0)
    col = lax.broadcasted_iota(jnp.int32, (width, width), 1)
    wide = jnp.where(row // 16 == col // piece, wide, 0.0).astype(BF)
    line = lax.broadcasted_iota(jnp.int32, (8, width), 0)
    vec[...] = mm((line == lax.broadcasted_iota(jnp.int32, (8, width), 1) % 16).astype(BF), wide)
    owner = lax.broadcasted_iota(jnp.int32, (FAST, width), 0) * 16 + 7
    rows = mm((owner == lax.broadcasted_iota(jnp.int32, (FAST, width), 1)).astype(BF), blocks)
    for j in range(FAST):
        bias[:, j * part : (j + 1) * part] = rows[j : j + 1, :part]


def cross_forward(place, x, mem, parts, ctx, vec, bias, augq, augk, hidden, fast):
    full, width = x.shape
    heads = width // HEAD

    def body(n):
        pair = pl.program_id(0)

        @pl.when(pair == 0)
        def _():
            me = n.place[0]
            start_weight(n.w, n.parts, 0, me, n.sems.at[0])
            x_copy = pltpu.make_async_copy(n.x, n.x_kept, n.sems.at[2])
            mem_copy = pltpu.make_async_copy(n.mem, n.mem_kept, n.sems.at[3])
            x_copy.start()
            mem_copy.start()
            if fast:
                start_weight(n.blocks, n.parts, 4 * width, me, n.sems.at[1])
                wait_all(n.blocks, n.sems.at[1])
                unfold_vectors(n.blocks[...], n.vec, n.bias)
            else:
                n.vec[...] = n.vec_in[0][...]
                n.bias[...] = n.bias_in[0][...]
            wait_all(n.w, n.sems.at[0])
            x_copy.wait()
            for i in range(0, full, TILE):
                rows = slice(i, i + TILE)
                attn = mm(n.ctx[rows], n.w[:, :width])
                normed, inverse = norm(n.x_kept[rows].astype(F4) + attn)
                n.xhat[rows] = normed.astype(BF)
                n.inv[rows] = jnp.broadcast_to(inverse, (TILE, PAIR))
                first = (normed * n.vec[0:1] + n.vec[3:4]).astype(BF)
                n.q[rows] = mm(first, n.w[:, width : 2 * width]).astype(BF)
            mem_copy.wait()
            for c in range(0, 2 * width, 512):
                n.kv[:, c : c + 512] = mm(n.mem_kept[...], n.w[:, 2 * width + c : 2 * width + c + 512]).astype(BF)

        lanes = pl.ds(pl.multiple_of(pair * PAIR, PAIR), PAIR)
        late = pl.ds(pl.multiple_of(width + pair * PAIR, PAIR), PAIR)
        value = n.kv[:, late]
        n.value[...] = value
        attend_pair(False, n.q[:, lanes], n.kv[:, lanes], value, n.augq, n.augk, None, n.cctx, n.qa, n.ka)

    both = pl.BlockSpec((2, full, PAIR), lambda p: (p, 0, 0))
    fixed = pl.BlockSpec((2, full, PAIR), lambda p: (0, 0, 0))
    cols = pl.BlockSpec((full, PAIR), lambda p: (0, p))

    def still(shape):
        return pl.BlockSpec(shape, lambda p: (0, 0))

    return call(
        body,
        "cross_forward",
        dict(
            place=(place, SMEM),
            x=(x, HBM),
            mem=(mem, HBM),
            parts=(parts, HBM),
            ctx=(ctx, still((full, width))),
            vec_in=([] if fast else [vec], still((8, width))),
            bias_in=([] if fast else [bias], still((1, hidden))),
            augq=(augq, fixed),
            augk=(augk, fixed),
        ),
        dict(
            cctx=(struct((full, width)), cols),
            qa=(struct((heads, full, PAIR)), both),
            ka=(struct((heads, full, PAIR)), both),
            value=(struct((full, width)), cols),
            xhat=(struct((full, width)), still((full, width))),
            inv=(struct((full, PAIR), F4), still((full, PAIR))),
            vec=(struct((8, width), F4), still((8, width))),
            bias=(struct((1, hidden), F4), still((1, hidden))),
        ),
        dict(
            w=vmem(width, 4 * width),
            q=vmem(full, width),
            kv=vmem(full, 2 * width),
            blocks=vmem(width, PAIR),
            x_kept=vmem(full, width),
            mem_kept=vmem(full, width),
            sems=pltpu.SemaphoreType.DMA((4,)),
        ),
        grid=(heads // 2,),
    )


def middle(place, x, cot, co_parts, ffn_parts, cctx, xhat, vec, bias, fast):
    full, width = x.shape
    hidden = bias.shape[1]
    fold = hidden // width
    late = hidden + width
    block = SUBS * TILE

    def body(n):
        me = n.place[0]
        step = pl.program_id(0)

        @pl.when(step == 0)
        def _():
            if fast:
                whole = n.ffn_parts[0]
                pltpu.make_async_copy(whole.at[:, :, pl.ds(2 * hidden, width)], n.co, n.sems.at[0]).start()
                pltpu.make_async_copy(whole.at[:, :, pl.ds(0, hidden)], n.up, n.sems.at[1]).start()
                for k in range(fold):
                    src = whole.at[:, :, pl.ds(hidden + k * width, width)]
                    pltpu.make_async_copy(src, n.down.at[:, k], n.sems.at[2]).start()
            else:
                start_weight(n.co, n.co_parts, 4 * width, me, n.sems.at[0])
                start_weight(n.up, n.ffn_parts[:1], 0, me, n.sems.at[1])
                start_weight(n.down, n.ffn_parts[1:], 0, me, n.sems.at[2])
            pltpu.make_async_copy(n.x, n.x_kept, n.sems.at[3]).start()
            pltpu.make_async_copy(n.cot, n.cot_kept, n.sems.at[4]).start()
            n.vec_sum[...] = jnp.zeros(n.vec_sum.shape, F4)
            n.bias_sum[...] = jnp.zeros(n.bias_sum.shape, F4)
            wait_all(n.co, n.sems.at[0])
            wait_all(n.up, n.sems.at[1])
            wait_all(n.down, n.sems.at[2])
            wait_all(n.x_kept, n.sems.at[3])
            wait_all(n.cot_kept, n.sems.at[4])

        vec = n.vec

        def tile_steps(k):
            rows = slice(k * TILE, (k + 1) * TILE)
            kept = pl.ds(pl.multiple_of(step * block + k * TILE, TILE), TILE)
            v = types.SimpleNamespace()

            def enter():
                context = n.cctx[rows]
                n.context[kept] = context
                v.first = n.xhat[rows].astype(F4) * vec[0:1] + vec[3:4] + mm(context, take(n.co))

            def norm_one():
                v.normed_one, v.inverse_one = norm(v.first)
                v.second = v.normed_one * vec[1:2] + vec[4:5]
                v.low = v.second.astype(BF)
                n.second[kept] = v.low

            def rise():
                v.pre = mm(v.low, take(n.up)) + n.bias[...]

            def gelu():
                pre = v.pre
                slope = GELU_A * GELU_B * (pre * pre) + GELU_A
                t = jnp.tanh(pre * slope)
                half = 0.5 * t + 0.5
                v.hid = (pre * half).astype(BF)
                n.hid[kept] = v.hid
                v.d_gelu = half + (0.5 - 0.5 * t * t) * pre * (3.0 * slope - 2.0 * GELU_A)

            def fall():
                v.ffn = mm(v.hid, take(n.down)) + vec[6:7]

            def norm_two():
                normed, inverse = norm(v.second + v.ffn + n.x_kept[kept].astype(F4))
                n.out[rows] = (normed * vec[2:3] + vec[5:6]).astype(BF)
                v.d_three, gain, shift = norm_back(n.cot_kept[kept].astype(F4), normed, inverse, vec[2:3])
                v.df = v.d_three.astype(BF)
                n.d3[rows] = v.df
                n.df[kept] = v.df
                n.vec_sum[2:3] += gain
                n.vec_sum[5:6] += shift
                n.vec_sum[6:7] += jnp.sum(v.d_three, axis=0, keepdims=True)

            def back_down():
                v.d_hid = mt(v.df, take(n.down))

            def back_gelu():
                d_pre = v.d_hid * v.d_gelu
                v.d_pre = d_pre.astype(BF)
                n.d_pre[kept] = v.d_pre
                n.bias_sum[...] += jnp.sum(d_pre, axis=0, keepdims=True)

            def back_up():
                v.d_second = v.d_three + mt(v.d_pre, take(n.up))

            def norm_one_back():
                d_two, gain, shift = norm_back(v.d_second, v.normed_one, v.inverse_one, vec[1:2])
                v.dc = d_two.astype(BF)
                n.d2[rows] = v.dc
                n.dc[kept] = v.dc
                n.vec_sum[1:2] += gain
                n.vec_sum[4:5] += shift

            def leave():
                n.dcctx[rows] = mt(v.dc, take(n.co)).astype(BF)

            return [
                enter, norm_one, rise, gelu, fall, norm_two, back_down, back_gelu, back_up, norm_one_back, leave
            ]

        tiles = [tile_steps(k) for k in range(SUBS)]
        for t in range(len(tiles[0]) + SKEW * (SUBS - 1)):
            for k, steps in enumerate(tiles):
                if 0 <= t - SKEW * k < len(steps):
                    steps[t - SKEW * k]()

        @pl.when(step == full // block - 1)
        def _():
            for c in range(0, hidden, 512):
                part = tm(n.hid[:, c : c + 512], n.df[...]).astype(BF)
                if fast:
                    rows = width // FAST
                    part = part.reshape(512 // (fold * rows), fold, rows, width)
                    top = c // fold
                    for a in range(fold):
                        n.grad[top : top + 512 // fold, late + a * width : late + (a + 1) * width] = part[
                            :, a
                        ].reshape(512 // fold, width)
                else:
                    n.grad_down[c : c + 512] = part
            if fast:
                edge = pl.ds(late, fold * width)
                first = pltpu.make_async_copy(n.grad.at[:, edge], n.grads[0].at[:, edge], n.sems.at[0])
                edge = pl.ds(0, late)
                last = pltpu.make_async_copy(n.grad.at[:, edge], n.grads[0].at[:, edge], n.sems.at[1])
            else:
                first = pltpu.make_async_copy(n.grad_down, n.grads[1], n.sems.at[0])
                last = pltpu.make_async_copy(n.grad, n.grads[0], n.sems.at[1])
            first.start()
            for c in range(0, hidden, 512):
                n.grad[:, c : c + 512] = tm(n.second[...], n.d_pre[:, c : c + 512]).astype(BF)
            n.grad[:, hidden : hidden + width] = tm(n.context[...], n.dc[...]).astype(BF)
            last.start()
            share = hidden // n.bias_rows.shape[0]
            n.bias_rows[...] = jnp.zeros(n.bias_rows.shape, BF)
            for j in range(n.bias_rows.shape[0]):
                n.bias_rows[j : j + 1, :share] = n.bias_sum[:, j * share : (j + 1) * share].astype(BF)
            first.wait()
            last.wait()

    if fast:
        grads = [struct((width, late + fold * width))]
        scratch = dict(
            co=vmem(FAST, width // FAST, width),
            up=vmem(FAST, width // FAST, hidden),
            down=vmem(FAST, fold, width // FAST, width),
            grad=vmem(width, late + fold * width),
        )
    else:
        grads = [struct((width, late)), struct((hidden, width))]
        scratch = dict(
            co=vmem(width, width),
            up=vmem(width, hidden),
            down=vmem(hidden, width),
            grad=vmem(width, late),
            grad_down=vmem(hidden, width),
        )
    tile = pl.BlockSpec((block, width), lambda i: (i, 0))

    def still(shape):
        return pl.BlockSpec(shape, lambda i: (0, 0))

    return call(
        body,
        "middle",
        dict(
            place=(place, SMEM),
            x=(x, HBM),
            cot=(cot, HBM),
            co_parts=(co_parts, HBM),
            ffn_parts=(ffn_parts, HBM),
            cctx=(cctx, tile),
            xhat=(xhat, tile),
            vec=(vec, still(vec.shape)),
            bias=(bias, still(bias.shape)),
        ),
        dict(
            out=(struct((full, width)), tile),
            d3=(struct((full, width)), tile),
            d2=(struct((full, width)), tile),
            dcctx=(struct((full, width)), tile),
            vec_sum=(struct((8, width), F4), still((8, width))),
            bias_sum=(struct((1, hidden), F4), still((1, hidden))),
            bias_rows=(struct((FAST, PAIR)), still((FAST, PAIR))),
            grads=(grads, ANY),
        ),
        dict(
            scratch,
            context=vmem(full, width),
            second=vmem(full, width),
            hid=vmem(full, hidden),
            d_pre=vmem(full, hidden),
            df=vmem(full, width),
            dc=vmem(full, width),
            x_kept=vmem(full, width),
            cot_kept=vmem(full, width),
            sems=pltpu.SemaphoreType.DMA((5,)),
        ),
        grid=(full // block,),
    )


def attend_pair_back(causal, qa, ka, value, ctx, dctx, tri, dq, dk, dv):
    own, spot = lane_masks(F4)
    total = value.shape[0]
    blocks = total // TILE
    upstream = dctx[...].astype(F4)
    product = upstream * ctx[...].astype(F4)
    row = lax.broadcasted_iota(jnp.int32, (PAIR, PAIR), 0) // HEAD
    col = lax.broadcasted_iota(jnp.int32, (PAIR, PAIR), 1) // HEAD
    swap = jnp.where(row != col, -1.0, 0.0).astype(BF)
    high = product.astype(BF)
    delta = mm(high, swap) + mm((product - high.astype(F4)).astype(BF), swap)
    delta_high = delta.astype(BF).astype(F4)
    delta_low = delta - delta_high
    values = value[...].astype(F4)
    d_query, d_key, d_value = [], [], []
    for h in range(2):
        spots = spot(h, 0) + spot(h, 1)
        do = (upstream * own[h] + delta_high * spot(h, 0) + delta_low * spot(h, 1)).astype(BF)
        va = (values * own[h] + spots).astype(BF)
        query, key = qa[h], ka[h]
        query_t = query.T[h * HEAD : (h + 1) * HEAD]
        do_t = do.T[h * HEAD : (h + 1) * HEAD]
        keys, vals, sums = [], [], [None] * blocks
        for j in range(blocks):
            start = j * TILE if causal else 0
            key_j, va_j = key[j * TILE : (j + 1) * TILE], va[j * TILE : (j + 1) * TILE]
            s = mt(query[start:], key_j)
            if causal:
                head = s[:TILE] + tri[...]
                s = jnp.concatenate([head, s[TILE:]], axis=0) if j < blocks - 1 else head
            prob = jnp.exp2(s * LOG2E)
            ds = (prob * mt(do[start:], va_j)).astype(BF)
            vals.append(mm(do_t[:, start:], prob.astype(BF)))
            keys.append(mm(query_t[:, start:], ds))
            back = mm(ds, key_j)
            for i in range(start // TILE, blocks):
                part = back[i * TILE - start : (i + 1) * TILE - start]
                sums[i] = part if sums[i] is None else sums[i] + part
        d_query.append(jnp.concatenate(sums, axis=0))
        d_key.append(jnp.concatenate(keys, axis=1))
        d_value.append(jnp.concatenate(vals, axis=1))
    dq[...] = ((d_query[0] * own[0] + d_query[1] * own[1]) * HEAD ** (-0.5)).astype(BF)
    dk[...] = jnp.concatenate(d_key, axis=0).T.astype(BF)
    dv[...] = jnp.concatenate(d_value, axis=0).T.astype(BF)


def cross_back(place, mem, parts, att, dcctx, tri, ctx, d2, d3, vec, vec_mid, bias_mid, fast, after):
    full, width = mem.shape
    extra = PAIR if fast else 0
    pairs, tiles = width // PAIR, full // TILE

    def body(n):
        me = n.place[0]
        step = pl.program_id(0)
        vec = n.vec
        loads = [(n.ctx, n.kept_ctx), (n.mem, n.kept_mem), (n.xhat, n.kept_xhat), (n.inv, n.kept_inv)]
        loads += [(n.d2, n.kept_d2), (n.d3, n.kept_d3)]

        @pl.when(step == 0)
        def _():
            n.vec_sum[...] = n.vec_mid[...]
            start_weight(n.w, n.parts, 0, me, n.sems.at[0])
            for k, (src, dst) in enumerate(loads):
                pltpu.make_async_copy(src, dst, n.sems.at[k + 1]).start()

        @pl.when(step < pairs)
        def _():
            lanes = pl.ds(pl.multiple_of(jnp.minimum(step, pairs - 1) * PAIR, PAIR), PAIR)
            attend_pair_back(
                False,
                n.qa,
                n.ka,
                n.value,
                n.cctx,
                n.dcctx,
                n.tri,
                n.dq.at[:, lanes],
                n.dk.at[:, lanes],
                n.dv.at[:, lanes],
            )

        @pl.when(step == pairs)
        def _():
            wait_all(n.w, n.sems.at[0])
            for k, (src, dst) in enumerate(loads):
                pltpu.make_async_copy(src, dst, n.sems.at[k + 1]).wait()

        @pl.when(step >= pairs)
        def _():
            rows = pl.ds(pl.multiple_of(jnp.maximum(step - pairs, 0) * TILE, TILE), TILE)
            normed = n.kept_xhat[rows].astype(F4)
            n.first[rows] = (normed * vec[0:1] + vec[3:4]).astype(BF)
            d_first = n.kept_d2[rows].astype(F4) + mt(n.dq[rows], n.w[:, width : 2 * width])
            back = mt(n.dk[rows], n.w[:, 2 * width : 3 * width]) + mt(n.dv[rows], n.w[:, 3 * width :])
            n.mg[...] = back.astype(BF)
            inverse = jnp.concatenate([n.kept_inv[rows]] * (width // PAIR), axis=1)
            d_one, gain, shift = norm_back(d_first, normed, inverse, vec[0:1])
            n.d13[...] = (n.kept_d3[rows].astype(F4) + d_one).astype(BF)
            da = d_one.astype(BF)
            n.da[rows] = da
            n.dctx[...] = mt(da, n.w[:, :width]).astype(BF)
            n.vec_sum[0:1] += gain
            n.vec_sum[3:4] += shift

        @pl.when(step == pairs + tiles - 1)
        def _():
            put(n.grad, tm(n.kept_mem[...], n.dk[...]), 2 * width)
            put(n.grad, tm(n.kept_mem[...], n.dv[...]), 3 * width)
            put(n.grad, tm(n.kept_ctx[...], n.da[...]), 0)
            put(n.grad, tm(n.first[...], n.dq[...]), width)
            if fast:
                piece = width // FAST
                row = lax.broadcasted_iota(jnp.int32, (width, width), 0)
                col = lax.broadcasted_iota(jnp.int32, (width, width), 1)
                line = lax.broadcasted_iota(jnp.int32, (width, 8), 0) % piece
                pick_line = (line == lax.broadcasted_iota(jnp.int32, (width, 8), 1)).astype(BF)
                spread = mm(pick_line, n.vec_sum[...].astype(BF))
                spread = jnp.where(row // piece == col // piece, spread, 0.0).astype(BF)
                lane = lax.broadcasted_iota(jnp.int32, (width, PAIR), 1)
                fold = (lax.broadcasted_iota(jnp.int32, (width, PAIR), 0) % piece == lane).astype(BF)
                owner = lax.broadcasted_iota(jnp.int32, (width, FAST), 0)
                wanted = lax.broadcasted_iota(jnp.int32, (width, FAST), 1) * piece + 8
                put(n.grad, mm(spread, fold) + mm((owner == wanted).astype(BF), n.bias_mid[...]), 4 * width)
            start_grad(n.grad, n.grads, me, n.sems.at[0])
            wait_all(n.grad, n.sems.at[0])

    def pair(i):
        return jnp.minimum(i, pairs - 1)

    both = pl.BlockSpec((2, full, PAIR), lambda i: (pair(i), 0, 0))
    cols = pl.BlockSpec((full, PAIR), lambda i: (0, pair(i)))
    tile = pl.BlockSpec((TILE, width), lambda i: (jnp.maximum(i - pairs, 0), 0))

    def still(array):
        return (array, pl.BlockSpec(array.shape, lambda i: (0, 0)))

    return call(
        body,
        "cross_back",
        dict(
            place=(place, SMEM),
            qa=(att.qa, both),
            ka=(att.ka, both),
            value=(att.value, cols),
            cctx=(att.cctx, cols),
            dcctx=(dcctx, cols),
            tri=still(tri),
            parts=(parts, HBM),
            mem=(mem, HBM),
            ctx=(ctx, HBM),
            xhat=(att.xhat, HBM),
            inv=(att.inv, HBM),
            d2=(d2, HBM),
            d3=(d3, HBM),
            vec=still(vec),
            vec_mid=still(vec_mid),
            bias_mid=still(bias_mid),
        ),
        dict(
            mg=(struct((full, width)), tile),
            d13=(struct((full, width)), tile),
            dctx=(struct((full, width)), tile),
            vec_sum=still(struct((8, width), F4)),
            grads=(grad_shapes(width, 4 * width + extra, fast), ANY),
        ),
        dict(
            w=vmem(width, 4 * width),
            dq=vmem(full, width),
            dk=vmem(full, width),
            dv=vmem(full, width),
            kept_ctx=vmem(full, width),
            kept_mem=vmem(full, width),
            kept_xhat=vmem(full, width),
            kept_inv=vmem(full, PAIR, dtype=F4),
            kept_d2=vmem(full, width),
            kept_d3=vmem(full, width),
            first=vmem(full, width),
            da=vmem(full, width),
            grad=vmem(width, 4 * width + extra),
            sems=pltpu.SemaphoreType.DMA((7,)),
        ),
        grid=(pairs + tiles,),
        after=after,
    )


def self_back(att, dctx, tri):
    full, width = att.value.shape

    def body(n):
        attend_pair_back(True, n.qa, n.ka, n.value, n.ctx, n.dctx, n.tri, n.dq, n.dk, n.dv)

    both = pl.BlockSpec((2, full, PAIR), lambda p: (p, 0, 0))
    cols = pl.BlockSpec((full, PAIR), lambda p: (0, p))
    made = (struct((full, width)), cols)
    return call(
        body,
        "self_back",
        dict(

            qa=(att.qa, both),
            ka=(att.ka, both),
            value=(att.value, cols),
            ctx=(att.ctx, cols),
            dctx=(dctx, cols),
            tri=(tri, pl.BlockSpec((TILE, TILE), lambda p: (0, 0))),
        ),
        dict(dq=made, dk=made, dv=made),
        {},
        grid=(width // PAIR,),
    )


def self_grads(place, x, parts, d, d13, fast, after):
    full, width = x.shape

    def body(n):
        me = n.place[0]
        start_weight(n.w, n.parts, 0, me, n.sems.at[0])
        late = [
            pltpu.make_async_copy(src, dst, n.sems.at[k + 2])
            for k, (src, dst) in enumerate([(n.dk, n.late_dk), (n.dv, n.late_dv), (n.d13, n.late_d13)])
        ]
        for copy in late:
            copy.start()
        put(n.grad, tm(n.x[...], n.dq[...]), 0)
        late[0].wait()
        put(n.grad, tm(n.x[...], n.late_dk[...]), width)
        late[1].wait()
        put(n.grad, tm(n.x[...], n.late_dv[...]), 2 * width)
        start_grad(n.grad, n.grads, me, n.sems.at[1])
        wait_all(n.w, n.sems.at[0])
        late[2].wait()
        for i in range(0, full, TILE):
            rows = slice(i, i + TILE)
            back = n.late_d13[rows].astype(F4)
            for c, d in enumerate((n.dq, n.late_dk, n.late_dv)):
                back = back + mt(d[rows], n.w[:, c * width : (c + 1) * width])
            n.ig[rows] = back.astype(BF)
        wait_all(n.grad, n.sems.at[1])

    return call(
        body,
        "self_grads",
        dict(
            place=(place, SMEM),
            x=(x, WHOLE),
            parts=(parts, HBM),
            dq=(d.dq, WHOLE),
            dk=(d.dk, HBM),
            dv=(d.dv, HBM),
            d13=(d13, HBM),
        ),
        dict(ig=(struct((full, width)), WHOLE), grads=(grad_shapes(width, 3 * width, fast), ANY)),
        dict(
            w=vmem(width, 3 * width),
            grad=vmem(width, 3 * width),
            late_dk=vmem(full, width),
            late_dv=vmem(full, width),
            late_d13=vmem(full, width),
            sems=pltpu.SemaphoreType.DMA((5,)),
        ),
        after=after,
    )


def total(groups, pieces, steps=1, after=()):
    rows = groups[0][0].shape[0]
    span = rows // pieces // steps
    widths = [group[0].shape[1] for group in groups]

    def body(n):
        left, at = 0, 0
        for group, columns in zip(groups, widths):
            for k, out in enumerate(n.outs):
                value = n.parts[at + k][...].astype(F4)
                for m in range(1, len(group)):
                    value = value + n.parts[at + m * pieces + k][...].astype(F4)
                out[:, left : left + columns] = value.astype(BF)
            left += columns
            at += len(group) * pieces

    def piece(k, columns):
        return pl.BlockSpec((span, columns), lambda i: (k * steps + i, 0))

    parts, specs = [], []
    for group, columns in zip(groups, widths):
        for array in group:
            for k in range(pieces):
                parts.append(array)
                specs.append(piece(k, columns))
    outs = [struct((rows // pieces, sum(widths)))] * pieces
    return call(
        body, "total", dict(parts=(parts, specs)), dict(outs=(outs, piece(0, sum(widths)))), {}, (steps,), after
    ).outs


def finish(arrays, cuts):
    rows = arrays[0].shape[0]

    def body(n):
        value = n.arrays[0][...].astype(F4)
        for array in n.arrays[1:]:
            value = value + array[...].astype(F4)
        for out, (low, high, *more) in zip(n.outs, cuts):
            if len(more) == 1:
                for k in range((high - low) // more[0]):
                    out[k * rows : (k + 1) * rows] = value[:, low + k * more[0] : low + (k + 1) * more[0]]
            elif more:
                out[...] = value[more[0] : more[1], low:high]
            else:
                out[...] = value[:, low:high]

    outs = []
    for low, high, *more in cuts:
        if len(more) == 1:
            outs.append(struct(((high - low) // more[0] * rows, more[0]), F4))
        else:
            outs.append(struct((more[1] - more[0] if more else rows, high - low), F4))
    return call(body, "total", dict(arrays=(arrays, WHOLE)), dict(outs=(outs, WHOLE)), {}).outs


def widen(array, dtype):
    def body(n):
        n.out[...] = n.array[...].astype(dtype)

    block = pl.BlockSpec((1,) + array.shape[1:], lambda i: (i, 0, 0))
    return call(
        body,
        "widen",
        dict(array=(array, block)),
        dict(out=(struct(array.shape, dtype), block)),
        {},
        grid=(array.shape[0],),
    ).out


def to_rows(array):
    seats = lax.axis_size("seq")
    blocks = array.reshape(seats, -1, array.shape[-1])
    return lax.all_to_all(blocks, "seq", split_axis=0, concat_axis=0, tiled=True)


def pack(weights, gains, shifts, bias, up, down, co):
    rows, hidden = up.shape
    width = co.shape[1]

    def body(n):
        at = 0
        for weight in n.weights:
            n.front[:, at : at + weight.shape[1]] = weight[...]
            at += weight.shape[1]
        block = jnp.zeros((rows, PAIR), F4)
        row = lax.broadcasted_iota(jnp.int32, (rows, PAIR), 0)
        lines = [(n.gains, k) for k in range(3)] + [(n.shifts, k) for k in range(4)] + [(n.bias, 0)]
        for k, (source, line) in enumerate(lines):
            piece = source[line : line + 1].astype(F4)
            piece = jnp.concatenate([piece, jnp.zeros((1, PAIR - piece.shape[1]), F4)], axis=1)
            block = jnp.where(row == k, piece, block)
        n.front[:, at:] = block.astype(BF)
        n.late[:, :hidden] = n.up[...]
        n.late[:, 2 * hidden :] = n.co[...]
        for k in range(hidden // width):
            n.late[:, hidden + k * width : hidden + (k + 1) * width] = n.down[k * rows : (k + 1) * rows]

    columns = sum(weight.shape[1] for weight in weights) + PAIR
    return call(
        body,
        "pack",
        dict(
            weights=(weights, WHOLE),
            gains=(gains, WHOLE),
            shifts=(shifts, WHOLE),
            bias=(bias, WHOLE),
            up=(up, WHOLE),
            down=(down, WHOLE),
            co=(co, WHOLE),
        ),
        dict(front=(struct((rows, columns)), WHOLE), late=(struct((rows, 2 * hidden + width)), WHOLE)),
        {},
    )


def held(array, after=()):
    def kernel(*refs):
        pass

    others = [other for other in LAST + list(after) if other is not array]
    result = pl.pallas_call(
        kernel,
        name="held",
        in_specs=[HBM] * (1 + len(others)),
        out_specs=HBM,
        out_shape=struct(array.shape, array.dtype),
        input_output_aliases={0: 0},
        cost_estimate=pl.CostEstimate(flops=1000000, bytes_accessed=0, transcendentals=0),
    )(array, *others)
    LAST[:] = [result]
    return result


def swap(value, bits):
    return lax.ppermute(value, AXES, [(i, i ^ bits) for i in range(FAST)])


def swap_all(value):
    groups = [list(range(core, FAST, 2)) for core in range(2)]
    return lax.all_to_all(value, AXES, split_axis=0, concat_axis=0, tiled=True, axis_index_groups=groups)


def join(arrays, cuts=(), after=()):
    arrays = list(arrays)
    rows, columns = sum(x.shape[0] for x in arrays), arrays[0].shape[1]
    edges = [0, *cuts, columns]

    def body(n):
        at, copies = 0, []
        for x in n.arrays:
            for out, low, high in zip(n.outs, edges[:-1], edges[1:]):
                src = x.at[:, pl.ds(low, high - low)]
                dst = out.at[pl.ds(at, x.shape[0])]
                copies.append(pltpu.make_async_copy(src, dst, n.sems.at[len(copies)]))
            at += x.shape[0]
        for copy in copies:
            copy.start()
        for copy in copies:
            copy.wait()

    outs = [struct((rows, high - low)) for low, high in zip(edges[:-1], edges[1:])]
    sems = pltpu.SemaphoreType.DMA((len(arrays) * len(outs),))
    return call(
        body, "join", dict(arrays=(arrays, HBM)), dict(outs=(outs, WHOLE)), dict(sems=sems), after=after
    ).outs


def swap_plane(held):
    return [held] + [swap(held, bits) for bits in (2, 4, 6)]


def swap_line(held):
    return [held] + [swap(held, z << 3) for z in (1, 2, 3)]


def swap_cores(parts):
    return parts + [swap(part, 1) for part in parts]


def spread_plane(pieces):
    return [pieces[0]] + [swap(piece, bits) for piece, bits in zip(pieces[1:], (2, 4, 6))]


def spread_line(pieces):
    return [pieces[0]] + [swap(piece, z << 3) for z, piece in enumerate(pieces[1:], 1)]


def on_device(
    inputs,
    memory,
    seg_ids,
    mem_lengths,
    cotangent,
    qkv_weight,
    self_out_weight,
    cross_q_weight,
    cross_kv_weight,
    cross_out_weight,
    ffn_in_weight,
    ffn_in_bias,
    ffn_out_weight,
    norm_gains,
    shift_vectors,
):
    seats = lax.axis_size("seq")
    devices = lax.axis_size("dp") * seats
    span, width = inputs.shape[1:]
    hidden = ffn_in_weight.shape[1]
    full = seats * span
    seat = lax.axis_index("seq")
    me = lax.axis_index("dp") * seats + seat
    LAST.clear()
    rows, piece, bias_piece = qkv_weight.shape[0], norm_gains.shape[1], ffn_in_bias.shape[0]
    fast = devices == FAST and rows == 16 and hidden == 4 * width
    place = me.astype(jnp.int32).reshape(1)
    second_group = [self_out_weight, cross_q_weight, cross_kv_weight, cross_out_weight]
    if fast:
        packed = pack(
            [qkv_weight, *second_group[:3]],
            norm_gains,
            shift_vectors,
            ffn_in_bias[None],
            ffn_in_weight,
            ffn_out_weight,
            cross_out_weight,
        )
        front = swap_line(packed.front)
        ffn_parts = [lax.all_gather(packed.late, AXES, axis=0, tiled=False)]
        x = to_rows(inputs).reshape(full, width)
        one, two = join(front, (3 * width,))
        (one,) = join(swap_plane(one), (), [x])
        qkv_parts = [one, swap(one, 1)]
        two = swap_plane(two)
        vec, bias = None, None
    else:
        x = to_rows(inputs).reshape(full, width)
        qkv_parts = [lax.all_gather(qkv_weight, AXES, axis=0, tiled=True)]
        two_parts = [lax.all_gather(jnp.concatenate(second_group, axis=1), AXES, axis=0, tiled=True)]
        ffn_parts = [lax.all_gather(w, AXES, axis=0, tiled=True) for w in (ffn_in_weight, ffn_out_weight)]
        vec = lax.all_gather(jnp.concatenate([norm_gains, shift_vectors], axis=0), AXES, axis=1, tiled=True)
        vec = jnp.pad(vec.astype(F4), ((0, 1), (0, 0)))
        bias = lax.all_gather(ffn_in_bias, AXES, axis=0, tiled=True).astype(F4)[None]
    mem = to_rows(memory).reshape(full, width)
    cot = to_rows(cotangent).reshape(full, width)

    segments = lax.dynamic_index_in_dim(seg_ids, seat, 0, keepdims=False)
    ends = jnp.cumsum(lax.dynamic_index_in_dim(mem_lengths, seat, 0, keepdims=False))
    places = jnp.arange(full, dtype=jnp.int32)
    mem_segments = jnp.sum((places[:, None] >= ends[None, :]).astype(jnp.int32), axis=1)
    lane = jnp.arange(PAIR, dtype=jnp.int32)
    half = jnp.arange(2, dtype=jnp.int32)[:, None, None]
    free = (lane // HEAD)[None, None] == 1 - half
    number = (lane % HEAD)[None, None]

    def key_side(ids):
        away = jnp.where(ids[None, :, None] == number, 0.0, AWAY)
        ones = jnp.where(number < 11, 1.0, 0.0)
        return jnp.where(free, jnp.where(number < 8, away, ones), 0.0).astype(BF)

    augq = jnp.where(free & (number < 8) & (segments[None, :, None] == number), 1.0, 0.0).astype(BF)
    augk, augm = key_side(segments), key_side(mem_segments)
    corner = jnp.arange(TILE, dtype=jnp.int32)
    tri = jnp.where(corner[None, :] <= corner[:, None], 0.0, AWAY).astype(F4)

    a = self_forward(place, x, qkv_parts, augq, augk, tri)
    if fast:
        (two,) = join(two, (), [mem])
        two_parts = [two, swap(two, 1)]
    c = cross_forward(place, x, mem, two_parts, a.ctx, vec, bias, augq, augm, hidden, fast)
    vec, bias = c.vec, c.bias
    m = middle(place, x, cot, [] if fast else two_parts, ffn_parts, c.cctx, c.xhat, vec, bias, fast)
    output = to_rows(m.out)

    if fast:
        big = lax.psum_scatter(m.grads[0], AXES, scatter_dimension=0, tiled=True)
    g = cross_back(
        place, mem, two_parts, c, m.dcctx, tri, a.ctx, m.d2, m.d3, vec, m.vec_sum, m.bias_rows, fast, []
    )
    two_sum = []
    if fast:
        two_sum = spread_plane(total([[g.grads[0], swap(held(g.grads[1], [output]), 1)]], 4))
    memory_grad = to_rows(g.mg)
    d = self_back(a, g.dctx, tri)
    s = self_grads(place, x, qkv_parts, d, g.d13, fast, [memory_grad])
    if fast:
        qkv_got = swap(held(s.grads[1], two_sum[1:]), 1)
        qkv_sum = spread_plane(total([[s.grads[0], qkv_got]], 4))
    memory_grad = widen(memory_grad, F4)
    output = widen(output, BF)
    if fast:
        line = spread_line(total([qkv_sum, two_sum], 4))
    input_grad = to_rows(held(s.ig))
    if fast:
        at = 7 * width
        qkv_sum, so_sum, cq_sum, ckv_sum, gains_sum, shifts_sum, bias_sum = finish(
            line,
            (
                (0, 3 * width),
                (3 * width, 4 * width),
                (4 * width, 5 * width),
                (5 * width, at),
                (at, at + piece, 0, 3),
                (at, at + piece, 3, 7),
                (at, at + bias_piece, 8, 9),
            ),
        )
        up_sum, co_sum, down_sum = finish(
            [big], ((0, hidden), (hidden, hidden + width), (hidden + width, 2 * hidden + width, width))
        )
    else:

        def scatter(value, dim=0):
            return lax.psum_scatter(value.astype(F4), AXES, scatter_dimension=dim, tiled=True)

        upco_sum, down_sum, two_sum, qkv_sum = [scatter(v) for v in (*m.grads, *g.grads, *s.grads)]
        up_sum, co_sum = upco_sum[:, :hidden], upco_sum[:, hidden:]
        so_sum, cq_sum, ckv_sum = two_sum[:, :width], two_sum[:, width : 2 * width], two_sum[:, 2 * width :]
        vec_sum, bias_sum = scatter(g.vec_sum[:7], 1), scatter(m.bias_sum[0])
        gains_sum, shifts_sum = vec_sum[:3], vec_sum[3:]
    return (
        output,
        input_grad.astype(F4),
        memory_grad,
        qkv_sum,
        so_sum,
        cq_sum,
        ckv_sum,
        co_sum,
        up_sum,
        bias_sum.reshape(-1),
        down_sum,
        gains_sum,
        shifts_sum,
    )


def solution(mesh):
    rows = P("dp", "seq", None)
    weight = P(AXES, None)
    vector = P(None, AXES)
    return jax.shard_map(
        on_device,
        mesh=mesh,
        in_specs=(rows, rows, P("dp", None), P("dp", None), rows)
        + (weight,) * 6
        + (P(AXES), weight, vector, vector),
        out_specs=(rows,) * 3 + (weight,) * 6 + (P(AXES), weight, vector, vector),
        check_vma=False,
    )
```

```python
import types

import jax
import jax.numpy as jnp
from jax import lax
from jax.experimental import pallas as pl
from jax.experimental.pallas import tpu as pltpu
from jax.sharding import PartitionSpec as P

HEAD = 64
PAIR = 2 * HEAD
TILE = 256
FAST = 32
HALF = FAST // 2
AXES = ("dp", "seq")
LOG2E = 1.4426950408889634
AWAY = -1e30
GELU_A = 0.7978845608028654
GELU_B = 0.044715
BF = jnp.bfloat16
F4 = jnp.float32
VMEM_BYTES = 58 << 20
SMALL_BYTES = 20 << 20


def mm(a, b):
    return lax.dot_general(a, b, (((1,), (0,)), ((), ())), preferred_element_type=F4)


def mt(a, b):
    return lax.dot_general(a, b, (((1,), (1,)), ((), ())), preferred_element_type=F4)


def tm(a, b):
    return lax.dot_general(a, b, (((0,), (0,)), ((), ())), preferred_element_type=F4)


def struct(shape, dtype=BF):
    return jax.ShapeDtypeStruct(tuple(shape), dtype)


ANY = pl.BlockSpec(memory_space=pl.ANY)
HBM = pl.BlockSpec(memory_space=pltpu.HBM)
WHOLE = pl.BlockSpec(memory_space=pltpu.VMEM)
SMEM = pl.BlockSpec(memory_space=pltpu.SMEM)


def aslist(value):
    return list(value) if isinstance(value, (list, tuple)) else [value]


LAST = []
COST = dict(
    self_forward=16,
    cross_forward=22,
    middle=31,
    cross_back=34,
    self_back=8,
    self_grads=0.2,
    total=2,
)
SMALL = ("total", "widen")
SCALE = 1.0
SUBS = 2
SKEW = 1


def call(body, name, ins, outs, scratch, grid=(), after=()):
    us = COST.get(name, 1.5)
    ins = dict(ins, after=(LAST + list(after), HBM))
    layout = [(key, len(aslist(value)), isinstance(value, (list, tuple))) for key, (value, _) in ins.items()]
    layout += [(key, len(aslist(value)), isinstance(value, (list, tuple))) for key, (value, _) in outs.items()]
    layout += [(key, 1, False) for key in scratch]

    def kernel(*refs):
        held, at = {}, 0
        for key, count, many in layout:
            held[key] = list(refs[at : at + count]) if many else refs[at]
            at += count
        body(types.SimpleNamespace(**held))

    arrays = [x for value, _ in ins.values() for x in aslist(value)]
    in_specs = []
    for value, spec in ins.values():
        in_specs += spec if isinstance(spec, list) else [spec] * len(aslist(value))
    out_specs = [spec for value, spec in outs.values() for _ in aslist(value)]
    out_shape = [x for value, _ in outs.values() for x in aslist(value)]
    result = pl.pallas_call(
        kernel,
        name=name,
        grid=grid,
        in_specs=in_specs,
        out_specs=out_specs,
        out_shape=out_shape,
        scratch_shapes=list(scratch.values()),
        compiler_params=pltpu.CompilerParams(vmem_limit_bytes=SMALL_BYTES if name in SMALL else VMEM_BYTES),
        cost_estimate=pl.CostEstimate(flops=int(us * SCALE * 1.1e9), bytes_accessed=0, transcendentals=0),
    )(*arrays)
    LAST[:] = [result[-1]]
    found, at = {}, 0
    for key, (value, _) in outs.items():
        count = len(aslist(value))
        found[key] = list(result[at : at + count]) if isinstance(value, (list, tuple)) else result[at]
        at += count
    return types.SimpleNamespace(**found)


def vmem(*shape, dtype=BF):
    return pltpu.VMEM(shape, dtype)


ORDER = [((p % 4) << 3) | ((p // 4 % 4) << 1) | (p // HALF) for p in range(FAST)]


def wait_all(buffer, sem):
    pltpu.make_async_copy(buffer, buffer, sem).wait()


def start_weight(dst, parts, first, me, sem):
    columns = dst.shape[-1]
    if len(parts) == 1:
        pltpu.make_async_copy(parts[0].at[:, pl.ds(first, columns)], dst, sem).start()
    else:
        span = dst.shape[0] // FAST
        each = FAST // len(parts)
        for p in range(FAST):
            place = pl.multiple_of((me ^ ORDER[p]) * span, span)
            src = parts[p // each].at[pl.ds((p % each) * span, span), pl.ds(first, columns)]
            pltpu.make_async_copy(src, dst.at[pl.ds(place, span)], sem).start()


def start_grad(src, parts, me, sem):
    if len(parts) == 1:
        pltpu.make_async_copy(src, parts[0], sem).start()
        return
    span = src.shape[0] // FAST
    for p in range(FAST):
        place = pl.multiple_of((me ^ ORDER[p]) * span, span)
        dst = parts[p // HALF].at[pl.ds((p % HALF) * span, span)]
        pltpu.make_async_copy(src.at[pl.ds(place, span)], dst, sem).start()


def grad_shapes(rows, columns, fast):
    return [struct((rows // 2, columns))] * 2 if fast else [struct((rows, columns))]


def take(ref, first=0, columns=None):
    columns = ref.shape[-1] - first if columns is None else columns
    return ref[..., first : first + columns].reshape(-1, columns)


def put(ref, value, first):
    ref[:, first : first + value.shape[1]] = value.astype(BF)


def norm(values):
    centered = values - jnp.mean(values, axis=-1, keepdims=True)
    inverse = lax.rsqrt(jnp.mean(centered * centered, axis=-1, keepdims=True) + 1e-05)
    return centered * inverse, inverse


def norm_back(upstream, normed, inverse, gain_row):
    gain_part = jnp.sum(upstream * normed, axis=0, keepdims=True)
    shift_part = jnp.sum(upstream, axis=0, keepdims=True)
    scaled = upstream * gain_row
    centered = scaled - jnp.mean(scaled, axis=-1, keepdims=True)
    value = inverse * (centered - normed * jnp.mean(scaled * normed, axis=-1, keepdims=True))
    return value, gain_part, shift_part


def lane_masks(dtype):
    lane = lax.broadcasted_iota(jnp.int32, (1, PAIR), 1)
    own = [(lane // HEAD == h).astype(dtype) for h in range(2)]

    def spot(h, k):
        return ((lane // HEAD == 1 - h) & (lane % HEAD == k)).astype(dtype)

    return own, spot


def attend_pair(causal, query, key, value, augq, augk, tri, ctx_out, qa_out, ka_out):
    total = key.shape[0]
    own, spot = lane_masks(F4)
    lane = lax.broadcasted_iota(jnp.int32, (TILE, PAIR), 1) % HEAD
    own_low = [mask.astype(BF) for mask in own]
    eighth = [(mask * HEAD ** (-0.5)).astype(BF) for mask in own]
    wide = jnp.concatenate([value, jnp.ones((total, PAIR), BF)], axis=1)
    keys = []
    for h in range(2):
        keys.append(key * own_low[h] + augk[h])
        ka_out[h] = keys[h]
    units = [(i, h) for i in range(query.shape[0] // TILE) for h in range(2)]
    scores, probs, halves = {}, {}, {}

    def score(i, h):
        rows = slice(i * TILE, (i + 1) * TILE)
        width = (i + 1) * TILE if causal else total
        head = query[rows] * eighth[h] + augq[h, rows]
        s = mt(head, keys[h][:width])
        if causal:
            tail = s[:, width - TILE :] + tri[...]
            s = jnp.concatenate([s[:, : width - TILE], tail], axis=1) if i else tail
        return s, head

    def finish(i, h, low, top, head):
        rows = slice(i * TILE, (i + 1) * TILE)
        both = mm(low, wide[: low.shape[1]])
        sums = both[:, PAIR:]
        halves[h] = both[:, :PAIR] / sums
        rest = -(top + jnp.log(sums))
        high = rest.astype(BF).astype(F4)
        rest = rest - high
        middle = rest.astype(BF).astype(F4)
        extra = jnp.where(lane == 8, high, jnp.where(lane == 9, middle, rest - middle))
        qa_out[h, rows] = head + (extra * (spot(h, 8) + spot(h, 9) + spot(h, 10))).astype(BF)
        if h == 1:
            ctx_out[rows] = (halves[0] * own[0] + halves[1] * own[1]).astype(BF)

    count = len(units)
    for t in range(count + 2):
        if t < count:
            scores[t] = score(*units[t])
        if 0 <= t - 2 < count:
            finish(*units[t - 2], *probs.pop(t - 2))
        if 0 <= t - 1 < count:
            s, head = scores.pop(t - 1)
            top = jnp.max(s, axis=1, keepdims=True)
            low = jnp.exp2(s * LOG2E - top * LOG2E).astype(BF)
            probs[t - 1] = (low, top, head)


def self_forward(place, x, parts, augq, augk, tri):
    full, width = x.shape
    heads = width // HEAD

    def body(n):
        pair = pl.program_id(0)

        @pl.when(pair == 0)
        def _():
            start_weight(n.w, n.parts, 0, n.place[0], n.sem)
            wait_all(n.w, n.sem)
            for c in range(0, 3 * width, 512):
                n.qkv[:, c : c + 512] = mm(n.x[...], take(n.w, c, 512)).astype(BF)

        def columns(part):
            return n.qkv[:, pl.ds(pl.multiple_of(part * width + pair * PAIR, PAIR), PAIR)]

        value = columns(2)
        n.value[...] = value
        attend_pair(True, columns(0), columns(1), value, n.augq, n.augk, n.tri, n.ctx, n.qa, n.ka)

    both = pl.BlockSpec((2, full, PAIR), lambda p: (p, 0, 0))
    fixed = pl.BlockSpec((2, full, PAIR), lambda p: (0, 0, 0))
    cols = pl.BlockSpec((full, PAIR), lambda p: (0, p))
    return call(
        body,
        "self_forward",
        dict(
            place=(place, SMEM),
            x=(x, pl.BlockSpec((full, width), lambda p: (0, 0))),
            parts=(parts, HBM),
            augq=(augq, fixed),
            augk=(augk, fixed),
            tri=(tri, pl.BlockSpec((TILE, TILE), lambda p: (0, 0))),
        ),
        dict(
            ctx=(struct((full, width)), cols),
            qa=(struct((heads, full, PAIR)), both),
            ka=(struct((heads, full, PAIR)), both),
            value=(struct((full, width)), cols),
        ),
        dict(
            w=vmem(width, 3 * width),
            qkv=vmem(full, 3 * width),
            sem=pltpu.SemaphoreType.DMA,
        ),
        grid=(heads // 2,),
    )


def unfold_vectors(blocks, vec, bias):
    width, hidden = vec.shape[1], bias.shape[1]
    piece, part = width // FAST, hidden // FAST
    lane = lax.broadcasted_iota(jnp.int32, (PAIR, width), 0)
    col = lax.broadcasted_iota(jnp.int32, (PAIR, width), 1)
    wide = mm(blocks, (lane == col % piece).astype(BF))
    row = lax.broadcasted_iota(jnp.int32, (width, width), 0)
    col = lax.broadcasted_iota(jnp.int32, (width, width), 1)
    wide = jnp.where(row // 16 == col // piece, wide, 0.0).astype(BF)
    line = lax.broadcasted_iota(jnp.int32, (8, width), 0)
    vec[...] = mm((line == lax.broadcasted_iota(jnp.int32, (8, width), 1) % 16).astype(BF), wide)
    owner = lax.broadcasted_iota(jnp.int32, (FAST, width), 0) * 16 + 7
    rows = mm((owner == lax.broadcasted_iota(jnp.int32, (FAST, width), 1)).astype(BF), blocks)
    for j in range(FAST):
        bias[:, j * part : (j + 1) * part] = rows[j : j + 1, :part]


def cross_forward(place, x, mem, parts, ctx, vec, bias, augq, augk, hidden, fast):
    full, width = x.shape
    heads = width // HEAD

    def body(n):
        pair = pl.program_id(0)

        @pl.when(pair == 0)
        def _():
            me = n.place[0]
            start_weight(n.w, n.parts, 0, me, n.sems.at[0])
            x_copy = pltpu.make_async_copy(n.x, n.x_kept, n.sems.at[2])
            mem_copy = pltpu.make_async_copy(n.mem, n.mem_kept, n.sems.at[3])
            x_copy.start()
            mem_copy.start()
            if fast:
                start_weight(n.blocks, n.parts, 4 * width, me, n.sems.at[1])
                wait_all(n.blocks, n.sems.at[1])
                unfold_vectors(n.blocks[...], n.vec, n.bias)
            else:
                n.vec[...] = n.vec_in[0][...]
                n.bias[...] = n.bias_in[0][...]
            wait_all(n.w, n.sems.at[0])
            x_copy.wait()
            for i in range(0, full, TILE):
                rows = slice(i, i + TILE)
                attn = mm(n.ctx[rows], n.w[:, :width])
                normed, inverse = norm(n.x_kept[rows].astype(F4) + attn)
                n.xhat[rows] = normed.astype(BF)
                n.inv[rows] = jnp.broadcast_to(inverse, (TILE, PAIR))
                first = (normed * n.vec[0:1] + n.vec[3:4]).astype(BF)
                n.q[rows] = mm(first, n.w[:, width : 2 * width]).astype(BF)
            mem_copy.wait()
            for c in range(0, 2 * width, 512):
                n.kv[:, c : c + 512] = mm(n.mem_kept[...], n.w[:, 2 * width + c : 2 * width + c + 512]).astype(BF)

        lanes = pl.ds(pl.multiple_of(pair * PAIR, PAIR), PAIR)
        late = pl.ds(pl.multiple_of(width + pair * PAIR, PAIR), PAIR)
        value = n.kv[:, late]
        n.value[...] = value
        attend_pair(False, n.q[:, lanes], n.kv[:, lanes], value, n.augq, n.augk, None, n.cctx, n.qa, n.ka)

    both = pl.BlockSpec((2, full, PAIR), lambda p: (p, 0, 0))
    fixed = pl.BlockSpec((2, full, PAIR), lambda p: (0, 0, 0))
    cols = pl.BlockSpec((full, PAIR), lambda p: (0, p))

    def still(shape):
        return pl.BlockSpec(shape, lambda p: (0, 0))

    return call(
        body,
        "cross_forward",
        dict(
            place=(place, SMEM),
            x=(x, HBM),
            mem=(mem, HBM),
            parts=(parts, HBM),
            ctx=(ctx, still((full, width))),
            vec_in=([] if fast else [vec], still((8, width))),
            bias_in=([] if fast else [bias], still((1, hidden))),
            augq=(augq, fixed),
            augk=(augk, fixed),
        ),
        dict(
            cctx=(struct((full, width)), cols),
            qa=(struct((heads, full, PAIR)), both),
            ka=(struct((heads, full, PAIR)), both),
            value=(struct((full, width)), cols),
            xhat=(struct((full, width)), still((full, width))),
            inv=(struct((full, PAIR), F4), still((full, PAIR))),
            vec=(struct((8, width), F4), still((8, width))),
            bias=(struct((1, hidden), F4), still((1, hidden))),
        ),
        dict(
            w=vmem(width, 4 * width),
            q=vmem(full, width),
            kv=vmem(full, 2 * width),
            blocks=vmem(width, PAIR),
            x_kept=vmem(full, width),
            mem_kept=vmem(full, width),
            sems=pltpu.SemaphoreType.DMA((4,)),
        ),
        grid=(heads // 2,),
    )


def middle(place, x, cot, co_parts, ffn_parts, cctx, xhat, vec, bias, fast):
    full, width = x.shape
    hidden = bias.shape[1]
    fold = hidden // width
    late = hidden + width
    block = SUBS * TILE

    def body(n):
        me = n.place[0]
        step = pl.program_id(0)

        @pl.when(step == 0)
        def _():
            if fast:
                whole = n.ffn_parts[0]
                pltpu.make_async_copy(whole.at[:, :, pl.ds(2 * hidden, width)], n.co, n.sems.at[0]).start()
                pltpu.make_async_copy(whole.at[:, :, pl.ds(0, hidden)], n.up, n.sems.at[1]).start()
                for k in range(fold):
                    src = whole.at[:, :, pl.ds(hidden + k * width, width)]
                    pltpu.make_async_copy(src, n.down.at[:, k], n.sems.at[2]).start()
            else:
                start_weight(n.co, n.co_parts, 4 * width, me, n.sems.at[0])
                start_weight(n.up, n.ffn_parts[:1], 0, me, n.sems.at[1])
                start_weight(n.down, n.ffn_parts[1:], 0, me, n.sems.at[2])
            pltpu.make_async_copy(n.x, n.x_kept, n.sems.at[3]).start()
            pltpu.make_async_copy(n.cot, n.cot_kept, n.sems.at[4]).start()
            n.vec_sum[...] = jnp.zeros(n.vec_sum.shape, F4)
            n.bias_sum[...] = jnp.zeros(n.bias_sum.shape, F4)
            wait_all(n.co, n.sems.at[0])

        vec = n.vec

        def first_use(k, *pairs):
            if k == 0:

                @pl.when(step == 0)
                def _():
                    for buffer, sem in pairs:
                        wait_all(buffer, n.sems.at[sem])

        def tile_steps(k):
            rows = slice(k * TILE, (k + 1) * TILE)
            kept = pl.ds(pl.multiple_of(step * block + k * TILE, TILE), TILE)
            v = types.SimpleNamespace()

            def enter():
                context = n.cctx[rows]
                n.context[kept] = context
                v.first = n.xhat[rows].astype(F4) * vec[0:1] + vec[3:4] + mm(context, take(n.co))

            def norm_one():
                v.normed_one, v.inverse_one = norm(v.first)
                v.second = v.normed_one * vec[1:2] + vec[4:5]
                v.low = v.second.astype(BF)
                n.second[kept] = v.low

            def rise():
                first_use(k, (n.up, 1))
                v.pre = mm(v.low, take(n.up)) + n.bias[...]

            def gelu():
                pre = v.pre
                slope = GELU_A * GELU_B * (pre * pre) + GELU_A
                t = jnp.tanh(pre * slope)
                half = 0.5 * t + 0.5
                v.hid = (pre * half).astype(BF)
                n.hid[kept] = v.hid
                v.d_gelu = half + (0.5 - 0.5 * t * t) * pre * (3.0 * slope - 2.0 * GELU_A)

            def fall():
                first_use(k, (n.down, 2))
                v.ffn = mm(v.hid, take(n.down)) + vec[6:7]

            def norm_two():
                first_use(k, (n.x_kept, 3), (n.cot_kept, 4))
                normed, inverse = norm(v.second + v.ffn + n.x_kept[kept].astype(F4))
                n.out[rows] = (normed * vec[2:3] + vec[5:6]).astype(BF)
                v.d_three, gain, shift = norm_back(n.cot_kept[kept].astype(F4), normed, inverse, vec[2:3])
                v.df = v.d_three.astype(BF)
                n.d3[rows] = v.df
                n.df[kept] = v.df
                n.vec_sum[2:3] += gain
                n.vec_sum[5:6] += shift
                n.vec_sum[6:7] += jnp.sum(v.d_three, axis=0, keepdims=True)

            def back_down():
                v.d_hid = mt(v.df, take(n.down))

            def back_gelu():
                d_pre = v.d_hid * v.d_gelu
                v.d_pre = d_pre.astype(BF)
                n.d_pre[kept] = v.d_pre
                n.bias_sum[...] += jnp.sum(d_pre, axis=0, keepdims=True)

            def back_up():
                v.d_second = v.d_three + mt(v.d_pre, take(n.up))

            def norm_one_back():
                d_two, gain, shift = norm_back(v.d_second, v.normed_one, v.inverse_one, vec[1:2])
                v.dc = d_two.astype(BF)
                n.d2[rows] = v.dc
                n.dc[kept] = v.dc
                n.vec_sum[1:2] += gain
                n.vec_sum[4:5] += shift

            def leave():
                n.dcctx[rows] = mt(v.dc, take(n.co)).astype(BF)

            return [
                enter, norm_one, rise, gelu, fall, norm_two, back_down, back_gelu, back_up, norm_one_back, leave
            ]

        tiles = [tile_steps(k) for k in range(SUBS)]
        for t in range(len(tiles[0]) + SKEW * (SUBS - 1)):
            for k, steps in enumerate(tiles):
                if 0 <= t - SKEW * k < len(steps):
                    steps[t - SKEW * k]()

        @pl.when(step == full // block - 1)
        def _():
            for c in range(0, hidden, 512):
                part = tm(n.hid[:, c : c + 512], n.df[...]).astype(BF)
                if fast:
                    rows = width // FAST
                    part = part.reshape(512 // (fold * rows), fold, rows, width)
                    top = c // fold
                    for a in range(fold):
                        n.grad[top : top + 512 // fold, late + a * width : late + (a + 1) * width] = part[
                            :, a
                        ].reshape(512 // fold, width)
                else:
                    n.grad_down[c : c + 512] = part
            if fast:
                edge = pl.ds(late, fold * width)
                first = pltpu.make_async_copy(n.grad.at[:, edge], n.grads[0].at[:, edge], n.sems.at[0])
                edge = pl.ds(0, late)
                last = pltpu.make_async_copy(n.grad.at[:, edge], n.grads[0].at[:, edge], n.sems.at[1])
            else:
                first = pltpu.make_async_copy(n.grad_down, n.grads[1], n.sems.at[0])
                last = pltpu.make_async_copy(n.grad, n.grads[0], n.sems.at[1])
            first.start()
            for c in range(0, hidden, 512):
                n.grad[:, c : c + 512] = tm(n.second[...], n.d_pre[:, c : c + 512]).astype(BF)
            n.grad[:, hidden : hidden + width] = tm(n.context[...], n.dc[...]).astype(BF)
            last.start()
            share = hidden // n.bias_rows.shape[0]
            n.bias_rows[...] = jnp.zeros(n.bias_rows.shape, BF)
            for j in range(n.bias_rows.shape[0]):
                n.bias_rows[j : j + 1, :share] = n.bias_sum[:, j * share : (j + 1) * share].astype(BF)
            first.wait()
            last.wait()

    if fast:
        grads = [struct((width, late + fold * width))]
        scratch = dict(
            co=vmem(FAST, width // FAST, width),
            up=vmem(FAST, width // FAST, hidden),
            down=vmem(FAST, fold, width // FAST, width),
            grad=vmem(width, late + fold * width),
        )
    else:
        grads = [struct((width, late)), struct((hidden, width))]
        scratch = dict(
            co=vmem(width, width),
            up=vmem(width, hidden),
            down=vmem(hidden, width),
            grad=vmem(width, late),
            grad_down=vmem(hidden, width),
        )
    tile = pl.BlockSpec((block, width), lambda i: (i, 0))

    def still(shape):
        return pl.BlockSpec(shape, lambda i: (0, 0))

    return call(
        body,
        "middle",
        dict(
            place=(place, SMEM),
            x=(x, HBM),
            cot=(cot, HBM),
            co_parts=(co_parts, HBM),
            ffn_parts=(ffn_parts, HBM),
            cctx=(cctx, tile),
            xhat=(xhat, tile),
            vec=(vec, still(vec.shape)),
            bias=(bias, still(bias.shape)),
        ),
        dict(
            out=(struct((full, width)), tile),
            d3=(struct((full, width)), tile),
            d2=(struct((full, width)), tile),
            dcctx=(struct((full, width)), tile),
            vec_sum=(struct((8, width), F4), still((8, width))),
            bias_sum=(struct((1, hidden), F4), still((1, hidden))),
            bias_rows=(struct((FAST, PAIR)), still((FAST, PAIR))),
            grads=(grads, ANY),
        ),
        dict(
            scratch,
            context=vmem(full, width),
            second=vmem(full, width),
            hid=vmem(full, hidden),
            d_pre=vmem(full, hidden),
            df=vmem(full, width),
            dc=vmem(full, width),
            x_kept=vmem(full, width),
            cot_kept=vmem(full, width),
            sems=pltpu.SemaphoreType.DMA((5,)),
        ),
        grid=(full // block,),
    )


def attend_pair_back(causal, qa, ka, value, ctx, dctx, tri, dq, dk, dv):
    own, spot = lane_masks(F4)
    total = value.shape[0]
    blocks = total // TILE
    upstream = dctx[...].astype(F4)
    product = upstream * ctx[...].astype(F4)
    row = lax.broadcasted_iota(jnp.int32, (PAIR, PAIR), 0) // HEAD
    col = lax.broadcasted_iota(jnp.int32, (PAIR, PAIR), 1) // HEAD
    swap = jnp.where(row != col, -1.0, 0.0).astype(BF)
    high = product.astype(BF)
    delta = mm(high, swap) + mm((product - high.astype(F4)).astype(BF), swap)
    delta_high = delta.astype(BF).astype(F4)
    delta_low = delta - delta_high
    values = value[...].astype(F4)
    d_query, d_key, d_value = [], [], []
    for h in range(2):
        spots = spot(h, 0) + spot(h, 1)
        do = (upstream * own[h] + delta_high * spot(h, 0) + delta_low * spot(h, 1)).astype(BF)
        va = (values * own[h] + spots).astype(BF)
        query, key = qa[h], ka[h]
        query_t = query.T[h * HEAD : (h + 1) * HEAD]
        do_t = do.T[h * HEAD : (h + 1) * HEAD]
        keys, vals, sums = [], [], [None] * blocks
        for j in range(blocks):
            start = j * TILE if causal else 0
            key_j, va_j = key[j * TILE : (j + 1) * TILE], va[j * TILE : (j + 1) * TILE]
            s = mt(query[start:], key_j)
            if causal:
                head = s[:TILE] + tri[...]
                s = jnp.concatenate([head, s[TILE:]], axis=0) if j < blocks - 1 else head
            prob = jnp.exp2(s * LOG2E)
            ds = (prob * mt(do[start:], va_j)).astype(BF)
            vals.append(mm(do_t[:, start:], prob.astype(BF)))
            keys.append(mm(query_t[:, start:], ds))
            back = mm(ds, key_j)
            for i in range(start // TILE, blocks):
                part = back[i * TILE - start : (i + 1) * TILE - start]
                sums[i] = part if sums[i] is None else sums[i] + part
        d_query.append(jnp.concatenate(sums, axis=0))
        d_key.append(jnp.concatenate(keys, axis=1))
        d_value.append(jnp.concatenate(vals, axis=1))
    dq[...] = ((d_query[0] * own[0] + d_query[1] * own[1]) * HEAD ** (-0.5)).astype(BF)
    dk[...] = jnp.concatenate(d_key, axis=0).T.astype(BF)
    dv[...] = jnp.concatenate(d_value, axis=0).T.astype(BF)


def cross_back(place, mem, parts, att, dcctx, tri, ctx, d2, d3, vec, vec_mid, bias_mid, fast, after):
    full, width = mem.shape
    extra = PAIR if fast else 0
    pairs, tiles = width // PAIR, full // TILE

    def body(n):
        me = n.place[0]
        step = pl.program_id(0)
        vec = n.vec
        loads = [(n.ctx, n.kept_ctx), (n.mem, n.kept_mem), (n.xhat, n.kept_xhat), (n.inv, n.kept_inv)]
        loads += [(n.d2, n.kept_d2), (n.d3, n.kept_d3)]

        @pl.when(step == 0)
        def _():
            n.vec_sum[...] = n.vec_mid[...]
            start_weight(n.w, n.parts, 0, me, n.sems.at[0])
            for k, (src, dst) in enumerate(loads):
                pltpu.make_async_copy(src, dst, n.sems.at[k + 1]).start()

        @pl.when(step < pairs)
        def _():
            lanes = pl.ds(pl.multiple_of(jnp.minimum(step, pairs - 1) * PAIR, PAIR), PAIR)
            attend_pair_back(
                False,
                n.qa,
                n.ka,
                n.value,
                n.cctx,
                n.dcctx,
                n.tri,
                n.dq.at[:, lanes],
                n.dk.at[:, lanes],
                n.dv.at[:, lanes],
            )

        @pl.when(step == pairs)
        def _():
            wait_all(n.w, n.sems.at[0])
            for k, (src, dst) in enumerate(loads):
                pltpu.make_async_copy(src, dst, n.sems.at[k + 1]).wait()

        @pl.when(step >= pairs)
        def _():
            rows = pl.ds(pl.multiple_of(jnp.maximum(step - pairs, 0) * TILE, TILE), TILE)
            normed = n.kept_xhat[rows].astype(F4)
            n.first[rows] = (normed * vec[0:1] + vec[3:4]).astype(BF)
            d_first = n.kept_d2[rows].astype(F4) + mt(n.dq[rows], n.w[:, width : 2 * width])
            back = mt(n.dk[rows], n.w[:, 2 * width : 3 * width]) + mt(n.dv[rows], n.w[:, 3 * width :])
            n.mg[...] = back.astype(BF)
            inverse = jnp.concatenate([n.kept_inv[rows]] * (width // PAIR), axis=1)
            d_one, gain, shift = norm_back(d_first, normed, inverse, vec[0:1])
            n.d13[...] = (n.kept_d3[rows].astype(F4) + d_one).astype(BF)
            da = d_one.astype(BF)
            n.da[rows] = da
            n.dctx[...] = mt(da, n.w[:, :width]).astype(BF)
            n.vec_sum[0:1] += gain
            n.vec_sum[3:4] += shift

        @pl.when(step == pairs + tiles - 1)
        def _():
            put(n.grad, tm(n.kept_mem[...], n.dk[...]), 2 * width)
            put(n.grad, tm(n.kept_mem[...], n.dv[...]), 3 * width)
            put(n.grad, tm(n.kept_ctx[...], n.da[...]), 0)
            put(n.grad, tm(n.first[...], n.dq[...]), width)
            if fast:
                piece = width // FAST
                row = lax.broadcasted_iota(jnp.int32, (width, width), 0)
                col = lax.broadcasted_iota(jnp.int32, (width, width), 1)
                line = lax.broadcasted_iota(jnp.int32, (width, 8), 0) % piece
                pick_line = (line == lax.broadcasted_iota(jnp.int32, (width, 8), 1)).astype(BF)
                spread = mm(pick_line, n.vec_sum[...].astype(BF))
                spread = jnp.where(row // piece == col // piece, spread, 0.0).astype(BF)
                lane = lax.broadcasted_iota(jnp.int32, (width, PAIR), 1)
                fold = (lax.broadcasted_iota(jnp.int32, (width, PAIR), 0) % piece == lane).astype(BF)
                owner = lax.broadcasted_iota(jnp.int32, (width, FAST), 0)
                wanted = lax.broadcasted_iota(jnp.int32, (width, FAST), 1) * piece + 8
                put(n.grad, mm(spread, fold) + mm((owner == wanted).astype(BF), n.bias_mid[...]), 4 * width)
            start_grad(n.grad, n.grads, me, n.sems.at[0])
            wait_all(n.grad, n.sems.at[0])

    def pair(i):
        return jnp.minimum(i, pairs - 1)

    both = pl.BlockSpec((2, full, PAIR), lambda i: (pair(i), 0, 0))
    cols = pl.BlockSpec((full, PAIR), lambda i: (0, pair(i)))
    tile = pl.BlockSpec((TILE, width), lambda i: (jnp.maximum(i - pairs, 0), 0))

    def still(array):
        return (array, pl.BlockSpec(array.shape, lambda i: (0, 0)))

    return call(
        body,
        "cross_back",
        dict(
            place=(place, SMEM),
            qa=(att.qa, both),
            ka=(att.ka, both),
            value=(att.value, cols),
            cctx=(att.cctx, cols),
            dcctx=(dcctx, cols),
            tri=still(tri),
            parts=(parts, HBM),
            mem=(mem, HBM),
            ctx=(ctx, HBM),
            xhat=(att.xhat, HBM),
            inv=(att.inv, HBM),
            d2=(d2, HBM),
            d3=(d3, HBM),
            vec=still(vec),
            vec_mid=still(vec_mid),
            bias_mid=still(bias_mid),
        ),
        dict(
            mg=(struct((full, width)), tile),
            d13=(struct((full, width)), tile),
            dctx=(struct((full, width)), tile),
            vec_sum=still(struct((8, width), F4)),
            grads=(grad_shapes(width, 4 * width + extra, fast), ANY),
        ),
        dict(
            w=vmem(width, 4 * width),
            dq=vmem(full, width),
            dk=vmem(full, width),
            dv=vmem(full, width),
            kept_ctx=vmem(full, width),
            kept_mem=vmem(full, width),
            kept_xhat=vmem(full, width),
            kept_inv=vmem(full, PAIR, dtype=F4),
            kept_d2=vmem(full, width),
            kept_d3=vmem(full, width),
            first=vmem(full, width),
            da=vmem(full, width),
            grad=vmem(width, 4 * width + extra),
            sems=pltpu.SemaphoreType.DMA((7,)),
        ),
        grid=(pairs + tiles,),
        after=after,
    )


def self_back(att, dctx, tri):
    full, width = att.value.shape

    def body(n):
        attend_pair_back(True, n.qa, n.ka, n.value, n.ctx, n.dctx, n.tri, n.dq, n.dk, n.dv)

    both = pl.BlockSpec((2, full, PAIR), lambda p: (p, 0, 0))
    cols = pl.BlockSpec((full, PAIR), lambda p: (0, p))
    made = (struct((full, width)), cols)
    return call(
        body,
        "self_back",
        dict(

            qa=(att.qa, both),
            ka=(att.ka, both),
            value=(att.value, cols),
            ctx=(att.ctx, cols),
            dctx=(dctx, cols),
            tri=(tri, pl.BlockSpec((TILE, TILE), lambda p: (0, 0))),
        ),
        dict(dq=made, dk=made, dv=made),
        {},
        grid=(width // PAIR,),
    )


def self_grads(place, x, parts, d, d13, fast, after):
    full, width = x.shape

    def body(n):
        me = n.place[0]
        start_weight(n.w, n.parts, 0, me, n.sems.at[0])
        late = [
            pltpu.make_async_copy(src, dst, n.sems.at[k + 2])
            for k, (src, dst) in enumerate([(n.dk, n.late_dk), (n.dv, n.late_dv), (n.d13, n.late_d13)])
        ]
        for copy in late:
            copy.start()
        put(n.grad, tm(n.x[...], n.dq[...]), 0)
        late[0].wait()
        put(n.grad, tm(n.x[...], n.late_dk[...]), width)
        late[1].wait()
        put(n.grad, tm(n.x[...], n.late_dv[...]), 2 * width)
        start_grad(n.grad, n.grads, me, n.sems.at[1])
        wait_all(n.w, n.sems.at[0])
        late[2].wait()
        for i in range(0, full, TILE):
            rows = slice(i, i + TILE)
            back = n.late_d13[rows].astype(F4)
            for c, d in enumerate((n.dq, n.late_dk, n.late_dv)):
                back = back + mt(d[rows], n.w[:, c * width : (c + 1) * width])
            n.ig[rows] = back.astype(BF)
        wait_all(n.grad, n.sems.at[1])

    return call(
        body,
        "self_grads",
        dict(
            place=(place, SMEM),
            x=(x, WHOLE),
            parts=(parts, HBM),
            dq=(d.dq, WHOLE),
            dk=(d.dk, HBM),
            dv=(d.dv, HBM),
            d13=(d13, HBM),
        ),
        dict(ig=(struct((full, width)), WHOLE), grads=(grad_shapes(width, 3 * width, fast), ANY)),
        dict(
            w=vmem(width, 3 * width),
            grad=vmem(width, 3 * width),
            late_dk=vmem(full, width),
            late_dv=vmem(full, width),
            late_d13=vmem(full, width),
            sems=pltpu.SemaphoreType.DMA((5,)),
        ),
        after=after,
    )


def total(groups, pieces, steps=1, after=()):
    rows = groups[0][0].shape[0]
    span = rows // pieces // steps
    widths = [group[0].shape[1] for group in groups]

    def body(n):
        left, at = 0, 0
        for group, columns in zip(groups, widths):
            for k, out in enumerate(n.outs):
                value = n.parts[at + k][...].astype(F4)
                for m in range(1, len(group)):
                    value = value + n.parts[at + m * pieces + k][...].astype(F4)
                out[:, left : left + columns] = value.astype(BF)
            left += columns
            at += len(group) * pieces

    def piece(k, columns):
        return pl.BlockSpec((span, columns), lambda i: (k * steps + i, 0))

    parts, specs = [], []
    for group, columns in zip(groups, widths):
        for array in group:
            for k in range(pieces):
                parts.append(array)
                specs.append(piece(k, columns))
    outs = [struct((rows // pieces, sum(widths)))] * pieces
    return call(
        body, "total", dict(parts=(parts, specs)), dict(outs=(outs, piece(0, sum(widths)))), {}, (steps,), after
    ).outs


def finish(arrays, cuts):
    rows = arrays[0].shape[0]

    def body(n):
        value = n.arrays[0][...].astype(F4)
        for array in n.arrays[1:]:
            value = value + array[...].astype(F4)
        for out, (low, high, *more) in zip(n.outs, cuts):
            if len(more) == 1:
                for k in range((high - low) // more[0]):
                    out[k * rows : (k + 1) * rows] = value[:, low + k * more[0] : low + (k + 1) * more[0]]
            elif more:
                out[...] = value[more[0] : more[1], low:high]
            else:
                out[...] = value[:, low:high]

    outs = []
    for low, high, *more in cuts:
        if len(more) == 1:
            outs.append(struct(((high - low) // more[0] * rows, more[0]), F4))
        else:
            outs.append(struct((more[1] - more[0] if more else rows, high - low), F4))
    return call(body, "total", dict(arrays=(arrays, WHOLE)), dict(outs=(outs, WHOLE)), {}).outs


def widen(array, dtype):
    def body(n):
        n.out[...] = n.array[...].astype(dtype)

    block = pl.BlockSpec((1,) + array.shape[1:], lambda i: (i, 0, 0))
    return call(
        body,
        "widen",
        dict(array=(array, block)),
        dict(out=(struct(array.shape, dtype), block)),
        {},
        grid=(array.shape[0],),
    ).out


def to_rows(array):
    seats = lax.axis_size("seq")
    blocks = array.reshape(seats, -1, array.shape[-1])
    return lax.all_to_all(blocks, "seq", split_axis=0, concat_axis=0, tiled=True)


def pack(weights, gains, shifts, bias, up, down, co):
    rows, hidden = up.shape
    width = co.shape[1]

    def body(n):
        at = 0
        for weight in n.weights:
            n.front[:, at : at + weight.shape[1]] = weight[...]
            at += weight.shape[1]
        block = jnp.zeros((rows, PAIR), F4)
        row = lax.broadcasted_iota(jnp.int32, (rows, PAIR), 0)
        lines = [(n.gains, k) for k in range(3)] + [(n.shifts, k) for k in range(4)] + [(n.bias, 0)]
        for k, (source, line) in enumerate(lines):
            piece = source[line : line + 1].astype(F4)
            piece = jnp.concatenate([piece, jnp.zeros((1, PAIR - piece.shape[1]), F4)], axis=1)
            block = jnp.where(row == k, piece, block)
        n.front[:, at:] = block.astype(BF)
        n.late[:, :hidden] = n.up[...]
        n.late[:, 2 * hidden :] = n.co[...]
        for k in range(hidden // width):
            n.late[:, hidden + k * width : hidden + (k + 1) * width] = n.down[k * rows : (k + 1) * rows]

    columns = sum(weight.shape[1] for weight in weights) + PAIR
    return call(
        body,
        "pack",
        dict(
            weights=(weights, WHOLE),
            gains=(gains, WHOLE),
            shifts=(shifts, WHOLE),
            bias=(bias, WHOLE),
            up=(up, WHOLE),
            down=(down, WHOLE),
            co=(co, WHOLE),
        ),
        dict(front=(struct((rows, columns)), WHOLE), late=(struct((rows, 2 * hidden + width)), WHOLE)),
        {},
    )


def held(array, after=()):
    def kernel(*refs):
        pass

    others = [other for other in LAST + list(after) if other is not array]
    result = pl.pallas_call(
        kernel,
        name="held",
        in_specs=[HBM] * (1 + len(others)),
        out_specs=HBM,
        out_shape=struct(array.shape, array.dtype),
        input_output_aliases={0: 0},
        cost_estimate=pl.CostEstimate(flops=1000000, bytes_accessed=0, transcendentals=0),
    )(array, *others)
    LAST[:] = [result]
    return result


def swap(value, bits):
    return lax.ppermute(value, AXES, [(i, i ^ bits) for i in range(FAST)])


def swap_all(value):
    groups = [list(range(core, FAST, 2)) for core in range(2)]
    return lax.all_to_all(value, AXES, split_axis=0, concat_axis=0, tiled=True, axis_index_groups=groups)


def join(arrays, cuts=(), after=()):
    arrays = list(arrays)
    rows, columns = sum(x.shape[0] for x in arrays), arrays[0].shape[1]
    edges = [0, *cuts, columns]

    def body(n):
        at, copies = 0, []
        for x in n.arrays:
            for out, low, high in zip(n.outs, edges[:-1], edges[1:]):
                src = x.at[:, pl.ds(low, high - low)]
                dst = out.at[pl.ds(at, x.shape[0])]
                copies.append(pltpu.make_async_copy(src, dst, n.sems.at[len(copies)]))
            at += x.shape[0]
        for copy in copies:
            copy.start()
        for copy in copies:
            copy.wait()

    outs = [struct((rows, high - low)) for low, high in zip(edges[:-1], edges[1:])]
    sems = pltpu.SemaphoreType.DMA((len(arrays) * len(outs),))
    return call(
        body, "join", dict(arrays=(arrays, HBM)), dict(outs=(outs, WHOLE)), dict(sems=sems), after=after
    ).outs


def swap_plane(held):
    return [held] + [swap(held, bits) for bits in (2, 4, 6)]


def swap_line(held):
    return [held] + [swap(held, z << 3) for z in (1, 2, 3)]


def swap_cores(parts):
    return parts + [swap(part, 1) for part in parts]


def spread_plane(pieces):
    return [pieces[0]] + [swap(piece, bits) for piece, bits in zip(pieces[1:], (2, 4, 6))]


def spread_line(pieces):
    return [pieces[0]] + [swap(piece, z << 3) for z, piece in enumerate(pieces[1:], 1)]


def on_device(
    inputs,
    memory,
    seg_ids,
    mem_lengths,
    cotangent,
    qkv_weight,
    self_out_weight,
    cross_q_weight,
    cross_kv_weight,
    cross_out_weight,
    ffn_in_weight,
    ffn_in_bias,
    ffn_out_weight,
    norm_gains,
    shift_vectors,
):
    seats = lax.axis_size("seq")
    devices = lax.axis_size("dp") * seats
    span, width = inputs.shape[1:]
    hidden = ffn_in_weight.shape[1]
    full = seats * span
    seat = lax.axis_index("seq")
    me = lax.axis_index("dp") * seats + seat
    LAST.clear()
    rows, piece, bias_piece = qkv_weight.shape[0], norm_gains.shape[1], ffn_in_bias.shape[0]
    fast = devices == FAST and rows == 16 and hidden == 4 * width
    place = me.astype(jnp.int32).reshape(1)
    second_group = [self_out_weight, cross_q_weight, cross_kv_weight, cross_out_weight]
    if fast:
        packed = pack(
            [qkv_weight, *second_group[:3]],
            norm_gains,
            shift_vectors,
            ffn_in_bias[None],
            ffn_in_weight,
            ffn_out_weight,
            cross_out_weight,
        )
        front = swap_line(packed.front)
        ffn_parts = [lax.all_gather(packed.late, AXES, axis=0, tiled=False)]
        x = to_rows(inputs).reshape(full, width)
        one, two = join(front, (3 * width,))
        (one,) = join(swap_plane(one), (), [x])
        qkv_parts = [one, swap(one, 1)]
        two = swap_plane(two)
        vec, bias = None, None
    else:
        x = to_rows(inputs).reshape(full, width)
        qkv_parts = [lax.all_gather(qkv_weight, AXES, axis=0, tiled=True)]
        two_parts = [lax.all_gather(jnp.concatenate(second_group, axis=1), AXES, axis=0, tiled=True)]
        ffn_parts = [lax.all_gather(w, AXES, axis=0, tiled=True) for w in (ffn_in_weight, ffn_out_weight)]
        vec = lax.all_gather(jnp.concatenate([norm_gains, shift_vectors], axis=0), AXES, axis=1, tiled=True)
        vec = jnp.pad(vec.astype(F4), ((0, 1), (0, 0)))
        bias = lax.all_gather(ffn_in_bias, AXES, axis=0, tiled=True).astype(F4)[None]
    mem = to_rows(memory).reshape(full, width)
    cot = to_rows(cotangent).reshape(full, width)

    segments = lax.dynamic_index_in_dim(seg_ids, seat, 0, keepdims=False)
    ends = jnp.cumsum(lax.dynamic_index_in_dim(mem_lengths, seat, 0, keepdims=False))
    places = jnp.arange(full, dtype=jnp.int32)
    mem_segments = jnp.sum((places[:, None] >= ends[None, :]).astype(jnp.int32), axis=1)
    lane = jnp.arange(PAIR, dtype=jnp.int32)
    half = jnp.arange(2, dtype=jnp.int32)[:, None, None]
    free = (lane // HEAD)[None, None] == 1 - half
    number = (lane % HEAD)[None, None]

    def key_side(ids):
        away = jnp.where(ids[None, :, None] == number, 0.0, AWAY)
        ones = jnp.where(number < 11, 1.0, 0.0)
        return jnp.where(free, jnp.where(number < 8, away, ones), 0.0).astype(BF)

    augq = jnp.where(free & (number < 8) & (segments[None, :, None] == number), 1.0, 0.0).astype(BF)
    augk, augm = key_side(segments), key_side(mem_segments)
    corner = jnp.arange(TILE, dtype=jnp.int32)
    tri = jnp.where(corner[None, :] <= corner[:, None], 0.0, AWAY).astype(F4)

    a = self_forward(place, x, qkv_parts, augq, augk, tri)
    if fast:
        (two,) = join(two, (), [mem])
        two_parts = [two, swap(two, 1)]
    c = cross_forward(place, x, mem, two_parts, a.ctx, vec, bias, augq, augm, hidden, fast)
    vec, bias = c.vec, c.bias
    m = middle(place, x, cot, [] if fast else two_parts, ffn_parts, c.cctx, c.xhat, vec, bias, fast)
    output = to_rows(m.out)

    if fast:
        big = lax.psum_scatter(m.grads[0], AXES, scatter_dimension=0, tiled=True)
    g = cross_back(
        place, mem, two_parts, c, m.dcctx, tri, a.ctx, m.d2, m.d3, vec, m.vec_sum, m.bias_rows, fast, []
    )
    two_sum = []
    if fast:
        two_sum = spread_plane(total([[g.grads[0], swap(held(g.grads[1], [output]), 1)]], 4))
    memory_grad = to_rows(g.mg)
    d = self_back(a, g.dctx, tri)
    s = self_grads(place, x, qkv_parts, d, g.d13, fast, [memory_grad])
    if fast:
        qkv_got = swap(held(s.grads[1], two_sum[1:]), 1)
        qkv_sum = spread_plane(total([[s.grads[0], qkv_got]], 4))
    memory_grad = widen(memory_grad, F4)
    output = widen(output, BF)
    if fast:
        line = spread_line(total([qkv_sum, two_sum], 4))
    input_grad = to_rows(held(s.ig))
    if fast:
        at = 7 * width
        qkv_sum, so_sum, cq_sum, ckv_sum, gains_sum, shifts_sum, bias_sum = finish(
            line,
            (
                (0, 3 * width),
                (3 * width, 4 * width),
                (4 * width, 5 * width),
                (5 * width, at),
                (at, at + piece, 0, 3),
                (at, at + piece, 3, 7),
                (at, at + bias_piece, 8, 9),
            ),
        )
        up_sum, co_sum, down_sum = finish(
            [big], ((0, hidden), (hidden, hidden + width), (hidden + width, 2 * hidden + width, width))
        )
    else:

        def scatter(value, dim=0):
            return lax.psum_scatter(value.astype(F4), AXES, scatter_dimension=dim, tiled=True)

        upco_sum, down_sum, two_sum, qkv_sum = [scatter(v) for v in (*m.grads, *g.grads, *s.grads)]
        up_sum, co_sum = upco_sum[:, :hidden], upco_sum[:, hidden:]
        so_sum, cq_sum, ckv_sum = two_sum[:, :width], two_sum[:, width : 2 * width], two_sum[:, 2 * width :]
        vec_sum, bias_sum = scatter(g.vec_sum[:7], 1), scatter(m.bias_sum[0])
        gains_sum, shifts_sum = vec_sum[:3], vec_sum[3:]
    return (
        output,
        input_grad.astype(F4),
        memory_grad,
        qkv_sum,
        so_sum,
        cq_sum,
        ckv_sum,
        co_sum,
        up_sum,
        bias_sum.reshape(-1),
        down_sum,
        gains_sum,
        shifts_sum,
    )


def solution(mesh):
    rows = P("dp", "seq", None)
    weight = P(AXES, None)
    vector = P(None, AXES)
    return jax.shard_map(
        on_device,
        mesh=mesh,
        in_specs=(rows, rows, P("dp", None), P("dp", None), rows)
        + (weight,) * 6
        + (P(AXES), weight, vector, vector),
        out_specs=(rows,) * 3 + (weight,) * 6 + (P(AXES), weight, vector, vector),
        check_vma=False,
    )
```
